32 devices in a mesh: groups: 2 (over x), pts: 16 (over z, y, core).
Axes of the slice: x: 2, y: 2, z: 4, core: 2. Of those that a mesh axis runs over, the one named last changes fastest.
Arguments:
- spectra_in: float32 [1152, 4096], P(None, ('groups', 'pts')), parts along dimension 1, may hold values from 0.02 to 40, as said below
- coarse_spectra: float32 [2, 1152, 4096], P(None, None, ('groups', 'pts')), parts along dimension 2, may hold values from 0.2 to 4
- wind_speed: float32 [4096], P('groups'), parts along dimension 0, may hold values from 2 to 20
- wind_heading: float32 [4096], P('groups'), parts along dimension 0, may hold values from -3.140625 to 3.140625
- sea_mask: int32 [2048], replicated, may hold values 0 or 1
- neighbours: int32 [6, 2048], replicated, may hold values from 0 to 2047
- edge_x: float32 [6, 2048], replicated, may hold values from -1 to 1
- edge_y: float32 [6, 2048], replicated, may hold values from -1 to 1
- bound_points: int32 [32], replicated, may hold values from 0 to 2047, as said below
- bound_cells: int32 [4, 32], replicated, may hold values from 0 to 2047
- bound_weights: float32 [4, 32], replicated, may hold values from 0.1 to 1
Outputs:
- spectra_out: float32 [1152, 4096], P(None, ('groups', 'pts')), parts along dimension 1
The draws below stay inside these ranges and needn't reach their ends.
There are 2 independent parts, one for each index of `groups`. The reference program is written for one: setup_inputs(seed, part) draws one part's arguments, and reference() takes and returns one part's arrays. A program takes and returns all parts, laid end to end along the dimension named above; an argument that names none is the same for every part. Nothing has to cross between parts.
Inputs may be any that keep to these rules, and one draw needn't show every extreme that they name: `spectra_in`: positive spectral densities. `bound_points`: 32 distinct fine point indices.
All inputs are finite; a program needn't handle non-finite values.
Results may differ from the reference program's by a relative error of at most 0.0003.
Values sent between devices are 32-bit elements; how exact they have to be, the bound alone decides.
No kernel may reach another device: no remote copies, remote signals or barrier semaphores. Data moves between devices by JAX's collectives and lax.ppermute only.
A program may use at most 256 MiB of HBM per device.

```python
import math
import jax
import jax.numpy as jnp
from jax import lax

NDIR = 36
NFREQ = 32
NC = 1152
K = 6
SUB = 4
STEPS = 2
NP = 2048
NCOARSE = 2048
NB = 32


def draw_spectra_in(key, part):
    key = jax.random.fold_in(key, 11)
    subkeys = jax.random.split(key, 3)
    freq_index = (jnp.arange(NC) // NDIR).astype(jnp.float32)
    amplitude = 0.5 * (1.0 + freq_index / 10.0)
    comp_scale = jnp.exp(jax.random.uniform(subkeys[0], (NC,), jnp.float32, jnp.log(0.3), jnp.log(3.0)))
    point_scale = jnp.exp(jax.random.uniform(subkeys[1], (NP,), jnp.float32, jnp.log(0.3), jnp.log(3.0)))
    noise = jnp.exp(jax.random.uniform(subkeys[2], (NC, NP), jnp.float32, jnp.log(0.5), jnp.log(2.0)))
    return (amplitude * comp_scale)[:, None] * point_scale[None, :] * noise


def draw_bound_points(key, part):
    key = jax.random.fold_in(key, 23)
    interior = jax.random.permutation(key, NP - 2)[:NB - 2] + 1
    end_points = jnp.array([0, NP - 1], dtype=jnp.int32)
    return jnp.concatenate([end_points, interior.astype(jnp.int32)])


def place_ends(result, rng, low, top_value):
    longest = result.shape.index(max(result.shape))
    spots = []
    for shift in (0, 1):
        where = [jax.random.randint(jax.random.fold_in(rng, axis), (), 0, length) for axis, length in enumerate(result.shape)]
        where[longest] = (where[longest] + shift) % result.shape[longest]
        spots.append(tuple(where))
    return result.at[spots[0]].set(low).at[spots[1]].set(top_value)


def level_of(own_key, extent, cuts, smallest, high):
    factor_of, own = 1.0, jax.random.fold_in(own_key, 6)
    for axis_at, blocks in cuts:
        heights = jnp.exp(jax.random.uniform(jax.random.fold_in(own, axis_at), (blocks,), jnp.float32, smallest / len(cuts), high / len(cuts)))
        factor_of = factor_of * jnp.repeat(heights, extent[axis_at] // blocks).reshape([-1 if axis == axis_at else 1 for axis in range(len(extent))])
    return factor_of


def setup_inputs(seed: int = 0, part: int = 0) -> dict:
    arg_keys = jax.random.split(jax.random.key(seed), 12)
    part_splits = jax.random.split(jax.random.fold_in(arg_keys[11], part), 12)
    return {
        "spectra_in": draw_spectra_in(jax.random.fold_in(jax.random.fold_in(arg_keys[11], part), 71), part),
        "coarse_spectra": jnp.clip(jnp.exp(math.log(4.0) - 2.9957323 * jax.random.uniform(part_splits[1], (2, NC, NCOARSE), jnp.float32) ** level_of(part_splits[1], (2, NC, NCOARSE), ((2, 16),), -0.2, 0.2)), 0.2, 4.0),
        "wind_speed": jnp.clip(jnp.exp(jax.random.uniform(part_splits[2], (NP,), jnp.float32, math.log(2.0), math.log(20.0))), 2.0, 20.0),
        "wind_heading": jnp.clip(jax.random.uniform(part_splits[3], (NP,), jnp.float32, -3.140625, 3.140625), -3.140625, 3.140625),
        "sea_mask": place_ends((jax.random.randint(arg_keys[4], (NP,), 0, 8) < 7).astype(jnp.int32), jax.random.fold_in(arg_keys[4], 1), 0, 1),
        "neighbours": place_ends(jax.random.randint(arg_keys[5], (K, NP), 0, NP), jax.random.fold_in(arg_keys[5], 1), 0, NP - 1).astype(jnp.int32),
        "edge_x": jnp.clip(jax.random.uniform(arg_keys[6], (K, NP), jnp.float32, -1.0, 1.0), -1.0, 1.0),
        "edge_y": jnp.clip(jax.random.uniform(arg_keys[7], (K, NP), jnp.float32, -1.0, 1.0), -1.0, 1.0),
        "bound_points": draw_bound_points(jax.random.fold_in(arg_keys[11], 71), part),
        "bound_cells": place_ends(jax.random.randint(arg_keys[9], (4, NB), 0, NCOARSE), jax.random.fold_in(arg_keys[9], 1), 0, NCOARSE - 1).astype(jnp.int32),
        "bound_weights": jnp.clip(jax.random.uniform(arg_keys[10], (4, NB), jnp.float32, 0.1, 1.0), 0.1, 1.0),
    }


epsilon = 1e-6
courant = 0.1


def freq_tables(components):
    freq_index = (components // NDIR).astype(jnp.float32)
    dir_index = (components % NDIR).astype(jnp.float32)
    growth = jnp.log(jnp.asarray(1.1, jnp.float32))
    radian_freq = 0.25 * jnp.exp(freq_index * growth)
    freq_top = 0.25 * jnp.exp((NFREQ - 1) * growth)
    freq_total = NDIR * jnp.sum(0.25 * jnp.exp(jnp.arange(NFREQ).astype(jnp.float32) * growth))
    weight = radian_freq / freq_total
    dir_angle = dir_index * (2.0 * jnp.pi / NDIR)
    return radian_freq, weight, dir_angle, freq_top


def statistics(spectra, components):
    radian_freq, weight, dir_angle, freq_top = freq_tables(components)
    energy = jnp.sum(weight[:, None] * spectra, axis=0)
    inverse = jnp.sum((weight / radian_freq)[:, None] * spectra, axis=0)
    return energy, inverse


def apply_sources(spectra, components, energy, inverse, wind_speed, wind_heading, active):
    radian_freq, weight, dir_angle, freq_top = freq_tables(components)
    mean_freq = energy / (inverse + epsilon)
    mean_period = inverse / (energy + epsilon)
    steepness = energy * (0.5 * mean_freq) ** 2
    steep_ratio = steepness / (1.0 + steepness)
    relative = radian_freq / freq_top
    wind_in = 0.6 * relative[:, None] * jax.nn.sigmoid(
        wind_speed[None, :] * jnp.cos(dir_angle[:, None] - wind_heading[None, :]) * radian_freq[:, None] / 8.0 - 1.0)
    dissipation = (relative * relative)[:, None] * (mean_period * freq_top * steep_ratio)[None, :]
    return spectra * jnp.exp(wind_in - dissipation) * active[None, :]


def interpolate(coarse_block, bound_cells, bound_weights):
    norm_weights = bound_weights / jnp.sum(bound_weights, axis=0, keepdims=True)
    corners = coarse_block[:, :, bound_cells]
    return jnp.sum(norm_weights[None, None] * corners, axis=2)


def coefficients(components, edge_x, edge_y):
    radian_freq, weight, dir_angle, freq_top = freq_tables(components)
    group_speed = courant * 0.25 / radian_freq
    edge_coef = group_speed[None, :, None] * (jnp.cos(dir_angle)[None, :, None] * edge_x[:, None, :]
                                              + jnp.sin(dir_angle)[None, :, None] * edge_y[:, None, :])
    return jnp.sum(jnp.maximum(edge_coef, 0.0), axis=0), jnp.minimum(edge_coef, 0.0)


def advect(spectra, outflow, inflow, neighbours, active, bound_values, bound_points, start):
    for sub_step in range(SUB):
        upwind = inflow[0] * spectra[:, neighbours[0]]
        for edge in range(1, K):
            upwind = upwind + inflow[edge] * spectra[:, neighbours[edge]]
        spectra = (spectra - outflow * spectra - upwind) * active[None, :]
        time_frac = (start + sub_step + 1) / (STEPS * SUB)
        edge_values = (1.0 - time_frac) * bound_values[0] + time_frac * bound_values[1]
        spectra = spectra.at[:, bound_points].set(edge_values)
    return spectra


def reference(spectra_in, coarse_spectra, wind_speed, wind_heading, sea_mask, neighbours, edge_x, edge_y, bound_points, bound_cells, bound_weights):
    active = sea_mask.astype(jnp.float32)
    components = jnp.arange(NC, dtype=jnp.int32)
    coarse_blocks = coarse_spectra.reshape(2, 16, NC // 16, NCOARSE).transpose(1, 0, 2, 3)
    spectra = spectra_in
    for coarse_step in range(STEPS):
        energy, inverse = statistics(spectra, components)
        spectra = apply_sources(spectra, components, energy, inverse, wind_speed, wind_heading, active)

        def run_block(pieces):
            spec_block, comp_block, coarse_block = pieces
            bound_values = interpolate(coarse_block, bound_cells, bound_weights)
            outflow, inflow = coefficients(comp_block, edge_x, edge_y)
            return advect(spec_block, outflow, inflow, neighbours, active, bound_values, bound_points, coarse_step * SUB)

        blocks = lax.map(run_block, (spectra.reshape(16, NC // 16, NP), components.reshape(16, NC // 16), coarse_blocks))
        spectra = blocks.reshape(NC, NP)
    return spectra
```

```python
import functools
import math

import jax
import jax.numpy as jnp
import numpy as np
from jax import lax
from jax.experimental import pallas as pl
from jax.experimental.pallas import tpu as pltpu
from jax.sharding import PartitionSpec as P

NDIR = 36
NFREQ = 32
SUB = 4
STEPS = 2
LANES = 128


epsilon = 1e-06
courant = 0.1


def freq_tables(components):
    freq_index = (components // NDIR).astype(jnp.float32)
    dir_index = (components % NDIR).astype(jnp.float32)
    growth = jnp.log(jnp.asarray(1.1, jnp.float32))
    radian_freq = 0.25 * jnp.exp(freq_index * growth)
    freq_top = 0.25 * jnp.exp((NFREQ - 1) * growth)
    freq_total = NDIR * jnp.sum(0.25 * jnp.exp(jnp.arange(NFREQ).astype(jnp.float32) * growth))
    weight = radian_freq / freq_total
    dir_angle = dir_index * (2.0 * jnp.pi / NDIR)
    return (radian_freq, weight, dir_angle, freq_top)


def statistics(spectra, components):
    radian_freq, weight, dir_angle, freq_top = freq_tables(components)
    energy = jnp.sum(weight[:, None] * spectra, axis=0)
    inverse = jnp.sum((weight / radian_freq)[:, None] * spectra, axis=0)
    return (energy, inverse)


def apply_sources(spectra, components, energy, inverse, wind_speed, wind_heading, active):
    radian_freq, weight, dir_angle, freq_top = freq_tables(components)
    mean_freq = energy / (inverse + epsilon)
    mean_period = inverse / (energy + epsilon)
    steepness = energy * (0.5 * mean_freq) ** 2
    steep_ratio = steepness / (1.0 + steepness)
    relative = radian_freq / freq_top
    wind_in = (
        0.6
        * relative[:, None]
        * jax.nn.sigmoid(
            wind_speed[None, :]
            * jnp.cos(dir_angle[:, None] - wind_heading[None, :])
            * radian_freq[:, None]
            / 8.0
            - 1.0
        )
    )
    dissipation = (relative * relative)[:, None] * (mean_period * freq_top * steep_ratio)[None, :]
    return spectra * jnp.exp(wind_in - dissipation) * active[None, :]


def interpolate(coarse_block, bound_cells, bound_weights):
    norm_weights = bound_weights / jnp.sum(bound_weights, axis=0, keepdims=True)
    corners = coarse_block[:, :, bound_cells]
    return jnp.sum(norm_weights[None, None] * corners, axis=2)


def coefficients(components, edge_x, edge_y):
    radian_freq, weight, dir_angle, freq_top = freq_tables(components)
    group_speed = courant * 0.25 / radian_freq
    edge_coef = group_speed[None, :, None] * (
        jnp.cos(dir_angle)[None, :, None] * edge_x[:, None, :]
        + jnp.sin(dir_angle)[None, :, None] * edge_y[:, None, :]
    )
    return (jnp.sum(jnp.maximum(edge_coef, 0.0), axis=0), jnp.minimum(edge_coef, 0.0))


def advect(spectra, outflow, inflow, neighbours, active, bound_values, bound_points, start):
    edge_count = neighbours.shape[0]
    for sub_step in range(SUB):
        upwind = inflow[0] * spectra[:, neighbours[0]]
        for edge in range(1, edge_count):
            upwind = upwind + inflow[edge] * spectra[:, neighbours[edge]]
        spectra = (spectra - outflow * spectra - upwind) * active[None, :]
        time_frac = (start + sub_step + 1) / (STEPS * SUB)
        edge_values = (1.0 - time_frac) * bound_values[0] + time_frac * bound_values[1]
        spectra = spectra.at[:, bound_points].set(edge_values)
    return spectra


def to_components(spectra):
    return lax.all_to_all(spectra, "pts", split_axis=0, concat_axis=1, tiled=True)


def to_points(spectra):
    return lax.all_to_all(spectra, "pts", split_axis=1, concat_axis=0, tiled=True)


GROUPS = 9
GROUP_ROWS = 8
BASE_GROUP = (0, 1, 2, 3, 0, 1, 2, 3, 4)


def row_layout():
    dirs = np.zeros((GROUPS * GROUP_ROWS,), np.int32)
    upper = np.zeros((GROUPS * GROUP_ROWS,), np.int32)
    for row in range(GROUPS * GROUP_ROWS):
        group, sub = divmod(row, GROUP_ROWS)
        if group < 8:
            dirs[row] = 8 * (group % 4) + sub
            upper[row] = group // 4
        else:
            dirs[row] = 32 + sub % 4
            upper[row] = sub // 4
    return dirs, upper


def group_rows(group):
    return pl.ds(GROUP_ROWS * group, GROUP_ROWS)


def load_natural(ref, block):
    lower = [ref[block, group_rows(group), :] for group in range(4)]
    upper = [ref[block, pl.ds(NDIR + GROUP_ROWS * group, GROUP_ROWS), :] for group in range(4)]
    sub = lax.broadcasted_iota(jnp.int32, (GROUP_ROWS, LANES), 0)
    last = jnp.where(sub < 4, ref[block, pl.ds(32, 8), :], ref[block, pl.ds(64, 8), :])
    return lower + upper + [last]


def store_natural(ref, block, values):
    for group in range(4):
        ref[block, group_rows(group), :] = values[group]
    for group in range(4):
        ref[block, pl.ds(NDIR + GROUP_ROWS * group, GROUP_ROWS), :] = values[4 + group]
    ref[block, pl.ds(32, 4), :] = values[8][0:4]
    ref[block, pl.ds(68, 4), :] = values[8][4:8]


def row_tables(device_place):
    dirs, upper = row_layout()
    freq = (2 * device_place + jnp.asarray(upper)).astype(jnp.int32)
    radian_freq, weight, _, freq_top = freq_tables(freq * NDIR)
    relative = radian_freq / freq_top
    group_speed = courant * 0.25 / radian_freq
    table = jnp.stack([radian_freq, 0.6 * relative, relative * relative * freq_top, group_speed, weight, weight / radian_freq])
    return jnp.broadcast_to(table[:, :, None], table.shape + (LANES,))


def direction_tables():
    dirs, _ = row_layout()
    angle = dirs.astype(np.float64) * (2.0 * np.pi / NDIR)
    table = np.stack([np.cos(angle), np.sin(angle)]).astype(np.float32)
    return jnp.asarray(np.broadcast_to(table[:, :, None], table.shape + (LANES,)))


def setup_kernel(points_ref, edge_ref, rows_ref, dirs_ref, keep_ref, base_ref, growth_ref):
    edge_count = edge_ref.shape[0]

    def block(place, _):
        speed = jnp.broadcast_to(points_ref[place, 0:1, :], (GROUP_ROWS, LANES)) * 0.125
        heading = jnp.broadcast_to(points_ref[place, 1:2, :], (GROUP_ROWS, LANES))
        active = jnp.broadcast_to(points_ref[place, 2:3, :], (GROUP_ROWS, LANES))
        free = jnp.broadcast_to(points_ref[place, 3:4, :], (GROUP_ROWS, LANES))
        along, across = speed * jnp.cos(heading), speed * jnp.sin(heading)
        total = []
        for base_group, group in enumerate((0, 1, 2, 3, 8)):
            cosine, sine = dirs_ref[0, group_rows(group), :], dirs_ref[1, group_rows(group), :]
            out = jnp.zeros((GROUP_ROWS, LANES), jnp.float32)
            for edge in range(edge_count):
                x = jnp.broadcast_to(edge_ref[edge, place, 0:1, :], (GROUP_ROWS, LANES))
                y = jnp.broadcast_to(edge_ref[edge, place, 1:2, :], (GROUP_ROWS, LANES))
                flow = cosine * x + sine * y
                out = out + jnp.maximum(flow, 0.0)
                base_ref[place, edge, group_rows(base_group), :] = jnp.minimum(flow, 0.0) * free
            total.append(out)
        for group in range(GROUPS):
            rows = group_rows(group)
            cosine, sine = dirs_ref[0, rows, :], dirs_ref[1, rows, :]
            wind = (along * cosine + across * sine) * rows_ref[0, rows, :] - 1.0
            growth_ref[place, rows, :] = jnp.exp(rows_ref[1, rows, :] * jax.nn.sigmoid(wind)) * active
            keep_ref[place, rows, :] = (1.0 - rows_ref[3, rows, :] * total[BASE_GROUP[group]]) * free
        return 0

    lax.fori_loop(0, keep_ref.shape[0], block, 0)


def boundary_kernel(bound_ref, select_ref, start_ref, slope_ref):
    total = bound_ref[0]
    for source in range(1, bound_ref.shape[0]):
        total = total + bound_ref[source]
    sub = lax.broadcasted_iota(jnp.int32, (GROUP_ROWS, LANES), 0)

    def block(place, _):
        pieces = []
        for piece in range(4):
            pieces.append(
                jnp.dot(
                    total,
                    select_ref[piece, place],
                    preferred_element_type=jnp.float32,
                    precision=lax.Precision.HIGHEST,
                )
            )
        for out_ref, values in (
            (start_ref, (pieces[0], pieces[2])),
            (slope_ref, (pieces[1] - pieces[0], pieces[3] - pieces[2])),
        ):
            for half in range(2):
                for group in range(4):
                    out_ref[place, group_rows(4 * half + group), :] = values[half][8 * group : 8 * group + 8]
            out_ref[place, pl.ds(64, 4), :] = values[0][32:36]
            out_ref[place, pl.ds(68, 4), :] = values[1][32:36]
        return 0

    lax.fori_loop(0, start_ref.shape[0], block, 0)


def take_lanes(values, lanes):
    return jnp.take_along_axis(values, lanes, axis=1, mode="promise_in_bounds")


def fine_kernel(
    first,
    state_ref,
    moments_ref,
    index_ref,
    keep_ref,
    base_ref,
    growth_ref,
    start_ref,
    slope_ref,
    rows_ref,
    out_ref,
    *rest,
):
    if first:
        sums_ref, field, words, speed = rest
    else:
        field, words, speed = rest
    blocks = keep_ref.shape[0]
    half = blocks // 2
    edge_count = base_ref.shape[1]
    first_step = 0 if first else SUB

    if first:

        def enter(place, _):
            for group, value in enumerate(load_natural(state_ref, place)):
                field[0, place, group_rows(group), :] = value
            return 0

    else:

        def enter(place, _):
            energy = jnp.broadcast_to(moments_ref[2 * place : 2 * place + 1, :], (GROUP_ROWS, LANES))
            inverse = jnp.broadcast_to(moments_ref[2 * place + 1 : 2 * place + 2, :], (GROUP_ROWS, LANES))
            mean_freq = energy / (inverse + epsilon)
            steepness = energy * (0.5 * mean_freq) * (0.5 * mean_freq)
            loss = inverse / (energy + epsilon) * (steepness / (1.0 + steepness))
            lower = jnp.exp(-rows_ref[2, group_rows(0), :] * loss)
            upper = jnp.exp(-rows_ref[2, group_rows(4), :] * loss)
            last = jnp.exp(-rows_ref[2, group_rows(8), :] * loss)
            decay = [lower] * 4 + [upper] * 4 + [last]
            for group in range(GROUPS):
                rows = group_rows(group)
                field[0, place, rows, :] = state_ref[place, rows, :] * growth_ref[place, rows, :] * decay[group]
            return 0

    if first:
        lax.fori_loop(0, blocks, enter, 0)
    else:
        for place in range(blocks):
            enter(place, 0)

    def fine_step(number, _):
        source = lax.rem(number, 2)
        time_frac = (number + (first_step + 1)).astype(jnp.float32) * (1.0 / (STEPS * SUB))
        for group in range(GROUPS):
            rows = group_rows(group)
            values = [field[source, place, rows, :] for place in range(blocks)]
            top = functools.reduce(jnp.maximum, values)
            top = jnp.maximum(jnp.max(top, axis=1, keepdims=True), 1e-30)
            scale = jnp.broadcast_to(65535.0 / top, (GROUP_ROWS, LANES))
            speed[rows, :] = rows_ref[3, rows, :] * (top * (1.0 / 65535.0))
            coded = [(value * scale + 0.5).astype(jnp.int32) for value in values]
            for place in range(half):
                words[place, rows, :] = (coded[place + half] << 16) | coded[place]

        def block(place, _):
            inflow = [None] * GROUPS
            for edge in range(edge_count):
                index = index_ref[place, edge]
                lanes = index & (LANES - 1)
                masks = [(index & (LANES << level)) != 0 for level in range(half.bit_length() - 1)]
                shift = (index >> (half.bit_length() + 6)) << 4

                def pick(low, level, rows):
                    if level == 0:
                        return take_lanes(words[low, rows, :], lanes)
                    step = 1 << (level - 1)
                    below = pick(low, level - 1, rows)
                    above = pick(low + step, level - 1, rows)
                    return jnp.where(masks[level - 1], above, below)

                for group in range(GROUPS):
                    word = pick(0, half.bit_length() - 1, group_rows(group))
                    value = (lax.shift_right_logical(word, shift) & 65535).astype(jnp.float32)
                    term = base_ref[place, edge, group_rows(BASE_GROUP[group]), :] * value
                    inflow[group] = term if inflow[group] is None else inflow[group] + term
            for group in range(GROUPS):
                rows = group_rows(group)
                field[1 - source, place, rows, :] = (
                    field[source, place, rows, :] * keep_ref[place, rows, :]
                    - speed[rows, :] * inflow[group]
                    + (start_ref[place, rows, :] + time_frac * slope_ref[place, rows, :])
                )
            return 0

        lax.fori_loop(0, blocks, block, 0)
        return 0

    lax.fori_loop(0, SUB, fine_step, 0)

    def leave(place, _):
        values = [field[SUB % 2, place, group_rows(group), :] for group in range(GROUPS)]
        if first:
            energy, inverse = None, None
            for group in range(GROUPS):
                rows = group_rows(group)
                out_ref[place, rows, :] = values[group]
                part = rows_ref[4, rows, :] * values[group]
                energy = part if energy is None else energy + part
                part = rows_ref[5, rows, :] * values[group]
                inverse = part if inverse is None else inverse + part
            sums_ref[place, 0:1, :] = jnp.sum(energy, axis=0, keepdims=True)
            sums_ref[place, 1:2, :] = jnp.sum(inverse, axis=0, keepdims=True)
        else:
            store_natural(out_ref, place, values)
        return 0

    lax.fori_loop(0, blocks, leave, 0)


def in_vmem(count):
    return [pl.BlockSpec(memory_space=pltpu.VMEM)] * count


def params():
    return pltpu.CompilerParams(vmem_limit_bytes=56 << 20)


def whole_frequencies(
    spectra_in,
    coarse_spectra,
    wind_speed,
    wind_heading,
    active,
    neighbours,
    edge_x,
    edge_y,
    bound_points,
    bound_cells,
    bound_weights,
):
    device_count = lax.axis_size("pts")
    device_place = lax.axis_index("pts")
    comp_total, point_count = spectra_in.shape
    local_count = comp_total // device_count
    edge_count, grid_points = neighbours.shape
    blocks = grid_points // LANES
    bound_count = bound_points.shape[0]
    f32 = jnp.float32
    all_comp = jnp.arange(comp_total, dtype=jnp.int32)
    first_point = device_place * point_count
    own_speed = lax.dynamic_slice_in_dim(wind_speed, first_point, point_count)
    own_heading = lax.dynamic_slice_in_dim(wind_heading, first_point, point_count)
    own_active = lax.dynamic_slice_in_dim(active, first_point, point_count)

    energy, inverse = statistics(spectra_in, all_comp)
    spectra = apply_sources(spectra_in, all_comp, energy, inverse, own_speed, own_heading, own_active)
    field = lax.all_to_all(
        spectra.reshape(device_count, local_count, LANES), "pts", split_axis=0, concat_axis=0, tiled=True
    )

    norm_weights = bound_weights / jnp.sum(bound_weights, axis=0, keepdims=True)
    own_cells = first_point + jnp.arange(point_count, dtype=jnp.int32)
    cell_weights = jnp.sum(
        jnp.where(bound_cells[:, None, :] == own_cells[None, :, None], norm_weights[:, None, :], 0.0), axis=0
    )
    shares = jnp.einsum(
        "tifdq,qj->idftj",
        coarse_spectra.reshape(2, device_count, 2, NDIR, point_count),
        cell_weights,
        precision=lax.Precision.HIGHEST,
    ).reshape(device_count, NDIR, 4 * bound_count)
    shares = jnp.pad(shares, ((0, 0), (0, 4), (0, 0)))
    shares = lax.all_to_all(shares, "pts", split_axis=0, concat_axis=0, tiled=True)
    spread = (bound_points[:, None] == jnp.arange(grid_points, dtype=jnp.int32)[None, :]).astype(f32)
    select = jnp.einsum("ab,jp->abjp", jnp.eye(4, dtype=f32), spread).reshape(4, 4 * bound_count, blocks, LANES)
    select = select.transpose(0, 2, 1, 3)
    start, slope = pl.pallas_call(
        boundary_kernel,
        out_shape=[jax.ShapeDtypeStruct((blocks, local_count, LANES), f32)] * 2,
        in_specs=in_vmem(2),
        out_specs=in_vmem(2),
        compiler_params=params(),
    )(shares, select)

    free = active * (1.0 - jnp.sum(spread, axis=0))
    per_point = jnp.stack([wind_speed, wind_heading, active, free]).reshape(4, blocks, LANES).transpose(1, 0, 2)
    edges = jnp.stack([edge_x, edge_y], axis=1).reshape(edge_count, 2, blocks, LANES).transpose(0, 2, 1, 3)
    rows = row_tables(device_place)
    keep, base, growth = pl.pallas_call(
        setup_kernel,
        out_shape=[
            jax.ShapeDtypeStruct((blocks, local_count, LANES), f32),
            jax.ShapeDtypeStruct((blocks, edge_count, 40, LANES), f32),
            jax.ShapeDtypeStruct((blocks, local_count, LANES), f32),
        ],
        in_specs=in_vmem(4),
        out_specs=in_vmem(3),
        compiler_params=params(),
    )(per_point, edges, rows, direction_tables())

    index = neighbours.reshape(edge_count, blocks, 1, LANES).transpose(1, 0, 2, 3)
    index = jnp.broadcast_to(index, (blocks, edge_count, GROUP_ROWS, LANES))

    def fine(first, state, moments):
        state_shape = jax.ShapeDtypeStruct((blocks, local_count, LANES), f32)
        out_shape = [state_shape]
        if first:
            out_shape.append(jax.ShapeDtypeStruct((blocks, 2, LANES), f32))
        return pl.pallas_call(
            functools.partial(fine_kernel, first),
            out_shape=out_shape,
            in_specs=in_vmem(9),
            out_specs=in_vmem(len(out_shape)),
            scratch_shapes=[
                pltpu.VMEM((2, blocks, local_count, LANES), f32),
                pltpu.VMEM((blocks // 2, local_count, LANES), jnp.int32),
                pltpu.VMEM((local_count, LANES), f32),
            ],
            compiler_params=params(),
        )(state, moments, index, keep, base, growth, start, slope, rows)

    field, sums = fine(True, field, jnp.zeros((2 * blocks, LANES), f32))
    sums = sums.reshape(2 * blocks, LANES)
    distance = 1
    while distance < device_count:
        pairs = [(place, place ^ distance) for place in range(device_count)]
        sums = sums + lax.ppermute(sums, "pts", pairs)
        distance *= 2
    (field,) = fine(False, field, sums)
    field = lax.all_to_all(field, "pts", split_axis=0, concat_axis=0, tiled=True)
    return field.reshape(comp_total, point_count)


def shards(
    spectra_in,
    coarse_spectra,
    wind_speed,
    wind_heading,
    sea_mask,
    neighbours,
    edge_x,
    edge_y,
    bound_points,
    bound_cells,
    bound_weights,
):
    device_count = lax.axis_size("pts")
    device_place = lax.axis_index("pts")
    point_count = spectra_in.shape[1]
    comp_total = spectra_in.shape[0]
    local_count = comp_total // device_count
    active = sea_mask.astype(jnp.float32)
    blocks = neighbours.shape[1] // LANES
    if (
        local_count == 2 * NDIR
        and point_count == LANES
        and 4 * bound_points.shape[0] == LANES
        and coarse_spectra.shape[2] == LANES
        and blocks == device_count
        and blocks & (blocks - 1) == 0
    ):
        return whole_frequencies(
            spectra_in,
            coarse_spectra,
            wind_speed,
            wind_heading,
            active,
            neighbours,
            edge_x,
            edge_y,
            bound_points,
            bound_cells,
            bound_weights,
        )
    all_comp = jnp.arange(comp_total, dtype=jnp.int32)
    my_comp = device_place * local_count + jnp.arange(local_count, dtype=jnp.int32)
    first_point = device_place * point_count
    own_speed = lax.dynamic_slice_in_dim(wind_speed, first_point, point_count)
    own_heading = lax.dynamic_slice_in_dim(wind_heading, first_point, point_count)
    own_active = lax.dynamic_slice_in_dim(active, first_point, point_count)
    coarse_here = lax.all_to_all(coarse_spectra, "pts", split_axis=1, concat_axis=2, tiled=True)
    bound_values = interpolate(coarse_here, bound_cells, bound_weights)
    outflow, inflow = coefficients(my_comp, edge_x, edge_y)
    spectra = spectra_in
    for coarse_step in range(STEPS):
        energy, inverse = statistics(spectra, all_comp)
        spectra = apply_sources(
            spectra, all_comp, energy, inverse, own_speed, own_heading, own_active
        )
        comp_field = to_components(spectra)
        comp_field = advect(
            comp_field,
            outflow,
            inflow,
            neighbours,
            active,
            bound_values,
            bound_points,
            coarse_step * SUB,
        )
        spectra = to_points(comp_field)
    return spectra


def solution(mesh):
    in_specs = (
        P(None, ("groups", "pts")),
        P(None, None, ("groups", "pts")),
        P("groups"),
        P("groups"),
        P(),
        P(),
        P(),
        P(),
        P(),
        P(),
        P(),
    )
    out_specs = P(None, ("groups", "pts"))
    return jax.shard_map(shards, mesh=mesh, in_specs=in_specs, out_specs=out_specs, check_vma=False)
```

```python
import functools
import math

import jax
import jax.numpy as jnp
import numpy as np
from jax import lax
from jax.experimental import pallas as pl
from jax.experimental.pallas import tpu as pltpu
from jax.sharding import PartitionSpec as P

NDIR = 36
NFREQ = 32
SUB = 4
STEPS = 2
LANES = 128


epsilon = 1e-06
courant = 0.1


def freq_tables(components):
    freq_index = (components // NDIR).astype(jnp.float32)
    dir_index = (components % NDIR).astype(jnp.float32)
    growth = jnp.log(jnp.asarray(1.1, jnp.float32))
    radian_freq = 0.25 * jnp.exp(freq_index * growth)
    freq_top = 0.25 * jnp.exp((NFREQ - 1) * growth)
    freq_total = NDIR * jnp.sum(0.25 * jnp.exp(jnp.arange(NFREQ).astype(jnp.float32) * growth))
    weight = radian_freq / freq_total
    dir_angle = dir_index * (2.0 * jnp.pi / NDIR)
    return (radian_freq, weight, dir_angle, freq_top)


def statistics(spectra, components):
    radian_freq, weight, dir_angle, freq_top = freq_tables(components)
    energy = jnp.sum(weight[:, None] * spectra, axis=0)
    inverse = jnp.sum((weight / radian_freq)[:, None] * spectra, axis=0)
    return (energy, inverse)


def apply_sources(spectra, components, energy, inverse, wind_speed, wind_heading, active):
    radian_freq, weight, dir_angle, freq_top = freq_tables(components)
    mean_freq = energy / (inverse + epsilon)
    mean_period = inverse / (energy + epsilon)
    steepness = energy * (0.5 * mean_freq) ** 2
    steep_ratio = steepness / (1.0 + steepness)
    relative = radian_freq / freq_top
    wind_in = (
        0.6
        * relative[:, None]
        * jax.nn.sigmoid(
            wind_speed[None, :]
            * jnp.cos(dir_angle[:, None] - wind_heading[None, :])
            * radian_freq[:, None]
            / 8.0
            - 1.0
        )
    )
    dissipation = (relative * relative)[:, None] * (mean_period * freq_top * steep_ratio)[None, :]
    return spectra * jnp.exp(wind_in - dissipation) * active[None, :]


def interpolate(coarse_block, bound_cells, bound_weights):
    norm_weights = bound_weights / jnp.sum(bound_weights, axis=0, keepdims=True)
    corners = coarse_block[:, :, bound_cells]
    return jnp.sum(norm_weights[None, None] * corners, axis=2)


def coefficients(components, edge_x, edge_y):
    radian_freq, weight, dir_angle, freq_top = freq_tables(components)
    group_speed = courant * 0.25 / radian_freq
    edge_coef = group_speed[None, :, None] * (
        jnp.cos(dir_angle)[None, :, None] * edge_x[:, None, :]
        + jnp.sin(dir_angle)[None, :, None] * edge_y[:, None, :]
    )
    return (jnp.sum(jnp.maximum(edge_coef, 0.0), axis=0), jnp.minimum(edge_coef, 0.0))


def advect(spectra, outflow, inflow, neighbours, active, bound_values, bound_points, start):
    edge_count = neighbours.shape[0]
    for sub_step in range(SUB):
        upwind = inflow[0] * spectra[:, neighbours[0]]
        for edge in range(1, edge_count):
            upwind = upwind + inflow[edge] * spectra[:, neighbours[edge]]
        spectra = (spectra - outflow * spectra - upwind) * active[None, :]
        time_frac = (start + sub_step + 1) / (STEPS * SUB)
        edge_values = (1.0 - time_frac) * bound_values[0] + time_frac * bound_values[1]
        spectra = spectra.at[:, bound_points].set(edge_values)
    return spectra


def to_components(spectra):
    return lax.all_to_all(spectra, "pts", split_axis=0, concat_axis=1, tiled=True)


def to_points(spectra):
    return lax.all_to_all(spectra, "pts", split_axis=1, concat_axis=0, tiled=True)


GROUPS = 9
GROUP_ROWS = 8
BASE_GROUP = (0, 1, 2, 3, 0, 1, 2, 3, 4)


def row_layout():
    dirs = np.zeros((GROUPS * GROUP_ROWS,), np.int32)
    upper = np.zeros((GROUPS * GROUP_ROWS,), np.int32)
    for row in range(GROUPS * GROUP_ROWS):
        group, sub = divmod(row, GROUP_ROWS)
        if group < 8:
            dirs[row] = 8 * (group % 4) + sub
            upper[row] = group // 4
        else:
            dirs[row] = 32 + sub % 4
            upper[row] = sub // 4
    return dirs, upper


def group_rows(group):
    return pl.ds(GROUP_ROWS * group, GROUP_ROWS)


def load_natural(ref, block):
    lower = [ref[block, group_rows(group), :] for group in range(4)]
    upper = [ref[block, pl.ds(NDIR + GROUP_ROWS * group, GROUP_ROWS), :] for group in range(4)]
    sub = lax.broadcasted_iota(jnp.int32, (GROUP_ROWS, LANES), 0)
    last = jnp.where(sub < 4, ref[block, pl.ds(32, 8), :], ref[block, pl.ds(64, 8), :])
    return lower + upper + [last]


def store_natural(ref, block, values):
    for group in range(4):
        ref[block, group_rows(group), :] = values[group]
    for group in range(4):
        ref[block, pl.ds(NDIR + GROUP_ROWS * group, GROUP_ROWS), :] = values[4 + group]
    ref[block, pl.ds(32, 4), :] = values[8][0:4]
    ref[block, pl.ds(68, 4), :] = values[8][4:8]


def row_tables(device_place):
    dirs, upper = row_layout()
    freq = (2 * device_place + jnp.asarray(upper)).astype(jnp.int32)
    radian_freq, weight, _, freq_top = freq_tables(freq * NDIR)
    relative = radian_freq / freq_top
    group_speed = courant * 0.25 / radian_freq
    table = jnp.stack([radian_freq, 0.6 * relative, relative * relative * freq_top, group_speed, weight, weight / radian_freq])
    return jnp.broadcast_to(table[:, :, None], table.shape + (LANES,))


def direction_tables():
    dirs, _ = row_layout()
    angle = dirs.astype(np.float64) * (2.0 * np.pi / NDIR)
    table = np.stack([np.cos(angle), np.sin(angle)]).astype(np.float32)
    return jnp.asarray(np.broadcast_to(table[:, :, None], table.shape + (LANES,)))


def setup_kernel(points_ref, edge_ref, rows_ref, dirs_ref, keep_ref, base_ref, growth_ref):
    edge_count = edge_ref.shape[0]

    def block(place, _):
        speed = jnp.broadcast_to(points_ref[place, 0:1, :], (GROUP_ROWS, LANES)) * 0.125
        heading = jnp.broadcast_to(points_ref[place, 1:2, :], (GROUP_ROWS, LANES))
        active = jnp.broadcast_to(points_ref[place, 2:3, :], (GROUP_ROWS, LANES))
        free = jnp.broadcast_to(points_ref[place, 3:4, :], (GROUP_ROWS, LANES))
        along, across = speed * jnp.cos(heading), speed * jnp.sin(heading)
        total = []
        for base_group, group in enumerate((0, 1, 2, 3, 8)):
            cosine, sine = dirs_ref[0, group_rows(group), :], dirs_ref[1, group_rows(group), :]
            out = jnp.zeros((GROUP_ROWS, LANES), jnp.float32)
            for edge in range(edge_count):
                x = jnp.broadcast_to(edge_ref[edge, place, 0:1, :], (GROUP_ROWS, LANES))
                y = jnp.broadcast_to(edge_ref[edge, place, 1:2, :], (GROUP_ROWS, LANES))
                flow = cosine * x + sine * y
                out = out + jnp.maximum(flow, 0.0)
                base_ref[place, edge, group_rows(base_group), :] = jnp.minimum(flow, 0.0) * free
            total.append(out)
        for group in range(GROUPS):
            rows = group_rows(group)
            cosine, sine = dirs_ref[0, rows, :], dirs_ref[1, rows, :]
            wind = (along * cosine + across * sine) * rows_ref[0, rows, :] - 1.0
            growth_ref[place, rows, :] = jnp.exp(rows_ref[1, rows, :] * jax.nn.sigmoid(wind)) * active
            keep_ref[place, rows, :] = (1.0 - rows_ref[3, rows, :] * total[BASE_GROUP[group]]) * free
        return 0

    lax.fori_loop(0, keep_ref.shape[0], block, 0)


def frequency(place):
    return 0.25 * 1.1**place


FREQ_TOP = frequency(NFREQ - 1)
FREQ_TOTAL = NDIR * sum(frequency(place) for place in range(NFREQ))


def dissipation_rate(energy, inverse):
    mean_freq = energy / (inverse + epsilon)
    steepness = energy * (0.5 * mean_freq) * (0.5 * mean_freq)
    return inverse / (energy + epsilon) * (steepness / (1.0 + steepness))


def split_bf16(values):
    high = values.astype(jnp.bfloat16).astype(jnp.float32)
    return high, values - high


def pack_kernel(first_ref, spectra_ref, coarse_ref, cells_ref, weights_ref, send_ref, shares):
    destinations = send_ref.shape[0]
    f32 = jnp.float32
    lane = lax.broadcasted_iota(jnp.int32, (LANES, LANES), 1)
    cell = lax.broadcasted_iota(jnp.int32, (LANES, LANES), 0) + first_ref[0]
    norm = weights_ref[...] / jnp.sum(weights_ref[...], axis=0, keepdims=True)
    table = jnp.zeros((LANES, LANES), f32)
    for corner in range(cells_ref.shape[0]):
        hit = jnp.broadcast_to(cells_ref[corner : corner + 1, :], (LANES, LANES)) == cell
        table = table + jnp.where(hit, jnp.broadcast_to(norm[corner : corner + 1, :], (LANES, LANES)), 0.0)
    later = (lane & 32) != 0
    bf16 = jnp.bfloat16
    parts = [split_bf16(jnp.where(later, 0.0, table)), split_bf16(jnp.where(later, table, 0.0))]
    parts = [(high.astype(bf16), low.astype(bf16)) for high, low in parts]
    chunk = 8 * NDIR

    for start in range(0, spectra_ref.shape[0], chunk):
        result = None
        for time in range(2):
            high, low = split_bf16(coarse_ref[time, pl.ds(start, chunk), :])
            high, low = high.astype(bf16), low.astype(bf16)
            weight_high, weight_low = parts[time]
            for left, right in ((high, weight_high), (low, weight_high), (high, weight_low)):
                term = jnp.dot(left, right, preferred_element_type=f32)
                result = term if result is None else result + term
        shares[pl.ds(start, chunk), :] = result

    sub = lax.broadcasted_iota(jnp.int32, (GROUP_ROWS, LANES), 0) < 4
    energy = jnp.zeros((GROUP_ROWS, LANES), f32)
    inverse = jnp.zeros((GROUP_ROWS, LANES), f32)
    lower_lanes = lax.broadcasted_iota(jnp.int32, (NDIR, LANES), 1) < 64
    for place in range(destinations):
        start = 2 * NDIR * place
        values = [spectra_ref[pl.ds(start + GROUP_ROWS * group, GROUP_ROWS), :] for group in range(GROUPS)]
        for group in range(GROUPS):
            send_ref[place, group_rows(group), :] = values[group]
        lower = values[0] + values[1] + values[2] + values[3] + jnp.where(sub, values[4], 0.0)
        upper = values[5] + values[6] + values[7] + values[8] + jnp.where(sub, 0.0, values[4])
        energy = energy + frequency(2 * place) * lower + frequency(2 * place + 1) * upper
        inverse = inverse + (lower + upper)
        send_ref[place, pl.ds(2 * NDIR, NDIR), :] = jnp.where(
            lower_lanes, shares[pl.ds(start, NDIR), :], shares[pl.ds(start + NDIR, NDIR), :]
        )
    energy = jnp.sum(energy, axis=0, keepdims=True) * (1.0 / FREQ_TOTAL)
    inverse = jnp.sum(inverse, axis=0, keepdims=True) * (1.0 / FREQ_TOTAL)
    rate = jnp.broadcast_to(dissipation_rate(energy, inverse), (4, LANES))
    for place in range(destinations):
        send_ref[place, pl.ds(3 * NDIR, 4), :] = rate


def take_lanes(values, lanes):
    return jnp.take_along_axis(values, lanes, axis=1, mode="promise_in_bounds")


def fine_kernel(
    first,
    state_ref,
    extra_ref,
    index_ref,
    keep_ref,
    base_ref,
    growth_ref,
    rows_ref,
    *rest,
):
    if first:
        out_ref, sums_ref, start_ref, slope_ref, field, words, speed = rest
    else:
        start_ref, slope_ref, out_ref, field, words, speed = rest
    blocks = keep_ref.shape[0]
    half = blocks // 2
    edge_count = base_ref.shape[1]
    first_step = 0 if first else SUB

    if first:
        total = state_ref[0, pl.ds(2 * NDIR, 40), :]
        for source in range(1, blocks):
            total = total + state_ref[source, pl.ds(2 * NDIR, 40), :]
        rolled = [total] + [pltpu.roll(total, LANES - 32 * piece, 1) for piece in range(1, 4)]
        high, low = split_bf16(jnp.concatenate(rolled, axis=0))
        bound = jnp.concatenate([high, low], axis=0).astype(jnp.bfloat16)

    def spread(place):
        values = jnp.dot(bound, extra_ref[place], preferred_element_type=jnp.float32)
        values = values[0:160] + values[160:320]
        pieces = [values[40 * piece : 40 * piece + 40] for piece in range(4)]
        for out, pair in (
            (start_ref, (pieces[0], pieces[2])),
            (slope_ref, (pieces[1] - pieces[0], pieces[3] - pieces[2])),
        ):
            for side in range(2):
                for group in range(4):
                    out[place, group_rows(4 * side + group), :] = pair[side][8 * group : 8 * group + 8]
            out[place, pl.ds(64, 4), :] = pair[0][32:36]
            out[place, pl.ds(68, 4), :] = pair[1][32:36]

    def enter(place, _):
        if first:
            loss = jnp.broadcast_to(state_ref[place, pl.ds(3 * NDIR, 1), :], (GROUP_ROWS, LANES))
            values = load_natural(state_ref, place)
            spread(place)
        else:
            energy = jnp.broadcast_to(extra_ref[place, 0:1, :], (GROUP_ROWS, LANES))
            inverse = jnp.broadcast_to(extra_ref[place, 1:2, :], (GROUP_ROWS, LANES))
            loss = dissipation_rate(energy, inverse)
            values = [state_ref[place, group_rows(group), :] for group in range(GROUPS)]
        lower, upper, last = [jnp.exp(-rows_ref[2, group_rows(group), :] * loss) for group in (0, 4, 8)]
        decay = [lower] * 4 + [upper] * 4 + [last]
        for group in range(GROUPS):
            rows = group_rows(group)
            field[0, place, rows, :] = values[group] * growth_ref[place, rows, :] * decay[group]
        return 0

    lax.fori_loop(0, blocks, enter, 0)

    def fine_step(number, _):
        source = lax.rem(number, 2)
        time_frac = (number + (first_step + 1)).astype(jnp.float32) * (1.0 / (STEPS * SUB))
        for group in range(GROUPS):
            rows = group_rows(group)
            values = [field[source, place, rows, :] for place in range(blocks)]
            top = functools.reduce(jnp.maximum, values)
            top = jnp.maximum(jnp.max(top, axis=1, keepdims=True), 1e-30)
            scale = jnp.broadcast_to(65535.0 / top, (GROUP_ROWS, LANES))
            speed[rows, :] = rows_ref[3, rows, :] * (top * (1.0 / 65535.0))
            coded = [(value * scale + 0.5).astype(jnp.int32) for value in values]
            for place in range(half):
                words[place, rows, :] = (coded[place + half] << 16) | coded[place]

        def block(place, _):
            inflow = [None] * GROUPS
            for edge in range(edge_count):
                index = index_ref[place, edge]
                lanes = index & (LANES - 1)
                masks = [(index & (LANES << level)) != 0 for level in range(half.bit_length() - 1)]
                shift = (index >> (half.bit_length() + 6)) << 4

                def pick(low, level, rows):
                    if level == 0:
                        return take_lanes(words[low, rows, :], lanes)
                    step = 1 << (level - 1)
                    below = pick(low, level - 1, rows)
                    above = pick(low + step, level - 1, rows)
                    return jnp.where(masks[level - 1], above, below)

                for group in range(GROUPS):
                    word = pick(0, half.bit_length() - 1, group_rows(group))
                    value = (lax.shift_right_logical(word, shift) & 65535).astype(jnp.float32)
                    term = base_ref[place, edge, group_rows(BASE_GROUP[group]), :] * value
                    inflow[group] = term if inflow[group] is None else inflow[group] + term
            for group in range(GROUPS):
                rows = group_rows(group)
                field[1 - source, place, rows, :] = (
                    field[source, place, rows, :] * keep_ref[place, rows, :]
                    - speed[rows, :] * inflow[group]
                    + (start_ref[place, rows, :] + time_frac * slope_ref[place, rows, :])
                )
            return 0

        lax.fori_loop(0, blocks, block, 0)
        return 0

    lax.fori_loop(0, SUB, fine_step, 0)

    def leave(place, _):
        values = [field[SUB % 2, place, group_rows(group), :] for group in range(GROUPS)]
        if first:
            energy, inverse = None, None
            for group in range(GROUPS):
                rows = group_rows(group)
                out_ref[place, rows, :] = values[group]
                part = rows_ref[4, rows, :] * values[group]
                energy = part if energy is None else energy + part
                part = rows_ref[5, rows, :] * values[group]
                inverse = part if inverse is None else inverse + part
            sums_ref[place, 0:1, :] = jnp.sum(energy, axis=0, keepdims=True)
            sums_ref[place, 1:2, :] = jnp.sum(inverse, axis=0, keepdims=True)
        else:
            store_natural(out_ref, place, values)
        return 0

    lax.fori_loop(0, blocks, leave, 0)


def in_vmem(count):
    return [pl.BlockSpec(memory_space=pltpu.VMEM)] * count


def params():
    return pltpu.CompilerParams(vmem_limit_bytes=56 << 20)


def whole_frequencies(
    spectra_in,
    coarse_spectra,
    wind_speed,
    wind_heading,
    active,
    neighbours,
    edge_x,
    edge_y,
    bound_points,
    bound_cells,
    bound_weights,
):
    device_count = lax.axis_size("pts")
    device_place = lax.axis_index("pts")
    comp_total, point_count = spectra_in.shape
    local_count = comp_total // device_count
    edge_count, grid_points = neighbours.shape
    blocks = grid_points // LANES
    bound_count = bound_points.shape[0]
    f32 = jnp.float32
    first_point = (device_place * point_count).astype(jnp.int32).reshape(1)
    send = pl.pallas_call(
        pack_kernel,
        out_shape=jax.ShapeDtypeStruct((device_count, 112, LANES), f32),
        in_specs=[pl.BlockSpec(memory_space=pltpu.SMEM)] + in_vmem(4),
        out_specs=pl.BlockSpec(memory_space=pltpu.VMEM),
        scratch_shapes=[pltpu.VMEM((comp_total, LANES), f32)],
        compiler_params=params(),
    )(first_point, spectra_in, coarse_spectra, jnp.tile(bound_cells, (1, 4)), jnp.tile(bound_weights, (1, 4)))
    received = lax.all_to_all(send, "pts", split_axis=0, concat_axis=0, tiled=True)

    spread = bound_points[:, None] == jnp.arange(grid_points, dtype=jnp.int32)[None, :]
    select = jnp.pad(spread.astype(jnp.bfloat16), ((0, LANES - bound_count), (0, 0)))
    select = select.reshape(LANES, blocks, LANES).transpose(1, 0, 2)
    free = jnp.where(jnp.any(spread, axis=0), 0.0, active)
    per_point = jnp.stack([wind_speed, wind_heading, active, free]).reshape(4, blocks, LANES).transpose(1, 0, 2)
    edges = jnp.stack([edge_x, edge_y], axis=1).reshape(edge_count, 2, blocks, LANES).transpose(0, 2, 1, 3)
    rows = row_tables(device_place)
    keep, base, growth = pl.pallas_call(
        setup_kernel,
        out_shape=[
            jax.ShapeDtypeStruct((blocks, local_count, LANES), f32),
            jax.ShapeDtypeStruct((blocks, edge_count, 40, LANES), f32),
            jax.ShapeDtypeStruct((blocks, local_count, LANES), f32),
        ],
        in_specs=in_vmem(4),
        out_specs=in_vmem(3),
        compiler_params=params(),
        cost_estimate=pl.CostEstimate(flops=100_000_000, bytes_accessed=4_000_000, transcendentals=1_000_000),
    )(per_point, edges, rows, direction_tables())

    index = neighbours.reshape(edge_count, blocks, 1, LANES).transpose(1, 0, 2, 3)
    index = jnp.broadcast_to(index, (blocks, edge_count, GROUP_ROWS, LANES))

    def fine(first, state, extra, bound):
        state_shape = jax.ShapeDtypeStruct((blocks, local_count, LANES), f32)
        out_shape = [state_shape]
        if first:
            out_shape += [jax.ShapeDtypeStruct((blocks, 2, LANES), f32), state_shape, state_shape]
        return pl.pallas_call(
            functools.partial(fine_kernel, first),
            out_shape=out_shape,
            in_specs=in_vmem(7 + len(bound)),
            out_specs=in_vmem(len(out_shape)),
            scratch_shapes=[
                pltpu.VMEM((2, blocks, local_count, LANES), f32),
                pltpu.VMEM((blocks // 2, local_count, LANES), jnp.int32),
                pltpu.VMEM((local_count, LANES), f32),
            ],
            compiler_params=params(),
        )(state, extra, index, keep, base, growth, rows, *bound)

    field, sums, start, slope = fine(True, received, select, ())
    distance = 1
    while distance < device_count:
        pairs = [(place, place ^ distance) for place in range(device_count)]
        sums = sums + lax.ppermute(sums, "pts", pairs)
        distance *= 2
    (field,) = fine(False, field, sums, (start, slope))
    field = lax.all_to_all(field, "pts", split_axis=0, concat_axis=0, tiled=True)
    return field.reshape(comp_total, point_count)


def shards(
    spectra_in,
    coarse_spectra,
    wind_speed,
    wind_heading,
    sea_mask,
    neighbours,
    edge_x,
    edge_y,
    bound_points,
    bound_cells,
    bound_weights,
):
    device_count = lax.axis_size("pts")
    device_place = lax.axis_index("pts")
    point_count = spectra_in.shape[1]
    comp_total = spectra_in.shape[0]
    local_count = comp_total // device_count
    active = sea_mask.astype(jnp.float32)
    blocks = neighbours.shape[1] // LANES
    if (
        local_count == 2 * NDIR
        and point_count == LANES
        and 4 * bound_points.shape[0] == LANES
        and coarse_spectra.shape[2] == LANES
        and blocks == device_count
        and blocks & (blocks - 1) == 0
    ):
        return whole_frequencies(
            spectra_in,
            coarse_spectra,
            wind_speed,
            wind_heading,
            active,
            neighbours,
            edge_x,
            edge_y,
            bound_points,
            bound_cells,
            bound_weights,
        )
    all_comp = jnp.arange(comp_total, dtype=jnp.int32)
    my_comp = device_place * local_count + jnp.arange(local_count, dtype=jnp.int32)
    first_point = device_place * point_count
    own_speed = lax.dynamic_slice_in_dim(wind_speed, first_point, point_count)
    own_heading = lax.dynamic_slice_in_dim(wind_heading, first_point, point_count)
    own_active = lax.dynamic_slice_in_dim(active, first_point, point_count)
    coarse_here = lax.all_to_all(coarse_spectra, "pts", split_axis=1, concat_axis=2, tiled=True)
    bound_values = interpolate(coarse_here, bound_cells, bound_weights)
    outflow, inflow = coefficients(my_comp, edge_x, edge_y)
    spectra = spectra_in
    for coarse_step in range(STEPS):
        energy, inverse = statistics(spectra, all_comp)
        spectra = apply_sources(
            spectra, all_comp, energy, inverse, own_speed, own_heading, own_active
        )
        comp_field = to_components(spectra)
        comp_field = advect(
            comp_field,
            outflow,
            inflow,
            neighbours,
            active,
            bound_values,
            bound_points,
            coarse_step * SUB,
        )
        spectra = to_points(comp_field)
    return spectra


def solution(mesh):
    in_specs = (
        P(None, ("groups", "pts")),
        P(None, None, ("groups", "pts")),
        P("groups"),
        P("groups"),
        P(),
        P(),
        P(),
        P(),
        P(),
        P(),
        P(),
    )
    out_specs = P(None, ("groups", "pts"))
    return jax.shard_map(shards, mesh=mesh, in_specs=in_specs, out_specs=out_specs, check_vma=False)
```

```python
import functools
import math

import jax
import jax.numpy as jnp
import numpy as np
from jax import lax
from jax.experimental import pallas as pl
from jax.experimental.pallas import tpu as pltpu
from jax.sharding import PartitionSpec as P

NDIR = 36
NFREQ = 32
SUB = 4
STEPS = 2
LANES = 128


epsilon = 1e-06
courant = 0.1


def freq_tables(components):
    freq_index = (components // NDIR).astype(jnp.float32)
    dir_index = (components % NDIR).astype(jnp.float32)
    growth = jnp.log(jnp.asarray(1.1, jnp.float32))
    radian_freq = 0.25 * jnp.exp(freq_index * growth)
    freq_top = 0.25 * jnp.exp((NFREQ - 1) * growth)
    freq_total = NDIR * jnp.sum(0.25 * jnp.exp(jnp.arange(NFREQ).astype(jnp.float32) * growth))
    weight = radian_freq / freq_total
    dir_angle = dir_index * (2.0 * jnp.pi / NDIR)
    return (radian_freq, weight, dir_angle, freq_top)


def statistics(spectra, components):
    radian_freq, weight, dir_angle, freq_top = freq_tables(components)
    energy = jnp.sum(weight[:, None] * spectra, axis=0)
    inverse = jnp.sum((weight / radian_freq)[:, None] * spectra, axis=0)
    return (energy, inverse)


def apply_sources(spectra, components, energy, inverse, wind_speed, wind_heading, active):
    radian_freq, weight, dir_angle, freq_top = freq_tables(components)
    mean_freq = energy / (inverse + epsilon)
    mean_period = inverse / (energy + epsilon)
    steepness = energy * (0.5 * mean_freq) ** 2
    steep_ratio = steepness / (1.0 + steepness)
    relative = radian_freq / freq_top
    wind_in = (
        0.6
        * relative[:, None]
        * jax.nn.sigmoid(
            wind_speed[None, :]
            * jnp.cos(dir_angle[:, None] - wind_heading[None, :])
            * radian_freq[:, None]
            / 8.0
            - 1.0
        )
    )
    dissipation = (relative * relative)[:, None] * (mean_period * freq_top * steep_ratio)[None, :]
    return spectra * jnp.exp(wind_in - dissipation) * active[None, :]


def interpolate(coarse_block, bound_cells, bound_weights):
    norm_weights = bound_weights / jnp.sum(bound_weights, axis=0, keepdims=True)
    corners = coarse_block[:, :, bound_cells]
    return jnp.sum(norm_weights[None, None] * corners, axis=2)


def coefficients(components, edge_x, edge_y):
    radian_freq, weight, dir_angle, freq_top = freq_tables(components)
    group_speed = courant * 0.25 / radian_freq
    edge_coef = group_speed[None, :, None] * (
        jnp.cos(dir_angle)[None, :, None] * edge_x[:, None, :]
        + jnp.sin(dir_angle)[None, :, None] * edge_y[:, None, :]
    )
    return (jnp.sum(jnp.maximum(edge_coef, 0.0), axis=0), jnp.minimum(edge_coef, 0.0))


def advect(spectra, outflow, inflow, neighbours, active, bound_values, bound_points, start):
    edge_count = neighbours.shape[0]
    for sub_step in range(SUB):
        upwind = inflow[0] * spectra[:, neighbours[0]]
        for edge in range(1, edge_count):
            upwind = upwind + inflow[edge] * spectra[:, neighbours[edge]]
        spectra = (spectra - outflow * spectra - upwind) * active[None, :]
        time_frac = (start + sub_step + 1) / (STEPS * SUB)
        edge_values = (1.0 - time_frac) * bound_values[0] + time_frac * bound_values[1]
        spectra = spectra.at[:, bound_points].set(edge_values)
    return spectra


def to_components(spectra):
    return lax.all_to_all(spectra, "pts", split_axis=0, concat_axis=1, tiled=True)


def to_points(spectra):
    return lax.all_to_all(spectra, "pts", split_axis=1, concat_axis=0, tiled=True)


GROUPS = 9
GROUP_ROWS = 8
BASE_GROUP = (0, 1, 2, 3, 0, 1, 2, 3, 4)
LISTED = 1024
CHUNK = 256


def row_layout():
    dirs = np.zeros((GROUPS * GROUP_ROWS,), np.int32)
    upper = np.zeros((GROUPS * GROUP_ROWS,), np.int32)
    for row in range(GROUPS * GROUP_ROWS):
        group, sub = divmod(row, GROUP_ROWS)
        if group < 8:
            dirs[row] = 8 * (group % 4) + sub
            upper[row] = group // 4
        else:
            dirs[row] = 32 + sub % 4
            upper[row] = sub // 4
    return dirs, upper


def group_rows(group):
    return pl.ds(GROUP_ROWS * group, GROUP_ROWS)


def load_natural(ref, block):
    lower = [ref[block, group_rows(group), :] for group in range(4)]
    upper = [ref[block, pl.ds(NDIR + GROUP_ROWS * group, GROUP_ROWS), :] for group in range(4)]
    sub = lax.broadcasted_iota(jnp.int32, (GROUP_ROWS, LANES), 0)
    last = jnp.where(sub < 4, ref[block, pl.ds(32, 8), :], ref[block, pl.ds(64, 8), :])
    return lower + upper + [last]


def store_natural(ref, block, values):
    for group in range(4):
        ref[block, group_rows(group), :] = values[group]
    for group in range(4):
        ref[block, pl.ds(NDIR + GROUP_ROWS * group, GROUP_ROWS), :] = values[4 + group]
    ref[block, pl.ds(32, 4), :] = values[8][0:4]
    ref[block, pl.ds(68, 4), :] = values[8][4:8]


def row_tables(device_place):
    dirs, upper = row_layout()
    freq = (2 * device_place + jnp.asarray(upper)).astype(jnp.int32)
    radian_freq, weight, _, freq_top = freq_tables(freq * NDIR)
    relative = radian_freq / freq_top
    group_speed = courant * 0.25 / radian_freq
    table = jnp.stack([radian_freq, 0.6 * relative, relative * relative * freq_top, group_speed, weight, weight / radian_freq])
    return jnp.broadcast_to(table[:, :, None], table.shape + (LANES,))


def direction_tables():
    dirs, _ = row_layout()
    angle = dirs.astype(np.float64) * (2.0 * np.pi / NDIR)
    table = np.stack([np.cos(angle), np.sin(angle)]).astype(np.float32)
    return jnp.asarray(np.broadcast_to(table[:, :, None], table.shape + (LANES,)))


def setup_kernel(points_ref, x_ref, y_ref, rows_ref, dirs_ref, keep_ref, growth_ref):
    edge_count = x_ref.shape[0]

    def block(place, _):
        speed = spread_row(points_ref, 0, place) * 0.125
        heading = spread_row(points_ref, 1, place)
        active = spread_row(points_ref, 2, place)
        free = spread_row(points_ref, 3, place)
        along, across = speed * jnp.cos(heading), speed * jnp.sin(heading)
        total = []
        for group in (0, 1, 2, 3, 8):
            cosine, sine = dirs_ref[0, group_rows(group), :], dirs_ref[1, group_rows(group), :]
            out = jnp.zeros((GROUP_ROWS, LANES), jnp.float32)
            for edge in range(edge_count):
                flow = cosine * spread_row(x_ref, edge, place) + sine * spread_row(y_ref, edge, place)
                out = out + jnp.maximum(flow, 0.0)
            total.append(out)
        for group in range(GROUPS):
            rows = group_rows(group)
            cosine, sine = dirs_ref[0, rows, :], dirs_ref[1, rows, :]
            wind = (along * cosine + across * sine) * rows_ref[0, rows, :] - 1.0
            growth_ref[place, rows, :] = jnp.exp(rows_ref[1, rows, :] * jax.nn.sigmoid(wind)) * active
            keep_ref[place, rows, :] = (1.0 - rows_ref[3, rows, :] * total[BASE_GROUP[group]]) * free
        return 0

    lax.fori_loop(0, keep_ref.shape[0], block, 0)


def spread_row(ref, *place):
    row = ref[place[:-1] + (pl.ds(place[-1], 1), slice(None))]
    return jnp.broadcast_to(row, (GROUP_ROWS, LANES))


def split_three(values):
    high = values.astype(jnp.bfloat16).astype(jnp.float32)
    rest = values - high
    middle = rest.astype(jnp.bfloat16).astype(jnp.float32)
    return high, middle, rest - middle


def plan_kernel(
    near_ref,
    x_ref,
    y_ref,
    points_ref,
    dirs_ref,
    first_out,
    base_out,
    gather_out,
    scatter_out,
    listed_ref,
    fits_ref,
    first,
    base,
    gather,
    scatter,
    marks,
    places,
    values,
    picked,
    sems,
):
    f32, bf16 = jnp.float32, jnp.bfloat16
    edge_count, blocks, _ = near_ref.shape
    free = points_ref[3]
    high = [near_ref[edge] >> 7 for edge in range(edge_count)]

    def block(place, _):
        wanted = lax.broadcasted_iota(jnp.int32, (blocks, LANES), 0)
        lanes = jnp.zeros((blocks, LANES), jnp.int32)
        x = jnp.zeros((blocks, LANES), f32)
        y = jnp.zeros((blocks, LANES), f32)
        for edge in reversed(range(edge_count)):
            near = jnp.broadcast_to(near_ref[edge, pl.ds(place, 1), :], (blocks, LANES))
            hit = (near >> 7) == wanted
            lanes = jnp.where(hit, near & (LANES - 1), lanes)
            x = jnp.where(hit, jnp.broadcast_to(x_ref[edge, pl.ds(place, 1), :], (blocks, LANES)), x)
            y = jnp.where(hit, jnp.broadcast_to(y_ref[edge, pl.ds(place, 1), :], (blocks, LANES)), y)
        open_row = spread_row(points_ref, 3, place)
        for source in range(blocks):
            first[place, source] = jnp.broadcast_to(lanes[source : source + 1], (GROUP_ROWS, LANES))
            x_row = jnp.broadcast_to(x[source : source + 1], (GROUP_ROWS, LANES))
            y_row = jnp.broadcast_to(y[source : source + 1], (GROUP_ROWS, LANES))
            for group, rows in enumerate((0, 1, 2, 3, 8)):
                flow = dirs_ref[0, group_rows(rows), :] * x_row + dirs_ref[1, group_rows(rows), :] * y_row
                base[place, source, group_rows(group), :] = jnp.minimum(flow, 0.0) * open_row
        return 0

    lax.fori_loop(0, blocks, block, 0)
    copies = [pltpu.make_async_copy(first, first_out, sems.at[0]), pltpu.make_async_copy(base, base_out, sems.at[1])]
    for copy in copies:
        copy.start()

    marks[...] = jnp.zeros_like(marks)
    for edge in range(edge_count):
        again = jnp.zeros((blocks, LANES), jnp.bool_)
        for before in range(edge):
            again = again | (high[before] == high[edge])
        marks[pl.ds(blocks * edge, blocks), :] = jnp.where(again, free, 0.0)
        x_parts, y_parts = split_three(x_ref[edge]), split_three(y_ref[edge])
        rows = ((near_ref[edge] & (LANES - 1)).astype(f32), high[edge].astype(f32)) + x_parts + y_parts
        for place in range(blocks):
            side, column = divmod(place, blocks // 2)
            for number, row in enumerate(rows):
                values[side, pl.ds(8 * edge + number, 1), pl.ds(LANES * column, LANES)] = row[place : place + 1]
    left = lax.broadcasted_iota(jnp.int32, (LANES, LANES), 0)
    right = lax.broadcasted_iota(jnp.int32, (LANES, LANES), 1)
    mark = marks[...].astype(bf16)
    within = jnp.dot(mark, jnp.where(left < right, 1.0, 0.0).astype(bf16), preferred_element_type=f32)
    count = jnp.dot(mark, jnp.ones((LANES, LANES), bf16), preferred_element_type=f32)
    earlier = (right < left) & ((left & (blocks // 2)) == (right & (blocks // 2)))
    offset = jnp.dot(jnp.where(earlier, 1.0, 0.0).astype(bf16), count.astype(bf16), preferred_element_type=f32)
    position = jnp.where(marks[...] > 0.0, within + offset, -1.0)
    places[0] = position
    places[1] = offset
    fits_ref[0] = (jnp.max(position) < LISTED).astype(jnp.int32)

    rank = lax.broadcasted_iota(jnp.int32, (16, LANES), 0).astype(f32)

    def scatter_block(place, _):
        rows = [
            jnp.broadcast_to(places[0, pl.ds(blocks * edge + place, 1), :], (16, LANES)) for edge in range(edge_count)
        ]
        for tile in range(LISTED // 16):
            here = rank + float(16 * tile)
            hit = rows[0] == here
            for row in rows[1:]:
                hit = hit | (row == here)
            value = jnp.where(hit, 1.0, 0.0).astype(bf16)
            scatter[place // 2, pl.ds(16 * tile, 16), pl.ds(pl.multiple_of((place % 2) * LANES, LANES), LANES)] = value
        return 0

    lax.fori_loop(0, blocks, scatter_block, 0)
    copies.append(pltpu.make_async_copy(scatter, scatter_out, sems.at[2]))
    copies[-1].start()

    chunks = LISTED // CHUNK
    for side in range(2):
        wide = None
        for column in range(chunks):
            term = lax.dot_general(
                values[side, :, pl.ds(CHUNK * column, CHUNK)].astype(bf16),
                scatter[chunks * side + column],
                (((1,), (1,)), ((), ())),
                preferred_element_type=f32,
            )
            wide = term if wide is None else wide + term
        for column in range(LISTED // LANES):
            here = lax.broadcasted_iota(jnp.int32, (8, LANES), 1).astype(f32) + float(LANES * column)
            chosen = wide[0:8, LANES * column : LANES * (column + 1)]
            for edge in range(1, edge_count):
                begin = spread_row(places, 1, blocks * edge + (blocks // 2) * side)
                chosen = jnp.where(
                    here >= begin, wide[8 * edge : 8 * edge + 8, LANES * column : LANES * (column + 1)], chosen
                )
            spot = (LISTED // LANES) * side + column
            x_row = jnp.broadcast_to(chosen[2:3] + chosen[3:4] + chosen[4:5], (GROUP_ROWS, LANES))
            y_row = jnp.broadcast_to(chosen[5:6] + chosen[6:7] + chosen[7:8], (GROUP_ROWS, LANES))
            picked[pl.ds(spot, 1), :] = chosen[0:1] + float(LANES) * chosen[1:2]
            lane = slice(LANES * (column % 2), LANES * (column % 2) + LANES)
            for group, rows in enumerate((0, 1, 2, 3, 8)):
                flow = dirs_ref[0, group_rows(rows), :] * x_row + dirs_ref[1, group_rows(rows), :] * y_row
                listed_ref[spot // 2, group_rows(group), lane] = jnp.minimum(flow, 0.0)

    def gather_block(spot, _):
        source = jnp.broadcast_to(picked[pl.ds(spot, 1), :], (16, LANES))
        for tile in range(gather.shape[1] // 16):
            value = jnp.where(rank + float(16 * tile) == source, 1.0, 0.0).astype(bf16)
            gather[spot // 2, pl.ds(16 * tile, 16), pl.ds(pl.multiple_of((spot % 2) * LANES, LANES), LANES)] = value
        return 0

    lax.fori_loop(0, 2 * LISTED // LANES, gather_block, 0)
    copies.append(pltpu.make_async_copy(gather, gather_out, sems.at[3]))
    copies[-1].start()
    for copy in copies:
        copy.wait()


def frequency(place):
    return 0.25 * 1.1**place


FREQ_TOP = frequency(NFREQ - 1)
FREQ_TOTAL = NDIR * sum(frequency(place) for place in range(NFREQ))


def dissipation_rate(energy, inverse):
    mean_freq = energy / (inverse + epsilon)
    steepness = energy * (0.5 * mean_freq) * (0.5 * mean_freq)
    return inverse / (energy + epsilon) * (steepness / (1.0 + steepness))


def split_bf16(values):
    high = values.astype(jnp.bfloat16).astype(jnp.float32)
    return high, values - high


def pack_kernel(first_ref, spectra_ref, coarse_ref, cells_ref, weights_ref, send_ref, shares):
    destinations = send_ref.shape[0]
    f32 = jnp.float32
    lane = lax.broadcasted_iota(jnp.int32, (LANES, LANES), 1)
    cell = lax.broadcasted_iota(jnp.int32, (LANES, LANES), 0) + first_ref[0]
    norm = weights_ref[...] / jnp.sum(weights_ref[...], axis=0, keepdims=True)
    table = jnp.zeros((LANES, LANES), f32)
    for corner in range(cells_ref.shape[0]):
        hit = jnp.broadcast_to(cells_ref[corner : corner + 1, :], (LANES, LANES)) == cell
        table = table + jnp.where(hit, jnp.broadcast_to(norm[corner : corner + 1, :], (LANES, LANES)), 0.0)
    later = (lane & 32) != 0
    bf16 = jnp.bfloat16
    parts = [split_bf16(jnp.where(later, 0.0, table)), split_bf16(jnp.where(later, table, 0.0))]
    parts = [(high.astype(bf16), low.astype(bf16)) for high, low in parts]
    chunk = 8 * NDIR

    for start in range(0, spectra_ref.shape[0], chunk):
        result = None
        for time in range(2):
            high, low = split_bf16(coarse_ref[time, pl.ds(start, chunk), :])
            high, low = high.astype(bf16), low.astype(bf16)
            weight_high, weight_low = parts[time]
            for left, right in ((high, weight_high), (low, weight_high), (high, weight_low)):
                term = jnp.dot(left, right, preferred_element_type=f32)
                result = term if result is None else result + term
        shares[pl.ds(start, chunk), :] = result

    sub = lax.broadcasted_iota(jnp.int32, (GROUP_ROWS, LANES), 0) < 4
    energy = jnp.zeros((GROUP_ROWS, LANES), f32)
    inverse = jnp.zeros((GROUP_ROWS, LANES), f32)
    lower_lanes = lax.broadcasted_iota(jnp.int32, (NDIR, LANES), 1) < 64
    for place in range(destinations):
        start = 2 * NDIR * place
        values = [spectra_ref[pl.ds(start + GROUP_ROWS * group, GROUP_ROWS), :] for group in range(GROUPS)]
        for group in range(GROUPS):
            send_ref[place, group_rows(group), :] = values[group]
        lower = values[0] + values[1] + values[2] + values[3] + jnp.where(sub, values[4], 0.0)
        upper = values[5] + values[6] + values[7] + values[8] + jnp.where(sub, 0.0, values[4])
        energy = energy + frequency(2 * place) * lower + frequency(2 * place + 1) * upper
        inverse = inverse + (lower + upper)
        send_ref[place, pl.ds(2 * NDIR, NDIR), :] = jnp.where(
            lower_lanes, shares[pl.ds(start, NDIR), :], shares[pl.ds(start + NDIR, NDIR), :]
        )
    energy = jnp.sum(energy, axis=0, keepdims=True) * (1.0 / FREQ_TOTAL)
    inverse = jnp.sum(inverse, axis=0, keepdims=True) * (1.0 / FREQ_TOTAL)
    rate = jnp.broadcast_to(dissipation_rate(energy, inverse), (4, LANES))
    for place in range(destinations):
        send_ref[place, pl.ds(3 * NDIR, 4), :] = rate


def take_lanes(values, lanes):
    return jnp.take_along_axis(values, lanes, axis=1, mode="promise_in_bounds")


def fine_kernel(
    first,
    fits_ref,
    state_ref,
    extra_ref,
    near_ref,
    x_ref,
    y_ref,
    points_ref,
    dirs_ref,
    keep_ref,
    growth_ref,
    rows_ref,
    listed_ref,
    first_in,
    base_in,
    gather_in,
    scatter_in,
    *rest,
):
    if first:
        out_ref, sums_ref, start_ref, slope_ref = rest[:4]
    else:
        start_ref, slope_ref, out_ref = rest[:3]
    scratch = rest[4:] if first else rest[3:]
    field, words, speed, first_ref, base_ref, gather_ref, scatter_ref, pairs, inflow_ref, terms, sems = scratch
    f32, bf16 = jnp.float32, jnp.bfloat16
    blocks = keep_ref.shape[0]
    half = blocks // 2
    edge_count = near_ref.shape[0]
    first_step = 0 if first else SUB
    copies = [
        pltpu.make_async_copy(source, target, sems.at[number])
        for number, (source, target) in enumerate(
            ((first_in, first_ref), (base_in, base_ref), (gather_in, gather_ref), (scatter_in, scatter_ref))
        )
    ]
    for copy in copies:
        copy.start()

    if first:
        total = state_ref[0, pl.ds(2 * NDIR, 40), :]
        for source in range(1, blocks):
            total = total + state_ref[source, pl.ds(2 * NDIR, 40), :]
        rolled = [total] + [pltpu.roll(total, LANES - 32 * piece, 1) for piece in range(1, 4)]
        high, low = split_bf16(jnp.concatenate(rolled, axis=0))
        bound = jnp.concatenate([high, low], axis=0).astype(jnp.bfloat16)

    def spread(place):
        values = jnp.dot(bound, extra_ref[place], preferred_element_type=jnp.float32)
        values = values[0:160] + values[160:320]
        pieces = [values[40 * piece : 40 * piece + 40] for piece in range(4)]
        for out, pair in (
            (start_ref, (pieces[0], pieces[2])),
            (slope_ref, (pieces[1] - pieces[0], pieces[3] - pieces[2])),
        ):
            for side in range(2):
                for group in range(4):
                    out[place, group_rows(4 * side + group), :] = pair[side][8 * group : 8 * group + 8]
            out[place, pl.ds(64, 4), :] = pair[0][32:36]
            out[place, pl.ds(68, 4), :] = pair[1][32:36]

    def enter(place, _):
        if first:
            loss = jnp.broadcast_to(state_ref[place, pl.ds(3 * NDIR, 1), :], (GROUP_ROWS, LANES))
            values = load_natural(state_ref, place)
            spread(place)
        else:
            energy = jnp.broadcast_to(extra_ref[place, 0:1, :], (GROUP_ROWS, LANES))
            inverse = jnp.broadcast_to(extra_ref[place, 1:2, :], (GROUP_ROWS, LANES))
            loss = dissipation_rate(energy, inverse)
            values = [state_ref[place, group_rows(group), :] for group in range(GROUPS)]
        lower, upper, last = [jnp.exp(-rows_ref[2, group_rows(group), :] * loss) for group in (0, 4, 8)]
        decay = [lower] * 4 + [upper] * 4 + [last]
        for group in range(GROUPS):
            rows = group_rows(group)
            field[0, place, rows, :] = values[group] * growth_ref[place, rows, :] * decay[group]
        return 0

    lax.fori_loop(0, blocks, enter, 0)

    def boundary(place, rows, number):
        time_frac = (number + (first_step + 1)).astype(f32) * (1.0 / (STEPS * SUB))
        return start_ref[place, rows, :] + time_frac * slope_ref[place, rows, :]

    def encode(group, top_code):
        rows = group_rows(group)
        values = [field[0, place, rows, :] for place in range(blocks)]
        top = functools.reduce(jnp.maximum, values)
        top = jnp.maximum(jnp.max(top, axis=1, keepdims=True), 1e-30)
        scale = jnp.broadcast_to(top_code / top, (GROUP_ROWS, LANES))
        speed[rows, :] = rows_ref[3, rows, :] * (top * (1.0 / top_code))
        return [(value * scale + 0.5).astype(jnp.int32) for value in values]

    def fine_step(number, _):
        for group in range(4):
            lower, upper = encode(group, 65535.0), encode(group + 4, 65535.0)
            for place in range(blocks):
                pairs[place, group_rows(group), :] = (upper[place] << 16) | lower[place]
        for place in range(blocks):
            for group in range(GROUPS):
                high, low = split_bf16(field[0, place, group_rows(group), :])
                both = jnp.concatenate([high, low], axis=0).astype(bf16)
                words[pl.ds(16 * group, 16), pl.ds(LANES * place, LANES)] = both

        def collect(chunk, _):
            found = jnp.dot(words[...], gather_ref[chunk], preferred_element_type=f32)
            for group in range(GROUPS):
                value = found[16 * group : 16 * group + 8] + found[16 * group + 8 : 16 * group + 16]
                high, low = split_bf16(value * listed_ref[chunk, group_rows(BASE_GROUP[group]), :])
                terms[chunk, pl.ds(16 * group, 16), :] = jnp.concatenate([high, low], axis=0).astype(bf16)
            for side in range(2):
                place = 2 * chunk + side
                inflow = [jnp.zeros((GROUP_ROWS, LANES), f32)] * GROUPS
                for source in range(blocks):
                    lanes = first_ref[place, source]
                    for group in range(4):
                        base = base_ref[place, source, group_rows(group), :]
                        word = take_lanes(pairs[source, group_rows(group), :], lanes)
                        lower = (word & 65535).astype(f32)
                        upper = lax.shift_right_logical(word, 16).astype(f32)
                        inflow[group] = inflow[group] + base * lower
                        inflow[group + 4] = inflow[group + 4] + base * upper
                    last = take_lanes(field[0, source, group_rows(8), :], lanes)
                    inflow[8] = inflow[8] + base_ref[place, source, group_rows(4), :] * last
                for group in range(GROUPS):
                    factor = speed[group_rows(group), :] if group < 8 else rows_ref[3, group_rows(8), :]
                    inflow_ref[place, group_rows(group), :] = factor * inflow[group]
            return 0

        lax.fori_loop(0, blocks // 2, collect, 0)

        def update(chunk, _):
            chunks = LISTED // CHUNK
            begin = (chunk // chunks) * chunks
            moved = None
            for part in range(chunks):
                term = jnp.dot(
                    terms[begin + part],
                    scatter_ref[chunk, pl.ds(CHUNK * part, CHUNK), :],
                    preferred_element_type=f32,
                )
                moved = term if moved is None else moved + term
            for side in range(2):
                place = 2 * chunk + side
                lanes = slice(LANES * side, LANES * (side + 1))
                for group in range(GROUPS):
                    rows = group_rows(group)
                    more = moved[16 * group : 16 * group + 8, lanes] + moved[16 * group + 8 : 16 * group + 16, lanes]
                    field[0, place, rows, :] = (
                        field[0, place, rows, :] * keep_ref[place, rows, :]
                        - inflow_ref[place, rows, :]
                        - rows_ref[3, rows, :] * more
                        + boundary(place, rows, number)
                    )
            return 0

        lax.fori_loop(0, blocks // 2, update, 0)
        return 0

    def plain_step(number, _):
        def block(place, _):
            free = spread_row(points_ref, 3, place)
            inflow = [jnp.zeros((GROUP_ROWS, LANES), f32)] * GROUPS
            for edge in range(edge_count):
                near = spread_row(near_ref, edge, place)
                lanes, home = near & (LANES - 1), near >> 7
                x, y = spread_row(x_ref, edge, place), spread_row(y_ref, edge, place)
                for group in range(GROUPS):
                    rows = group_rows(group)
                    value = jnp.zeros((GROUP_ROWS, LANES), f32)
                    for source in range(blocks):
                        value = jnp.where(home == source, take_lanes(field[0, source, rows, :], lanes), value)
                    flow = dirs_ref[0, rows, :] * x + dirs_ref[1, rows, :] * y
                    inflow[group] = inflow[group] + jnp.minimum(flow, 0.0) * free * value
            for group in range(GROUPS):
                rows = group_rows(group)
                field[1, place, rows, :] = (
                    field[0, place, rows, :] * keep_ref[place, rows, :]
                    - rows_ref[3, rows, :] * inflow[group]
                    + boundary(place, rows, number)
                )
            return 0

        lax.fori_loop(0, blocks, block, 0)
        field[0] = field[1]
        return 0

    for copy in copies:
        copy.wait()
    fits = fits_ref[0]

    @pl.when(fits != 0)
    def _():
        lax.fori_loop(0, SUB, fine_step, 0)

    @pl.when(fits == 0)
    def _():
        lax.fori_loop(0, SUB, plain_step, 0)

    def leave(place, _):
        values = [field[0, place, group_rows(group), :] for group in range(GROUPS)]
        if first:
            energy, inverse = None, None
            for group in range(GROUPS):
                rows = group_rows(group)
                out_ref[place, rows, :] = values[group]
                part = rows_ref[4, rows, :] * values[group]
                energy = part if energy is None else energy + part
                part = rows_ref[5, rows, :] * values[group]
                inverse = part if inverse is None else inverse + part
            sums_ref[place, 0:1, :] = jnp.sum(energy, axis=0, keepdims=True)
            sums_ref[place, 1:2, :] = jnp.sum(inverse, axis=0, keepdims=True)
        else:
            store_natural(out_ref, place, values)
        return 0

    lax.fori_loop(0, blocks, leave, 0)


def in_vmem(count):
    return [pl.BlockSpec(memory_space=pltpu.VMEM)] * count


def params():
    return pltpu.CompilerParams(vmem_limit_bytes=56 << 20)


def whole_frequencies(
    spectra_in,
    coarse_spectra,
    wind_speed,
    wind_heading,
    active,
    neighbours,
    edge_x,
    edge_y,
    bound_points,
    bound_cells,
    bound_weights,
):
    device_count = lax.axis_size("pts")
    device_place = lax.axis_index("pts")
    comp_total, point_count = spectra_in.shape
    local_count = comp_total // device_count
    edge_count, grid_points = neighbours.shape
    blocks = grid_points // LANES
    bound_count = bound_points.shape[0]
    f32 = jnp.float32
    first_point = (device_place * point_count).astype(jnp.int32).reshape(1)
    send = pl.pallas_call(
        pack_kernel,
        out_shape=jax.ShapeDtypeStruct((device_count, 112, LANES), f32),
        in_specs=[pl.BlockSpec(memory_space=pltpu.SMEM)] + in_vmem(4),
        out_specs=pl.BlockSpec(memory_space=pltpu.VMEM),
        scratch_shapes=[pltpu.VMEM((comp_total, LANES), f32)],
        compiler_params=params(),
    )(first_point, spectra_in, coarse_spectra, jnp.tile(bound_cells, (1, 4)), jnp.tile(bound_weights, (1, 4)))
    received = lax.all_to_all(send, "pts", split_axis=0, concat_axis=0, tiled=True)

    spread = bound_points[:, None] == jnp.arange(grid_points, dtype=jnp.int32)[None, :]
    select = jnp.pad(spread.astype(jnp.bfloat16), ((0, LANES - bound_count), (0, 0)))
    select = select.reshape(LANES, blocks, LANES).transpose(1, 0, 2)
    free = jnp.where(jnp.any(spread, axis=0), 0.0, active)
    points = jnp.stack([wind_speed, wind_heading, active, free]).reshape(4, blocks, LANES)
    near, edge_x, edge_y = [array.reshape(edge_count, blocks, LANES) for array in (neighbours, edge_x, edge_y)]
    rows, dirs = row_tables(device_place), direction_tables()
    state_shape = jax.ShapeDtypeStruct((blocks, local_count, LANES), f32)
    keep, growth = pl.pallas_call(
        setup_kernel,
        out_shape=[state_shape] * 2,
        in_specs=in_vmem(5),
        out_specs=in_vmem(2),
        compiler_params=params(),
        cost_estimate=pl.CostEstimate(flops=100_000_000, bytes_accessed=4_000_000, transcendentals=1_000_000),
    )(points, edge_x, edge_y, rows, dirs)

    shapes = [
        ((blocks, blocks, GROUP_ROWS, LANES), jnp.int32),
        ((blocks, blocks, 40, LANES), f32),
        ((2 * LISTED // CHUNK, grid_points, CHUNK), jnp.bfloat16),
        ((grid_points // CHUNK, LISTED, CHUNK), jnp.bfloat16),
    ]
    tables = [pltpu.VMEM(shape, dtype) for shape, dtype in shapes]
    first_edge, base, gather, scatter, listed, fits = pl.pallas_call(
        plan_kernel,
        out_shape=[jax.ShapeDtypeStruct(shape, dtype) for shape, dtype in shapes]
        + [jax.ShapeDtypeStruct((2 * LISTED // CHUNK, 40, CHUNK), f32), jax.ShapeDtypeStruct((1,), jnp.int32)],
        in_specs=in_vmem(5),
        out_specs=[pl.BlockSpec(memory_space=pl.ANY)] * 4
        + [pl.BlockSpec(memory_space=pltpu.VMEM), pl.BlockSpec(memory_space=pltpu.SMEM)],
        scratch_shapes=tables
        + [
            pltpu.VMEM((LANES, LANES), f32),
            pltpu.VMEM((2, LANES, LANES), f32),
            pltpu.VMEM((2, 8 * edge_count, LISTED), f32),
            pltpu.VMEM((16, LANES), f32),
            pltpu.SemaphoreType.DMA((4,)),
        ],
        compiler_params=params(),
        cost_estimate=pl.CostEstimate(flops=1_000_000_000, bytes_accessed=20_000_000, transcendentals=0),
    )(near, edge_x, edge_y, points, dirs)

    def fine(is_first, state, extra, bound):
        out_shape = [state_shape]
        if is_first:
            out_shape += [jax.ShapeDtypeStruct((blocks, 2, LANES), f32), state_shape, state_shape]
        return pl.pallas_call(
            functools.partial(fine_kernel, is_first),
            out_shape=out_shape,
            in_specs=[pl.BlockSpec(memory_space=pltpu.SMEM)]
            + in_vmem(11)
            + [pl.BlockSpec(memory_space=pl.ANY)] * 4
            + in_vmem(len(bound)),
            out_specs=in_vmem(len(out_shape)),
            scratch_shapes=[
                pltpu.VMEM((2, blocks, local_count, LANES), f32),
                pltpu.VMEM((2 * local_count, grid_points), jnp.bfloat16),
                pltpu.VMEM((local_count, LANES), f32),
            ]
            + tables
            + [
                pltpu.VMEM((blocks, 32, LANES), jnp.int32),
                pltpu.VMEM((blocks, local_count, LANES), f32),
                pltpu.VMEM((2 * LISTED // CHUNK, 2 * local_count, CHUNK), jnp.bfloat16),
                pltpu.SemaphoreType.DMA((4,)),
            ],
            compiler_params=params(),
        )(
            fits,
            state,
            extra,
            near,
            edge_x,
            edge_y,
            points,
            dirs,
            keep,
            growth,
            rows,
            listed,
            first_edge,
            base,
            gather,
            scatter,
            *bound,
        )

    field, sums, start, slope = fine(True, received, select, ())
    distance = 1
    while distance < device_count:
        pairs = [(place, place ^ distance) for place in range(device_count)]
        sums = sums + lax.ppermute(sums, "pts", pairs)
        distance *= 2
    (field,) = fine(False, field, sums, (start, slope))
    field = lax.all_to_all(field, "pts", split_axis=0, concat_axis=0, tiled=True)
    return field.reshape(comp_total, point_count)


def shards(
    spectra_in,
    coarse_spectra,
    wind_speed,
    wind_heading,
    sea_mask,
    neighbours,
    edge_x,
    edge_y,
    bound_points,
    bound_cells,
    bound_weights,
):
    device_count = lax.axis_size("pts")
    device_place = lax.axis_index("pts")
    point_count = spectra_in.shape[1]
    comp_total = spectra_in.shape[0]
    local_count = comp_total // device_count
    active = sea_mask.astype(jnp.float32)
    blocks = neighbours.shape[1] // LANES
    if (
        local_count == 2 * NDIR
        and point_count == LANES
        and 4 * bound_points.shape[0] == LANES
        and coarse_spectra.shape[2] == LANES
        and blocks == device_count
        and blocks == 16
        and neighbours.shape[0] * blocks <= LANES
    ):
        return whole_frequencies(
            spectra_in,
            coarse_spectra,
            wind_speed,
            wind_heading,
            active,
            neighbours,
            edge_x,
            edge_y,
            bound_points,
            bound_cells,
            bound_weights,
        )
    all_comp = jnp.arange(comp_total, dtype=jnp.int32)
    my_comp = device_place * local_count + jnp.arange(local_count, dtype=jnp.int32)
    first_point = device_place * point_count
    own_speed = lax.dynamic_slice_in_dim(wind_speed, first_point, point_count)
    own_heading = lax.dynamic_slice_in_dim(wind_heading, first_point, point_count)
    own_active = lax.dynamic_slice_in_dim(active, first_point, point_count)
    coarse_here = lax.all_to_all(coarse_spectra, "pts", split_axis=1, concat_axis=2, tiled=True)
    bound_values = interpolate(coarse_here, bound_cells, bound_weights)
    outflow, inflow = coefficients(my_comp, edge_x, edge_y)
    spectra = spectra_in
    for coarse_step in range(STEPS):
        energy, inverse = statistics(spectra, all_comp)
        spectra = apply_sources(
            spectra, all_comp, energy, inverse, own_speed, own_heading, own_active
        )
        comp_field = to_components(spectra)
        comp_field = advect(
            comp_field,
            outflow,
            inflow,
            neighbours,
            active,
            bound_values,
            bound_points,
            coarse_step * SUB,
        )
        spectra = to_points(comp_field)
    return spectra


def solution(mesh):
    in_specs = (
        P(None, ("groups", "pts")),
        P(None, None, ("groups", "pts")),
        P("groups"),
        P("groups"),
        P(),
        P(),
        P(),
        P(),
        P(),
        P(),
        P(),
    )
    out_specs = P(None, ("groups", "pts"))
    return jax.shard_map(shards, mesh=mesh, in_specs=in_specs, out_specs=out_specs, check_vma=False)
```

```python
import functools
import math

import jax
import jax.numpy as jnp
import numpy as np
from jax import lax
from jax.experimental import pallas as pl
from jax.experimental.pallas import tpu as pltpu
from jax.sharding import PartitionSpec as P

NDIR = 36
NFREQ = 32
SUB = 4
STEPS = 2
LANES = 128


epsilon = 1e-06
courant = 0.1


def freq_tables(components):
    freq_index = (components // NDIR).astype(jnp.float32)
    dir_index = (components % NDIR).astype(jnp.float32)
    growth = jnp.log(jnp.asarray(1.1, jnp.float32))
    radian_freq = 0.25 * jnp.exp(freq_index * growth)
    freq_top = 0.25 * jnp.exp((NFREQ - 1) * growth)
    freq_total = NDIR * jnp.sum(0.25 * jnp.exp(jnp.arange(NFREQ).astype(jnp.float32) * growth))
    weight = radian_freq / freq_total
    dir_angle = dir_index * (2.0 * jnp.pi / NDIR)
    return (radian_freq, weight, dir_angle, freq_top)


def statistics(spectra, components):
    radian_freq, weight, dir_angle, freq_top = freq_tables(components)
    energy = jnp.sum(weight[:, None] * spectra, axis=0)
    inverse = jnp.sum((weight / radian_freq)[:, None] * spectra, axis=0)
    return (energy, inverse)


def apply_sources(spectra, components, energy, inverse, wind_speed, wind_heading, active):
    radian_freq, weight, dir_angle, freq_top = freq_tables(components)
    mean_freq = energy / (inverse + epsilon)
    mean_period = inverse / (energy + epsilon)
    steepness = energy * (0.5 * mean_freq) ** 2
    steep_ratio = steepness / (1.0 + steepness)
    relative = radian_freq / freq_top
    wind_in = (
        0.6
        * relative[:, None]
        * jax.nn.sigmoid(
            wind_speed[None, :]
            * jnp.cos(dir_angle[:, None] - wind_heading[None, :])
            * radian_freq[:, None]
            / 8.0
            - 1.0
        )
    )
    dissipation = (relative * relative)[:, None] * (mean_period * freq_top * steep_ratio)[None, :]
    return spectra * jnp.exp(wind_in - dissipation) * active[None, :]


def interpolate(coarse_block, bound_cells, bound_weights):
    norm_weights = bound_weights / jnp.sum(bound_weights, axis=0, keepdims=True)
    corners = coarse_block[:, :, bound_cells]
    return jnp.sum(norm_weights[None, None] * corners, axis=2)


def coefficients(components, edge_x, edge_y):
    radian_freq, weight, dir_angle, freq_top = freq_tables(components)
    group_speed = courant * 0.25 / radian_freq
    edge_coef = group_speed[None, :, None] * (
        jnp.cos(dir_angle)[None, :, None] * edge_x[:, None, :]
        + jnp.sin(dir_angle)[None, :, None] * edge_y[:, None, :]
    )
    return (jnp.sum(jnp.maximum(edge_coef, 0.0), axis=0), jnp.minimum(edge_coef, 0.0))


def advect(spectra, outflow, inflow, neighbours, active, bound_values, bound_points, start):
    edge_count = neighbours.shape[0]
    for sub_step in range(SUB):
        upwind = inflow[0] * spectra[:, neighbours[0]]
        for edge in range(1, edge_count):
            upwind = upwind + inflow[edge] * spectra[:, neighbours[edge]]
        spectra = (spectra - outflow * spectra - upwind) * active[None, :]
        time_frac = (start + sub_step + 1) / (STEPS * SUB)
        edge_values = (1.0 - time_frac) * bound_values[0] + time_frac * bound_values[1]
        spectra = spectra.at[:, bound_points].set(edge_values)
    return spectra


def to_components(spectra):
    return lax.all_to_all(spectra, "pts", split_axis=0, concat_axis=1, tiled=True)


def to_points(spectra):
    return lax.all_to_all(spectra, "pts", split_axis=1, concat_axis=0, tiled=True)


GROUPS = 9
GROUP_ROWS = 8
BASE_GROUP = (0, 1, 2, 3, 0, 1, 2, 3, 4)
LISTED = 768
CHUNK = 256


def group_rows(group):
    return pl.ds(GROUP_ROWS * group, GROUP_ROWS)


def load_natural(ref, block):
    lower = [ref[block, group_rows(group), :] for group in range(4)]
    upper = [ref[block, pl.ds(NDIR + GROUP_ROWS * group, GROUP_ROWS), :] for group in range(4)]
    sub = lax.broadcasted_iota(jnp.int32, (GROUP_ROWS, LANES), 0)
    last = jnp.where(sub < 4, ref[block, pl.ds(32, 8), :], ref[block, pl.ds(64, 8), :])
    return lower + upper + [last]


def store_natural(ref, block, values):
    for group in range(4):
        ref[block, group_rows(group), :] = values[group]
    for group in range(4):
        ref[block, pl.ds(NDIR + GROUP_ROWS * group, GROUP_ROWS), :] = values[4 + group]
    ref[block, pl.ds(32, 4), :] = values[8][0:4]
    ref[block, pl.ds(68, 4), :] = values[8][4:8]


def frequency(place):
    return 0.25 * 1.1**place


FREQ_TOP = frequency(NFREQ - 1)
FREQ_TOTAL = NDIR * sum(frequency(place) for place in range(NFREQ))


def setup_kernel(
    place_ref,
    bound_ref,
    speed_ref,
    heading_ref,
    mask_ref,
    near_in,
    x_in,
    y_in,
    keep_ref,
    growth_ref,
    rows_ref,
    dirs_ref,
    points_ref,
    select_ref,
    near_ref,
    x_ref,
    y_ref,
):
    f32 = jnp.float32
    edge_count = near_ref.shape[0]
    blocks = keep_ref.shape[0]
    sub = lax.broadcasted_iota(jnp.int32, (GROUP_ROWS, LANES), 0)
    for group in range(GROUPS):
        rows = group_rows(group)
        upper = jnp.where(sub < 4, 0, 1) if group == 8 else jnp.full((GROUP_ROWS, LANES), group // 4, jnp.int32)
        number = 32 + (sub & 3) if group == 8 else 8 * (group % 4) + sub
        radian_freq = 0.25 * jnp.exp((2 * place_ref[0] + upper).astype(f32) * math.log(1.1))
        relative = radian_freq * (1.0 / FREQ_TOP)
        rows_ref[0, rows, :] = radian_freq
        rows_ref[1, rows, :] = 0.6 * relative
        rows_ref[2, rows, :] = relative * relative * FREQ_TOP
        rows_ref[3, rows, :] = courant * 0.25 / radian_freq
        rows_ref[4, rows, :] = radian_freq * (1.0 / FREQ_TOTAL)
        rows_ref[5, rows, :] = jnp.full((GROUP_ROWS, LANES), 1.0 / FREQ_TOTAL, f32)
        angle = number.astype(f32) * (2.0 * math.pi / NDIR)
        dirs_ref[0, rows, :] = jnp.cos(angle)
        dirs_ref[1, rows, :] = jnp.sin(angle)

    for place in range(blocks):
        lanes = slice(LANES * place, LANES * (place + 1))
        for source, target in ((near_in, near_ref), (x_in, x_ref), (y_in, y_ref)):
            tile = source[:, lanes]
            for edge in range(edge_count):
                target[edge, place : place + 1, :] = tile[edge : edge + 1]

    count = bound_ref.shape[0]
    order = lax.broadcasted_iota(jnp.int32, (count, LANES), 0)
    lane = lax.broadcasted_iota(jnp.int32, (count, LANES), 1)
    spots = jnp.zeros((count, LANES), jnp.int32)
    for number in range(count):
        spots = jnp.where(order == number, bound_ref[number], spots)
    rest = jnp.zeros((LANES - count, LANES), f32)

    def block(place, _):
        hit = jnp.where(spots == lane + LANES * place, 1.0, 0.0)
        select_ref[place] = jnp.concatenate([hit, rest], axis=0).astype(jnp.bfloat16)
        fixed = jnp.max(hit, axis=0, keepdims=True) > 0.0
        sea = mask_ref[pl.ds(place, 1), :].astype(f32)
        open_row = jnp.where(fixed, 0.0, sea)
        points_ref[0, pl.ds(place, 1), :] = sea
        points_ref[1, pl.ds(place, 1), :] = open_row
        points_ref[2, pl.ds(place, 1), :] = jnp.where(fixed, 1.0, sea)
        active = jnp.broadcast_to(sea, (GROUP_ROWS, LANES))
        free = jnp.broadcast_to(open_row, (GROUP_ROWS, LANES))
        speed = spread_row(speed_ref, place) * 0.125
        heading = spread_row(heading_ref, place)
        along, across = speed * jnp.cos(heading), speed * jnp.sin(heading)
        total = []
        for group in (0, 1, 2, 3, 8):
            cosine, sine = dirs_ref[0, group_rows(group), :], dirs_ref[1, group_rows(group), :]
            out = jnp.zeros((GROUP_ROWS, LANES), f32)
            for edge in range(edge_count):
                flow = cosine * spread_row(x_ref, edge, place) + sine * spread_row(y_ref, edge, place)
                out = out + jnp.maximum(flow, 0.0)
            total.append(out)
        for group in range(GROUPS):
            rows = group_rows(group)
            cosine, sine = dirs_ref[0, rows, :], dirs_ref[1, rows, :]
            wind = (along * cosine + across * sine) * rows_ref[0, rows, :] - 1.0
            growth_ref[place, rows, :] = jnp.exp(rows_ref[1, rows, :] * jax.nn.sigmoid(wind)) * active
            keep_ref[place, rows, :] = (1.0 - rows_ref[3, rows, :] * total[BASE_GROUP[group]]) * free
        return 0

    lax.fori_loop(0, blocks, block, 0)


def spread_row(ref, *place):
    row = ref[place[:-1] + (pl.ds(place[-1], 1), slice(None))]
    return jnp.broadcast_to(row, (GROUP_ROWS, LANES))


def split_three(values):
    high = values.astype(jnp.bfloat16).astype(jnp.float32)
    rest = values - high
    middle = rest.astype(jnp.bfloat16).astype(jnp.float32)
    return high, middle, rest - middle


def plan_kernel(
    near_ref,
    x_ref,
    y_ref,
    points_ref,
    dirs_ref,
    first_out,
    base_out,
    gather_out,
    scatter_out,
    listed_ref,
    fits_ref,
    first,
    base,
    gather,
    scatter,
    marks,
    places,
    values,
    picked,
    homes,
    sems,
):
    f32, bf16 = jnp.float32, jnp.bfloat16
    edge_count, blocks, _ = near_ref.shape
    for edge in range(edge_count):
        for part in range(blocks // GROUP_ROWS):
            rows = pl.ds(GROUP_ROWS * part, GROUP_ROWS)
            near = near_ref[edge, rows, :]
            lanes, home = near & (LANES - 1), near >> 7
            alive = jnp.zeros((GROUP_ROWS, LANES), f32)
            for source in range(blocks):
                alive = jnp.where(home == source, take_lanes(spread_row(points_ref, 2, source), lanes), alive)
            homes[edge, rows, :] = jnp.where(alive * points_ref[1, rows, :] > 0.0, home, -1)
    high = [homes[edge] for edge in range(edge_count)]

    def block(place, _):
        wanted = lax.broadcasted_iota(jnp.int32, (blocks, LANES), 0)
        lanes = jnp.zeros((blocks, LANES), jnp.int32)
        x = jnp.zeros((blocks, LANES), f32)
        y = jnp.zeros((blocks, LANES), f32)
        for edge in reversed(range(edge_count)):
            near = jnp.broadcast_to(near_ref[edge, pl.ds(place, 1), :], (blocks, LANES))
            hit = jnp.broadcast_to(homes[edge, pl.ds(place, 1), :], (blocks, LANES)) == wanted
            lanes = jnp.where(hit, near & (LANES - 1), lanes)
            x = jnp.where(hit, jnp.broadcast_to(x_ref[edge, pl.ds(place, 1), :], (blocks, LANES)), x)
            y = jnp.where(hit, jnp.broadcast_to(y_ref[edge, pl.ds(place, 1), :], (blocks, LANES)), y)
        for source in range(blocks):
            first[place, source] = jnp.broadcast_to(lanes[source : source + 1], (GROUP_ROWS, LANES))
            x_row = jnp.broadcast_to(x[source : source + 1], (GROUP_ROWS, LANES))
            y_row = jnp.broadcast_to(y[source : source + 1], (GROUP_ROWS, LANES))
            for group, rows in enumerate((0, 1, 2, 3, 8)):
                flow = dirs_ref[0, group_rows(rows), :] * x_row + dirs_ref[1, group_rows(rows), :] * y_row
                base[place, source, group_rows(group), :] = jnp.minimum(flow, 0.0)
        return 0

    lax.fori_loop(0, blocks, block, 0)
    copies = [pltpu.make_async_copy(first, first_out, sems.at[0]), pltpu.make_async_copy(base, base_out, sems.at[1])]
    for copy in copies:
        copy.start()

    marks[...] = jnp.zeros_like(marks)
    for edge in range(edge_count):
        again = jnp.zeros((blocks, LANES), f32)
        for before in range(edge):
            again = jnp.where(high[before] == high[edge], 1.0, again)
        marks[pl.ds(blocks * edge, blocks), :] = jnp.where(high[edge] >= 0, again, 0.0)
        x_parts, y_parts = split_three(x_ref[edge]), split_three(y_ref[edge])
        rows = ((near_ref[edge] & (LANES - 1)).astype(f32), (near_ref[edge] >> 7).astype(f32)) + x_parts + y_parts
        for place in range(blocks):
            side, column = divmod(place, blocks // 2)
            for number, row in enumerate(rows):
                values[side, pl.ds(8 * edge + number, 1), pl.ds(LANES * column, LANES)] = row[place : place + 1]
    left = lax.broadcasted_iota(jnp.int32, (LANES, LANES), 0)
    right = lax.broadcasted_iota(jnp.int32, (LANES, LANES), 1)
    mark = marks[...].astype(bf16)
    within = jnp.dot(mark, jnp.where(left < right, 1.0, 0.0).astype(bf16), preferred_element_type=f32)
    count = jnp.dot(mark, jnp.ones((LANES, LANES), bf16), preferred_element_type=f32)
    earlier = (right < left) & ((left & (blocks // 2)) == (right & (blocks // 2)))
    offset = jnp.dot(jnp.where(earlier, 1.0, 0.0).astype(bf16), count.astype(bf16), preferred_element_type=f32)
    position = jnp.where(marks[...] > 0.0, within + offset, -1.0)
    places[0] = position
    places[1] = offset
    fits_ref[0] = (jnp.max(position) < LISTED).astype(jnp.int32)

    rank = lax.broadcasted_iota(jnp.int32, (16, LANES), 0).astype(f32)

    def scatter_block(place, _):
        rows = [
            jnp.broadcast_to(places[0, pl.ds(blocks * edge + place, 1), :], (16, LANES)) for edge in range(edge_count)
        ]
        for tile in range(LISTED // 16):
            here = rank + float(16 * tile)
            hit = rows[0] == here
            for row in rows[1:]:
                hit = hit | (row == here)
            value = jnp.where(hit, 1.0, 0.0).astype(bf16)
            scatter[place // 2, pl.ds(16 * tile, 16), pl.ds(pl.multiple_of((place % 2) * LANES, LANES), LANES)] = value
        return 0

    lax.fori_loop(0, blocks, scatter_block, 0)
    copies.append(pltpu.make_async_copy(scatter, scatter_out, sems.at[2]))
    copies[-1].start()

    chunks = blocks * LANES // (2 * CHUNK)
    for side in range(2):
        wide = None
        for column in range(chunks):
            term = lax.dot_general(
                values[side, :, pl.ds(CHUNK * column, CHUNK)].astype(bf16),
                scatter[chunks * side + column],
                (((1,), (1,)), ((), ())),
                preferred_element_type=f32,
            )
            wide = term if wide is None else wide + term
        for column in range(LISTED // LANES):
            here = lax.broadcasted_iota(jnp.int32, (8, LANES), 1).astype(f32) + float(LANES * column)
            chosen = wide[0:8, LANES * column : LANES * (column + 1)]
            for edge in range(1, edge_count):
                begin = spread_row(places, 1, blocks * edge + (blocks // 2) * side)
                chosen = jnp.where(
                    here >= begin, wide[8 * edge : 8 * edge + 8, LANES * column : LANES * (column + 1)], chosen
                )
            spot = (LISTED // LANES) * side + column
            x_row = jnp.broadcast_to(chosen[2:3] + chosen[3:4] + chosen[4:5], (GROUP_ROWS, LANES))
            y_row = jnp.broadcast_to(chosen[5:6] + chosen[6:7] + chosen[7:8], (GROUP_ROWS, LANES))
            picked[pl.ds(spot, 1), :] = chosen[0:1] + float(LANES) * chosen[1:2]
            lane = slice(LANES * (column % 2), LANES * (column % 2) + LANES)
            for group, rows in enumerate((0, 1, 2, 3, 8)):
                flow = dirs_ref[0, group_rows(rows), :] * x_row + dirs_ref[1, group_rows(rows), :] * y_row
                listed_ref[spot // 2, group_rows(group), lane] = jnp.minimum(flow, 0.0)

    def gather_block(spot, _):
        source = jnp.broadcast_to(picked[pl.ds(spot, 1), :], (16, LANES))
        for tile in range(gather.shape[1] // 16):
            value = jnp.where(rank + float(16 * tile) == source, 1.0, 0.0).astype(bf16)
            gather[spot // 2, pl.ds(16 * tile, 16), pl.ds(pl.multiple_of((spot % 2) * LANES, LANES), LANES)] = value
        return 0

    lax.fori_loop(0, 2 * LISTED // LANES, gather_block, 0)
    copies.append(pltpu.make_async_copy(gather, gather_out, sems.at[3]))
    copies[-1].start()
    for copy in copies:
        copy.wait()


def dissipation_rate(energy, inverse):
    mean_freq = energy / (inverse + epsilon)
    steepness = energy * (0.5 * mean_freq) * (0.5 * mean_freq)
    return inverse / (energy + epsilon) * (steepness / (1.0 + steepness))


def split_bf16(values):
    high = values.astype(jnp.bfloat16).astype(jnp.float32)
    return high, values - high


def pack_kernel(first_ref, spectra_ref, coarse_ref, cells_ref, weights_ref, send_ref, shares):
    destinations = send_ref.shape[0]
    f32 = jnp.float32
    lane = lax.broadcasted_iota(jnp.int32, (LANES, LANES), 1)
    cell = lax.broadcasted_iota(jnp.int32, (LANES, LANES), 0) + first_ref[0]
    weights = jnp.concatenate([weights_ref[...]] * 4, axis=1)
    norm = weights / jnp.sum(weights, axis=0, keepdims=True)
    cells = jnp.concatenate([cells_ref[...]] * 4, axis=1)
    table = jnp.zeros((LANES, LANES), f32)
    for corner in range(cells_ref.shape[0]):
        hit = jnp.broadcast_to(cells[corner : corner + 1], (LANES, LANES)) == cell
        table = table + jnp.where(hit, jnp.broadcast_to(norm[corner : corner + 1], (LANES, LANES)), 0.0)
    later = (lane & 32) != 0
    bf16 = jnp.bfloat16
    parts = [split_bf16(jnp.where(later, 0.0, table)), split_bf16(jnp.where(later, table, 0.0))]
    parts = [(high.astype(bf16), low.astype(bf16)) for high, low in parts]
    chunk = 8 * NDIR

    for start in range(0, spectra_ref.shape[0], chunk):
        result = None
        for time in range(2):
            high, low = split_bf16(coarse_ref[time, pl.ds(start, chunk), :])
            high, low = high.astype(bf16), low.astype(bf16)
            weight_high, weight_low = parts[time]
            for left, right in ((high, weight_high), (low, weight_high), (high, weight_low)):
                term = jnp.dot(left, right, preferred_element_type=f32)
                result = term if result is None else result + term
        shares[pl.ds(start, chunk), :] = result

    sub = lax.broadcasted_iota(jnp.int32, (GROUP_ROWS, LANES), 0) < 4
    energy = jnp.zeros((GROUP_ROWS, LANES), f32)
    inverse = jnp.zeros((GROUP_ROWS, LANES), f32)
    lower_lanes = lax.broadcasted_iota(jnp.int32, (NDIR, LANES), 1) < 64
    for place in range(destinations):
        start = 2 * NDIR * place
        values = [spectra_ref[pl.ds(start + GROUP_ROWS * group, GROUP_ROWS), :] for group in range(GROUPS)]
        for group in range(GROUPS):
            send_ref[place, group_rows(group), :] = values[group]
        lower = values[0] + values[1] + values[2] + values[3] + jnp.where(sub, values[4], 0.0)
        upper = values[5] + values[6] + values[7] + values[8] + jnp.where(sub, 0.0, values[4])
        energy = energy + frequency(2 * place) * lower + frequency(2 * place + 1) * upper
        inverse = inverse + (lower + upper)
        send_ref[place, pl.ds(2 * NDIR, NDIR), :] = jnp.where(
            lower_lanes, shares[pl.ds(start, NDIR), :], shares[pl.ds(start + NDIR, NDIR), :]
        )
    energy = jnp.sum(energy, axis=0, keepdims=True) * (1.0 / FREQ_TOTAL)
    inverse = jnp.sum(inverse, axis=0, keepdims=True) * (1.0 / FREQ_TOTAL)
    rate = jnp.broadcast_to(dissipation_rate(energy, inverse), (4, LANES))
    for place in range(destinations):
        send_ref[place, pl.ds(3 * NDIR, 4), :] = rate


def take_lanes(values, lanes):
    return jnp.take_along_axis(values, lanes, axis=1, mode="promise_in_bounds")


def fine_kernel(
    first,
    fits_ref,
    state_ref,
    extra_ref,
    near_ref,
    x_ref,
    y_ref,
    points_ref,
    dirs_ref,
    keep_ref,
    growth_ref,
    rows_ref,
    listed_ref,
    first_in,
    base_in,
    gather_in,
    scatter_in,
    *rest,
):
    if first:
        out_ref, sums_ref, start_ref, slope_ref = rest[:4]
    else:
        start_ref, slope_ref, out_ref = rest[:3]
    scratch = rest[4:] if first else rest[3:]
    field, words, speed, first_ref, base_ref, gather_ref, scatter_ref, pairs, ends, inflow_ref, terms, sems = scratch
    f32, bf16 = jnp.float32, jnp.bfloat16
    blocks = keep_ref.shape[0]
    half = blocks // 2
    edge_count = near_ref.shape[0]
    first_step = 0 if first else SUB
    halves = []
    for side in range(2):
        points = pl.ds(half * side, half)
        chunks = pl.ds(LISTED // CHUNK * side, LISTED // CHUNK)
        columns = pl.ds(half * LANES // CHUNK * side, half * LANES // CHUNK)
        halves.append(
            [
                pltpu.make_async_copy(source.at[part], target.at[part], sems.at[side, number])
                for number, (source, target, part) in enumerate(
                    (
                        (first_in, first_ref, points),
                        (base_in, base_ref, points),
                        (gather_in, gather_ref, chunks),
                        (scatter_in, scatter_ref, columns),
                    )
                )
            ]
        )
    order = halves[0][:3] + halves[1][:3] + halves[0][3:] + halves[1][3:]
    for copy in order:
        copy.start()

    if first:
        total = state_ref[0, pl.ds(2 * NDIR, 40), :]
        for source in range(1, blocks):
            total = total + state_ref[source, pl.ds(2 * NDIR, 40), :]
        rolled = [total] + [pltpu.roll(total, LANES - 32 * piece, 1) for piece in range(1, 4)]
        high, low = split_bf16(jnp.concatenate(rolled, axis=0))
        bound = jnp.concatenate([high, low], axis=0).astype(jnp.bfloat16)

    def spread(place):
        values = jnp.dot(bound, extra_ref[place], preferred_element_type=jnp.float32)
        values = values[0:160] + values[160:320]
        pieces = [values[40 * piece : 40 * piece + 40] for piece in range(4)]
        for out, pair in (
            (start_ref, (pieces[0], pieces[2])),
            (slope_ref, (pieces[1] - pieces[0], pieces[3] - pieces[2])),
        ):
            for side in range(2):
                for group in range(4):
                    out[place, group_rows(4 * side + group), :] = pair[side][8 * group : 8 * group + 8]
            out[place, pl.ds(64, 4), :] = pair[0][32:36]
            out[place, pl.ds(68, 4), :] = pair[1][32:36]

    def enter(place, _):
        if first:
            loss = jnp.broadcast_to(state_ref[place, pl.ds(3 * NDIR, 1), :], (GROUP_ROWS, LANES))
            values = load_natural(state_ref, place)
            spread(place)
        else:
            energy = jnp.broadcast_to(extra_ref[place, 0:1, :], (GROUP_ROWS, LANES))
            inverse = jnp.broadcast_to(extra_ref[place, 1:2, :], (GROUP_ROWS, LANES))
            loss = dissipation_rate(energy, inverse)
            values = [state_ref[place, group_rows(group), :] for group in range(GROUPS)]
        lower, upper, last = [jnp.exp(-rows_ref[2, group_rows(group), :] * loss) for group in (0, 4, 8)]
        decay = [lower] * 4 + [upper] * 4 + [last]
        for group in range(GROUPS):
            rows = group_rows(group)
            field[0, place, rows, :] = values[group] * growth_ref[place, rows, :] * decay[group]
        return 0

    lax.fori_loop(0, blocks, enter, 0)

    def boundary(place, rows, number):
        time_frac = (number + (first_step + 1)).astype(f32) * (1.0 / (STEPS * SUB))
        return start_ref[place, rows, :] + time_frac * slope_ref[place, rows, :]

    def encode(group, top_code):
        rows = group_rows(group)
        values = [field[0, place, rows, :] for place in range(blocks)]
        top = functools.reduce(jnp.maximum, values)
        top = jnp.maximum(jnp.max(top, axis=1, keepdims=True), 1e-30)
        scale = jnp.broadcast_to(top_code / top, (GROUP_ROWS, LANES))
        speed[rows, :] = rows_ref[3, rows, :] * (top * (1.0 / top_code))
        return [(value * scale + 0.5).astype(jnp.int32) for value in values]

    def collect(side):
        for chunk in range(LISTED // CHUNK * side, LISTED // CHUNK * (side + 1)):
            found = jnp.dot(words[...], gather_ref[chunk], preferred_element_type=f32)
            for group in range(GROUPS):
                value = found[16 * group : 16 * group + 8] + found[16 * group + 8 : 16 * group + 16]
                high, low = split_bf16(value * listed_ref[chunk, group_rows(BASE_GROUP[group]), :])
                terms[chunk, pl.ds(16 * group, 16), :] = jnp.concatenate([high, low], axis=0).astype(bf16)
        for place in range(half * side, half * (side + 1)):
            inflow = [jnp.zeros((GROUP_ROWS, LANES), f32)] * GROUPS
            for source in range(blocks):
                lanes = first_ref[place, source]
                for group in range(4):
                    base = base_ref[place, source, group_rows(group), :]
                    word = take_lanes(pairs[source, group_rows(group), :], lanes)
                    lower = (word & 65535).astype(f32)
                    upper = lax.shift_right_logical(word, 16).astype(f32)
                    inflow[group] = inflow[group] + base * lower
                    inflow[group + 4] = inflow[group + 4] + base * upper
                inflow[8] = inflow[8] + base_ref[place, source, group_rows(4), :] * take_lanes(ends[source], lanes)
            for group in range(GROUPS):
                factor = speed[group_rows(group), :] if group < 8 else rows_ref[3, group_rows(8), :]
                inflow_ref[place, group_rows(group), :] = factor * inflow[group]

    def update(side, number):
        parts = LISTED // CHUNK
        for chunk in range(half // 2 * side, half // 2 * (side + 1)):
            moved = None
            for part in range(parts):
                term = jnp.dot(
                    terms[parts * side + part],
                    scatter_ref[chunk, pl.ds(CHUNK * part, CHUNK), :],
                    preferred_element_type=f32,
                )
                moved = term if moved is None else moved + term
            for column in range(2):
                place = 2 * chunk + column
                lanes = slice(LANES * column, LANES * (column + 1))
                for group in range(GROUPS):
                    rows = group_rows(group)
                    more = moved[16 * group : 16 * group + 8, lanes] + moved[16 * group + 8 : 16 * group + 16, lanes]
                    field[0, place, rows, :] = (
                        field[0, place, rows, :] * keep_ref[place, rows, :]
                        - inflow_ref[place, rows, :]
                        - rows_ref[3, rows, :] * more
                        + boundary(place, rows, number)
                    )

    def fine_step(number, _):
        for group in range(4):
            lower, upper = encode(group, 65535.0), encode(group + 4, 65535.0)
            for place in range(blocks):
                pairs[place, group_rows(group), :] = (upper[place] << 16) | lower[place]
        for place in range(blocks):
            ends[place] = field[0, place, group_rows(8), :]
            for group in range(GROUPS):
                high, low = split_bf16(field[0, place, group_rows(group), :])
                both = jnp.concatenate([high, low], axis=0).astype(bf16)
                words[pl.ds(16 * group, 16), pl.ds(LANES * place, LANES)] = both

        def arrive(copies):
            @pl.when(number == 0)
            def _():
                for copy in copies:
                    copy.wait()

        arrive(order[:3])
        collect(0)
        arrive(order[3:7])
        update(0, number)
        collect(1)
        arrive(order[7:])
        update(1, number)
        return 0

    def plain_step(number, _):
        def block(place, _):
            free = spread_row(points_ref, 1, place)
            inflow = [jnp.zeros((GROUP_ROWS, LANES), f32)] * GROUPS
            for edge in range(edge_count):
                near = spread_row(near_ref, edge, place)
                lanes, home = near & (LANES - 1), near >> 7
                x, y = spread_row(x_ref, edge, place), spread_row(y_ref, edge, place)
                for group in range(GROUPS):
                    rows = group_rows(group)
                    value = jnp.zeros((GROUP_ROWS, LANES), f32)
                    for source in range(blocks):
                        value = jnp.where(home == source, take_lanes(field[0, source, rows, :], lanes), value)
                    flow = dirs_ref[0, rows, :] * x + dirs_ref[1, rows, :] * y
                    inflow[group] = inflow[group] + jnp.minimum(flow, 0.0) * free * value
            for group in range(GROUPS):
                rows = group_rows(group)
                field[1, place, rows, :] = (
                    field[0, place, rows, :] * keep_ref[place, rows, :]
                    - rows_ref[3, rows, :] * inflow[group]
                    + boundary(place, rows, number)
                )
            return 0

        lax.fori_loop(0, blocks, block, 0)
        field[0] = field[1]
        return 0

    fits = fits_ref[0]

    @pl.when(fits != 0)
    def _():
        lax.fori_loop(0, SUB, fine_step, 0)

    @pl.when(fits == 0)
    def _():
        for copy in order:
            copy.wait()
        lax.fori_loop(0, SUB, plain_step, 0)

    def leave(place, _):
        values = [field[0, place, group_rows(group), :] for group in range(GROUPS)]
        if first:
            energy, inverse = None, None
            for group in range(GROUPS):
                rows = group_rows(group)
                out_ref[place, rows, :] = values[group]
                part = rows_ref[4, rows, :] * values[group]
                energy = part if energy is None else energy + part
                part = rows_ref[5, rows, :] * values[group]
                inverse = part if inverse is None else inverse + part
            sums_ref[place, 0:1, :] = jnp.sum(energy, axis=0, keepdims=True)
            sums_ref[place, 1:2, :] = jnp.sum(inverse, axis=0, keepdims=True)
        else:
            store_natural(out_ref, place, values)
        return 0

    lax.fori_loop(0, blocks, leave, 0)


def in_vmem(count):
    return [pl.BlockSpec(memory_space=pltpu.VMEM)] * count


def params():
    return pltpu.CompilerParams(vmem_limit_bytes=56 << 20)


def whole_frequencies(
    spectra_in,
    coarse_spectra,
    wind_speed,
    wind_heading,
    sea_mask,
    neighbours,
    edge_x,
    edge_y,
    bound_points,
    bound_cells,
    bound_weights,
):
    device_count = lax.axis_size("pts")
    device_place = lax.axis_index("pts")
    comp_total, point_count = spectra_in.shape
    local_count = comp_total // device_count
    edge_count, grid_points = neighbours.shape
    blocks = grid_points // LANES
    bound_count = bound_points.shape[0]
    f32 = jnp.float32
    first_point = (device_place * point_count).astype(jnp.int32).reshape(1)
    send = pl.pallas_call(
        pack_kernel,
        out_shape=jax.ShapeDtypeStruct((device_count, 112, LANES), f32),
        in_specs=[pl.BlockSpec(memory_space=pltpu.SMEM)] + in_vmem(4),
        out_specs=pl.BlockSpec(memory_space=pltpu.VMEM),
        scratch_shapes=[pltpu.VMEM((comp_total, LANES), f32)],
        compiler_params=params(),
    )(first_point, spectra_in, coarse_spectra, bound_cells, bound_weights)
    received = lax.all_to_all(send, "pts", split_axis=0, concat_axis=0, tiled=True)

    by_block = (blocks, LANES)
    state_shape = jax.ShapeDtypeStruct((blocks, local_count, LANES), f32)
    edge_shape = (edge_count, blocks, LANES)
    keep, growth, rows, dirs, points, select, near, edge_x, edge_y = pl.pallas_call(
        setup_kernel,
        out_shape=[
            state_shape,
            state_shape,
            jax.ShapeDtypeStruct((6, local_count, LANES), f32),
            jax.ShapeDtypeStruct((2, local_count, LANES), f32),
            jax.ShapeDtypeStruct((3,) + by_block, f32),
            jax.ShapeDtypeStruct((blocks, LANES, LANES), jnp.bfloat16),
            jax.ShapeDtypeStruct(edge_shape, jnp.int32),
            jax.ShapeDtypeStruct(edge_shape, f32),
            jax.ShapeDtypeStruct(edge_shape, f32),
        ],
        in_specs=[pl.BlockSpec(memory_space=pltpu.SMEM)] * 2 + in_vmem(6),
        out_specs=in_vmem(9),
        compiler_params=params(),
        cost_estimate=pl.CostEstimate(flops=100_000_000, bytes_accessed=4_000_000, transcendentals=1_000_000),
    )(
        device_place.astype(jnp.int32).reshape(1),
        bound_points,
        wind_speed.reshape(by_block),
        wind_heading.reshape(by_block),
        sea_mask.reshape(by_block),
        neighbours,
        edge_x,
        edge_y,
    )

    shapes = [
        ((blocks, blocks, GROUP_ROWS, LANES), jnp.int32),
        ((blocks, blocks, 40, LANES), f32),
        ((2 * LISTED // CHUNK, grid_points, CHUNK), jnp.bfloat16),
        ((grid_points // CHUNK, LISTED, CHUNK), jnp.bfloat16),
    ]
    tables = [pltpu.VMEM(shape, dtype) for shape, dtype in shapes]
    first_edge, base, gather, scatter, listed, fits = pl.pallas_call(
        plan_kernel,
        out_shape=[jax.ShapeDtypeStruct(shape, dtype) for shape, dtype in shapes]
        + [jax.ShapeDtypeStruct((2 * LISTED // CHUNK, 40, CHUNK), f32), jax.ShapeDtypeStruct((1,), jnp.int32)],
        in_specs=in_vmem(5),
        out_specs=[pl.BlockSpec(memory_space=pl.ANY)] * 4
        + [pl.BlockSpec(memory_space=pltpu.VMEM), pl.BlockSpec(memory_space=pltpu.SMEM)],
        scratch_shapes=tables
        + [
            pltpu.VMEM((LANES, LANES), f32),
            pltpu.VMEM((2, LANES, LANES), f32),
            pltpu.VMEM((2, 8 * edge_count, grid_points // 2), f32),
            pltpu.VMEM((2 * LISTED // LANES, LANES), f32),
            pltpu.VMEM(edge_shape, jnp.int32),
            pltpu.SemaphoreType.DMA((4,)),
        ],
        compiler_params=params(),
        cost_estimate=pl.CostEstimate(flops=1_000_000_000, bytes_accessed=20_000_000, transcendentals=0),
    )(near, edge_x, edge_y, points, dirs)

    def fine(is_first, state, extra, bound):
        out_shape = [state_shape]
        if is_first:
            out_shape += [jax.ShapeDtypeStruct((blocks, 2, LANES), f32), state_shape, state_shape]
        return pl.pallas_call(
            functools.partial(fine_kernel, is_first),
            out_shape=out_shape,
            in_specs=[pl.BlockSpec(memory_space=pltpu.SMEM)]
            + in_vmem(11)
            + [pl.BlockSpec(memory_space=pl.ANY)] * 4
            + in_vmem(len(bound)),
            out_specs=in_vmem(len(out_shape)),
            scratch_shapes=[
                pltpu.VMEM((2, blocks, local_count, LANES), f32),
                pltpu.VMEM((2 * local_count, grid_points), jnp.bfloat16),
                pltpu.VMEM((local_count, LANES), f32),
            ]
            + tables
            + [
                pltpu.VMEM((blocks, 32, LANES), jnp.int32),
                pltpu.VMEM((blocks, GROUP_ROWS, LANES), f32),
                pltpu.VMEM((blocks, local_count, LANES), f32),
                pltpu.VMEM((2 * LISTED // CHUNK, 2 * local_count, CHUNK), jnp.bfloat16),
                pltpu.SemaphoreType.DMA((2, 4)),
            ],
            compiler_params=params(),
        )(
            fits,
            state,
            extra,
            near,
            edge_x,
            edge_y,
            points,
            dirs,
            keep,
            growth,
            rows,
            listed,
            first_edge,
            base,
            gather,
            scatter,
            *bound,
        )

    field, sums, start, slope = fine(True, received, select, ())
    distance = 1
    while distance < device_count:
        pairs = [(place, place ^ distance) for place in range(device_count)]
        sums = sums + lax.ppermute(sums, "pts", pairs)
        distance *= 2
    (field,) = fine(False, field, sums, (start, slope))
    field = lax.all_to_all(field, "pts", split_axis=0, concat_axis=0, tiled=True)
    return field.reshape(comp_total, point_count)


def shards(
    spectra_in,
    coarse_spectra,
    wind_speed,
    wind_heading,
    sea_mask,
    neighbours,
    edge_x,
    edge_y,
    bound_points,
    bound_cells,
    bound_weights,
):
    device_count = lax.axis_size("pts")
    device_place = lax.axis_index("pts")
    point_count = spectra_in.shape[1]
    comp_total = spectra_in.shape[0]
    local_count = comp_total // device_count
    active = sea_mask.astype(jnp.float32)
    blocks = neighbours.shape[1] // LANES
    if (
        local_count == 2 * NDIR
        and point_count == LANES
        and 4 * bound_points.shape[0] == LANES
        and coarse_spectra.shape[2] == LANES
        and blocks == device_count
        and blocks == 16
        and neighbours.shape[0] * blocks <= LANES
    ):
        return whole_frequencies(
            spectra_in,
            coarse_spectra,
            wind_speed,
            wind_heading,
            sea_mask,
            neighbours,
            edge_x,
            edge_y,
            bound_points,
            bound_cells,
            bound_weights,
        )
    all_comp = jnp.arange(comp_total, dtype=jnp.int32)
    my_comp = device_place * local_count + jnp.arange(local_count, dtype=jnp.int32)
    first_point = device_place * point_count
    own_speed = lax.dynamic_slice_in_dim(wind_speed, first_point, point_count)
    own_heading = lax.dynamic_slice_in_dim(wind_heading, first_point, point_count)
    own_active = lax.dynamic_slice_in_dim(active, first_point, point_count)
    coarse_here = lax.all_to_all(coarse_spectra, "pts", split_axis=1, concat_axis=2, tiled=True)
    bound_values = interpolate(coarse_here, bound_cells, bound_weights)
    outflow, inflow = coefficients(my_comp, edge_x, edge_y)
    spectra = spectra_in
    for coarse_step in range(STEPS):
        energy, inverse = statistics(spectra, all_comp)
        spectra = apply_sources(
            spectra, all_comp, energy, inverse, own_speed, own_heading, own_active
        )
        comp_field = to_components(spectra)
        comp_field = advect(
            comp_field,
            outflow,
            inflow,
            neighbours,
            active,
            bound_values,
            bound_points,
            coarse_step * SUB,
        )
        spectra = to_points(comp_field)
    return spectra


def solution(mesh):
    in_specs = (
        P(None, ("groups", "pts")),
        P(None, None, ("groups", "pts")),
        P("groups"),
        P("groups"),
        P(),
        P(),
        P(),
        P(),
        P(),
        P(),
        P(),
    )
    out_specs = P(None, ("groups", "pts"))
    return jax.shard_map(shards, mesh=mesh, in_specs=in_specs, out_specs=out_specs, check_vma=False)
```

```python
import functools
import math

import jax
import jax.numpy as jnp
import numpy as np
from jax import lax
from jax.experimental import pallas as pl
from jax.experimental.pallas import tpu as pltpu
from jax.sharding import PartitionSpec as P

NDIR = 36
NFREQ = 32
SUB = 4
STEPS = 2
LANES = 128


epsilon = 1e-06
courant = 0.1


def freq_tables(components):
    freq_index = (components // NDIR).astype(jnp.float32)
    dir_index = (components % NDIR).astype(jnp.float32)
    growth = jnp.log(jnp.asarray(1.1, jnp.float32))
    radian_freq = 0.25 * jnp.exp(freq_index * growth)
    freq_top = 0.25 * jnp.exp((NFREQ - 1) * growth)
    freq_total = NDIR * jnp.sum(0.25 * jnp.exp(jnp.arange(NFREQ).astype(jnp.float32) * growth))
    weight = radian_freq / freq_total
    dir_angle = dir_index * (2.0 * jnp.pi / NDIR)
    return (radian_freq, weight, dir_angle, freq_top)


def statistics(spectra, components):
    radian_freq, weight, dir_angle, freq_top = freq_tables(components)
    energy = jnp.sum(weight[:, None] * spectra, axis=0)
    inverse = jnp.sum((weight / radian_freq)[:, None] * spectra, axis=0)
    return (energy, inverse)


def apply_sources(spectra, components, energy, inverse, wind_speed, wind_heading, active):
    radian_freq, weight, dir_angle, freq_top = freq_tables(components)
    mean_freq = energy / (inverse + epsilon)
    mean_period = inverse / (energy + epsilon)
    steepness = energy * (0.5 * mean_freq) ** 2
    steep_ratio = steepness / (1.0 + steepness)
    relative = radian_freq / freq_top
    wind_in = (
        0.6
        * relative[:, None]
        * jax.nn.sigmoid(
            wind_speed[None, :]
            * jnp.cos(dir_angle[:, None] - wind_heading[None, :])
            * radian_freq[:, None]
            / 8.0
            - 1.0
        )
    )
    dissipation = (relative * relative)[:, None] * (mean_period * freq_top * steep_ratio)[None, :]
    return spectra * jnp.exp(wind_in - dissipation) * active[None, :]


def interpolate(coarse_block, bound_cells, bound_weights):
    norm_weights = bound_weights / jnp.sum(bound_weights, axis=0, keepdims=True)
    corners = coarse_block[:, :, bound_cells]
    return jnp.sum(norm_weights[None, None] * corners, axis=2)


def coefficients(components, edge_x, edge_y):
    radian_freq, weight, dir_angle, freq_top = freq_tables(components)
    group_speed = courant * 0.25 / radian_freq
    edge_coef = group_speed[None, :, None] * (
        jnp.cos(dir_angle)[None, :, None] * edge_x[:, None, :]
        + jnp.sin(dir_angle)[None, :, None] * edge_y[:, None, :]
    )
    return (jnp.sum(jnp.maximum(edge_coef, 0.0), axis=0), jnp.minimum(edge_coef, 0.0))


def advect(spectra, outflow, inflow, neighbours, active, bound_values, bound_points, start):
    edge_count = neighbours.shape[0]
    for sub_step in range(SUB):
        upwind = inflow[0] * spectra[:, neighbours[0]]
        for edge in range(1, edge_count):
            upwind = upwind + inflow[edge] * spectra[:, neighbours[edge]]
        spectra = (spectra - outflow * spectra - upwind) * active[None, :]
        time_frac = (start + sub_step + 1) / (STEPS * SUB)
        edge_values = (1.0 - time_frac) * bound_values[0] + time_frac * bound_values[1]
        spectra = spectra.at[:, bound_points].set(edge_values)
    return spectra


def to_components(spectra):
    return lax.all_to_all(spectra, "pts", split_axis=0, concat_axis=1, tiled=True)


def to_points(spectra):
    return lax.all_to_all(spectra, "pts", split_axis=1, concat_axis=0, tiled=True)


GROUPS = 9
GROUP_ROWS = 8
BASE_GROUP = (0, 1, 2, 3, 0, 1, 2, 3, 4)
LISTED = 768
CHUNK = 256


def group_rows(group):
    return pl.ds(GROUP_ROWS * group, GROUP_ROWS)


def load_natural(ref, block):
    lower = [ref[block, group_rows(group), :] for group in range(4)]
    upper = [ref[block, pl.ds(NDIR + GROUP_ROWS * group, GROUP_ROWS), :] for group in range(4)]
    sub = lax.broadcasted_iota(jnp.int32, (GROUP_ROWS, LANES), 0)
    last = jnp.where(sub < 4, ref[block, pl.ds(32, 8), :], ref[block, pl.ds(64, 8), :])
    return lower + upper + [last]


def store_natural(ref, block, values):
    for group in range(4):
        ref[block, group_rows(group), :] = values[group]
    for group in range(4):
        ref[block, pl.ds(NDIR + GROUP_ROWS * group, GROUP_ROWS), :] = values[4 + group]
    ref[block, pl.ds(32, 4), :] = values[8][0:4]
    ref[block, pl.ds(68, 4), :] = values[8][4:8]


def frequency(place):
    return 0.25 * 1.1**place


FREQ_TOP = frequency(NFREQ - 1)
FREQ_TOTAL = NDIR * sum(frequency(place) for place in range(NFREQ))


def setup_kernel(
    place_ref,
    bound_ref,
    speed_ref,
    heading_ref,
    mask_ref,
    near_in,
    x_in,
    y_in,
    keep_ref,
    growth_ref,
    rows_ref,
    dirs_ref,
    points_ref,
    select_ref,
    near_ref,
    x_ref,
    y_ref,
):
    f32 = jnp.float32
    edge_count = near_ref.shape[0]
    blocks = keep_ref.shape[0]
    sub = lax.broadcasted_iota(jnp.int32, (GROUP_ROWS, LANES), 0)
    for group in range(GROUPS):
        rows = group_rows(group)
        upper = jnp.where(sub < 4, 0, 1) if group == 8 else jnp.full((GROUP_ROWS, LANES), group // 4, jnp.int32)
        number = 32 + (sub & 3) if group == 8 else 8 * (group % 4) + sub
        radian_freq = 0.25 * jnp.exp((2 * place_ref[0] + upper).astype(f32) * math.log(1.1))
        relative = radian_freq * (1.0 / FREQ_TOP)
        rows_ref[0, rows, :] = radian_freq
        rows_ref[1, rows, :] = 0.6 * relative
        rows_ref[2, rows, :] = relative * relative * FREQ_TOP
        rows_ref[3, rows, :] = courant * 0.25 / radian_freq
        rows_ref[4, rows, :] = radian_freq * (1.0 / FREQ_TOTAL)
        rows_ref[5, rows, :] = jnp.full((GROUP_ROWS, LANES), 1.0 / FREQ_TOTAL, f32)
        angle = number.astype(f32) * (2.0 * math.pi / NDIR)
        dirs_ref[0, rows, :] = jnp.cos(angle)
        dirs_ref[1, rows, :] = jnp.sin(angle)

    for place in range(blocks):
        lanes = slice(LANES * place, LANES * (place + 1))
        for source, target in ((near_in, near_ref), (x_in, x_ref), (y_in, y_ref)):
            tile = source[:, lanes]
            for edge in range(edge_count):
                target[edge, place : place + 1, :] = tile[edge : edge + 1]

    count = bound_ref.shape[0]
    order = lax.broadcasted_iota(jnp.int32, (count, LANES), 0)
    lane = lax.broadcasted_iota(jnp.int32, (count, LANES), 1)
    spots = jnp.zeros((count, LANES), jnp.int32)
    for number in range(count):
        spots = jnp.where(order == number, bound_ref[number], spots)
    rest = jnp.zeros((LANES - count, LANES), f32)

    def block(place, _):
        hit = jnp.where(spots == lane + LANES * place, 1.0, 0.0)
        select_ref[place] = jnp.concatenate([hit, rest], axis=0).astype(jnp.bfloat16)
        fixed = jnp.max(hit, axis=0, keepdims=True) > 0.0
        sea = mask_ref[pl.ds(place, 1), :].astype(f32)
        open_row = jnp.where(fixed, 0.0, sea)
        points_ref[0, pl.ds(place, 1), :] = sea
        points_ref[1, pl.ds(place, 1), :] = open_row
        points_ref[2, pl.ds(place, 1), :] = jnp.where(fixed, 1.0, sea)
        active = jnp.broadcast_to(sea, (GROUP_ROWS, LANES))
        free = jnp.broadcast_to(open_row, (GROUP_ROWS, LANES))
        speed = spread_row(speed_ref, place) * 0.125
        heading = spread_row(heading_ref, place)
        along, across = speed * jnp.cos(heading), speed * jnp.sin(heading)
        total = []
        for group in (0, 1, 2, 3, 8):
            cosine, sine = dirs_ref[0, group_rows(group), :], dirs_ref[1, group_rows(group), :]
            out = jnp.zeros((GROUP_ROWS, LANES), f32)
            for edge in range(edge_count):
                flow = cosine * spread_row(x_ref, edge, place) + sine * spread_row(y_ref, edge, place)
                out = out + jnp.maximum(flow, 0.0)
            total.append(out)
        for group in range(GROUPS):
            rows = group_rows(group)
            cosine, sine = dirs_ref[0, rows, :], dirs_ref[1, rows, :]
            wind = (along * cosine + across * sine) * rows_ref[0, rows, :] - 1.0
            growth_ref[place, rows, :] = jnp.exp(rows_ref[1, rows, :] * jax.nn.sigmoid(wind)) * active
            keep_ref[place, rows, :] = (1.0 - rows_ref[3, rows, :] * total[BASE_GROUP[group]]) * free
        return 0

    lax.fori_loop(0, blocks, block, 0)


def spread_row(ref, *place):
    row = ref[place[:-1] + (pl.ds(place[-1], 1), slice(None))]
    return jnp.broadcast_to(row, (GROUP_ROWS, LANES))


def split_three(values):
    high = values.astype(jnp.bfloat16).astype(jnp.float32)
    rest = values - high
    middle = rest.astype(jnp.bfloat16).astype(jnp.float32)
    return high, middle, rest - middle


def plan_kernel(
    near_ref,
    x_ref,
    y_ref,
    points_ref,
    dirs_ref,
    first_ref,
    normal_ref,
    gather_out,
    scatter_out,
    listed_ref,
    fits_ref,
    gather,
    scatter,
    marks,
    places,
    values,
    picked,
    homes,
    sems,
):
    f32, bf16 = jnp.float32, jnp.bfloat16
    edge_count, blocks, _ = near_ref.shape
    for edge in range(edge_count):
        for part in range(blocks // GROUP_ROWS):
            rows = pl.ds(GROUP_ROWS * part, GROUP_ROWS)
            near = near_ref[edge, rows, :]
            lanes, home = near & (LANES - 1), near >> 7
            alive = jnp.zeros((GROUP_ROWS, LANES), f32)
            for source in range(blocks):
                alive = jnp.where(home == source, take_lanes(spread_row(points_ref, 2, source), lanes), alive)
            homes[edge, rows, :] = jnp.where(alive * points_ref[1, rows, :] > 0.0, home, -1)
    high = [homes[edge] for edge in range(edge_count)]

    def block(place, _):
        wanted = lax.broadcasted_iota(jnp.int32, (blocks, LANES), 0)
        lanes = jnp.zeros((blocks, LANES), jnp.int32)
        x = jnp.zeros((blocks, LANES), f32)
        y = jnp.zeros((blocks, LANES), f32)
        for edge in reversed(range(edge_count)):
            near = jnp.broadcast_to(near_ref[edge, pl.ds(place, 1), :], (blocks, LANES))
            hit = jnp.broadcast_to(homes[edge, pl.ds(place, 1), :], (blocks, LANES)) == wanted
            lanes = jnp.where(hit, near & (LANES - 1), lanes)
            x = jnp.where(hit, jnp.broadcast_to(x_ref[edge, pl.ds(place, 1), :], (blocks, LANES)), x)
            y = jnp.where(hit, jnp.broadcast_to(y_ref[edge, pl.ds(place, 1), :], (blocks, LANES)), y)
        first_ref[place] = lanes
        normal_ref[0, place] = x
        normal_ref[1, place] = y
        return 0

    lax.fori_loop(0, blocks, block, 0)
    copies = []

    marks[...] = jnp.zeros_like(marks)
    for edge in range(edge_count):
        again = jnp.zeros((blocks, LANES), f32)
        for before in range(edge):
            again = jnp.where(high[before] == high[edge], 1.0, again)
        marks[pl.ds(blocks * edge, blocks), :] = jnp.where(high[edge] >= 0, again, 0.0)
        x_parts, y_parts = split_three(x_ref[edge]), split_three(y_ref[edge])
        rows = ((near_ref[edge] & (LANES - 1)).astype(f32), (near_ref[edge] >> 7).astype(f32)) + x_parts + y_parts
        for place in range(blocks):
            side, column = divmod(place, blocks // 2)
            for number, row in enumerate(rows):
                values[side, pl.ds(8 * edge + number, 1), pl.ds(LANES * column, LANES)] = row[place : place + 1]
    left = lax.broadcasted_iota(jnp.int32, (LANES, LANES), 0)
    right = lax.broadcasted_iota(jnp.int32, (LANES, LANES), 1)
    mark = marks[...].astype(bf16)
    within = jnp.dot(mark, jnp.where(left < right, 1.0, 0.0).astype(bf16), preferred_element_type=f32)
    count = jnp.dot(mark, jnp.ones((LANES, LANES), bf16), preferred_element_type=f32)
    earlier = (right < left) & ((left & (blocks // 2)) == (right & (blocks // 2)))
    offset = jnp.dot(jnp.where(earlier, 1.0, 0.0).astype(bf16), count.astype(bf16), preferred_element_type=f32)
    position = jnp.where(marks[...] > 0.0, within + offset, -1.0)
    places[0] = position
    places[1] = offset
    fits_ref[0] = (jnp.max(position) < LISTED).astype(jnp.int32)

    rank = lax.broadcasted_iota(jnp.int32, (16, LANES), 0).astype(f32)

    def scatter_block(place, _):
        rows = [
            jnp.broadcast_to(places[0, pl.ds(blocks * edge + place, 1), :], (16, LANES)) for edge in range(edge_count)
        ]
        for tile in range(LISTED // 16):
            here = rank + float(16 * tile)
            hit = rows[0] == here
            for row in rows[1:]:
                hit = hit | (row == here)
            value = jnp.where(hit, 1.0, 0.0).astype(bf16)
            scatter[place // 2, pl.ds(16 * tile, 16), pl.ds(pl.multiple_of((place % 2) * LANES, LANES), LANES)] = value
        return 0

    lax.fori_loop(0, blocks, scatter_block, 0)
    copies.append(pltpu.make_async_copy(scatter, scatter_out, sems.at[0]))
    copies[-1].start()

    chunks = blocks * LANES // (2 * CHUNK)
    for side in range(2):
        wide = None
        for column in range(chunks):
            term = lax.dot_general(
                values[side, :, pl.ds(CHUNK * column, CHUNK)].astype(bf16),
                scatter[chunks * side + column],
                (((1,), (1,)), ((), ())),
                preferred_element_type=f32,
            )
            wide = term if wide is None else wide + term
        for column in range(LISTED // LANES):
            here = lax.broadcasted_iota(jnp.int32, (8, LANES), 1).astype(f32) + float(LANES * column)
            chosen = wide[0:8, LANES * column : LANES * (column + 1)]
            for edge in range(1, edge_count):
                begin = spread_row(places, 1, blocks * edge + (blocks // 2) * side)
                chosen = jnp.where(
                    here >= begin, wide[8 * edge : 8 * edge + 8, LANES * column : LANES * (column + 1)], chosen
                )
            spot = (LISTED // LANES) * side + column
            x_row = jnp.broadcast_to(chosen[2:3] + chosen[3:4] + chosen[4:5], (GROUP_ROWS, LANES))
            y_row = jnp.broadcast_to(chosen[5:6] + chosen[6:7] + chosen[7:8], (GROUP_ROWS, LANES))
            picked[pl.ds(spot, 1), :] = chosen[0:1] + float(LANES) * chosen[1:2]
            lane = slice(LANES * (column % 2), LANES * (column % 2) + LANES)
            for group, rows in enumerate((0, 1, 2, 3, 8)):
                flow = dirs_ref[0, group_rows(rows), :] * x_row + dirs_ref[1, group_rows(rows), :] * y_row
                listed_ref[spot // 2, group_rows(group), lane] = jnp.minimum(flow, 0.0)

    def gather_block(spot, _):
        source = jnp.broadcast_to(picked[pl.ds(spot, 1), :], (16, LANES))
        for tile in range(gather.shape[1] // 16):
            value = jnp.where(rank + float(16 * tile) == source, 1.0, 0.0).astype(bf16)
            gather[spot // 2, pl.ds(16 * tile, 16), pl.ds(pl.multiple_of((spot % 2) * LANES, LANES), LANES)] = value
        return 0

    lax.fori_loop(0, 2 * LISTED // LANES, gather_block, 0)
    copies.append(pltpu.make_async_copy(gather, gather_out, sems.at[1]))
    copies[-1].start()
    for copy in copies:
        copy.wait()


def dissipation_rate(energy, inverse):
    mean_freq = energy / (inverse + epsilon)
    steepness = energy * (0.5 * mean_freq) * (0.5 * mean_freq)
    return inverse / (energy + epsilon) * (steepness / (1.0 + steepness))


def split_bf16(values):
    high = values.astype(jnp.bfloat16).astype(jnp.float32)
    return high, values - high


def pack_kernel(first_ref, spectra_ref, coarse_ref, cells_ref, weights_ref, send_ref, shares):
    destinations = send_ref.shape[0]
    f32 = jnp.float32
    lane = lax.broadcasted_iota(jnp.int32, (LANES, LANES), 1)
    cell = lax.broadcasted_iota(jnp.int32, (LANES, LANES), 0) + first_ref[0]
    weights = jnp.concatenate([weights_ref[...]] * 4, axis=1)
    norm = weights / jnp.sum(weights, axis=0, keepdims=True)
    cells = jnp.concatenate([cells_ref[...]] * 4, axis=1)
    table = jnp.zeros((LANES, LANES), f32)
    for corner in range(cells_ref.shape[0]):
        hit = jnp.broadcast_to(cells[corner : corner + 1], (LANES, LANES)) == cell
        table = table + jnp.where(hit, jnp.broadcast_to(norm[corner : corner + 1], (LANES, LANES)), 0.0)
    later = (lane & 32) != 0
    bf16 = jnp.bfloat16
    parts = [split_bf16(jnp.where(later, 0.0, table)), split_bf16(jnp.where(later, table, 0.0))]
    parts = [(high.astype(bf16), low.astype(bf16)) for high, low in parts]
    chunk = 8 * NDIR

    for start in range(0, spectra_ref.shape[0], chunk):
        result = None
        for time in range(2):
            high, low = split_bf16(coarse_ref[time, pl.ds(start, chunk), :])
            high, low = high.astype(bf16), low.astype(bf16)
            weight_high, weight_low = parts[time]
            for left, right in ((high, weight_high), (low, weight_high), (high, weight_low)):
                term = jnp.dot(left, right, preferred_element_type=f32)
                result = term if result is None else result + term
        shares[pl.ds(start, chunk), :] = result

    sub = lax.broadcasted_iota(jnp.int32, (GROUP_ROWS, LANES), 0) < 4
    energy = jnp.zeros((GROUP_ROWS, LANES), f32)
    inverse = jnp.zeros((GROUP_ROWS, LANES), f32)
    lower_lanes = lax.broadcasted_iota(jnp.int32, (NDIR, LANES), 1) < 64
    for place in range(destinations):
        start = 2 * NDIR * place
        values = [spectra_ref[pl.ds(start + GROUP_ROWS * group, GROUP_ROWS), :] for group in range(GROUPS)]
        for group in range(GROUPS):
            send_ref[place, group_rows(group), :] = values[group]
        lower = values[0] + values[1] + values[2] + values[3] + jnp.where(sub, values[4], 0.0)
        upper = values[5] + values[6] + values[7] + values[8] + jnp.where(sub, 0.0, values[4])
        energy = energy + frequency(2 * place) * lower + frequency(2 * place + 1) * upper
        inverse = inverse + (lower + upper)
        send_ref[place, pl.ds(2 * NDIR, NDIR), :] = jnp.where(
            lower_lanes, shares[pl.ds(start, NDIR), :], shares[pl.ds(start + NDIR, NDIR), :]
        )
    energy = jnp.sum(energy, axis=0, keepdims=True) * (1.0 / FREQ_TOTAL)
    inverse = jnp.sum(inverse, axis=0, keepdims=True) * (1.0 / FREQ_TOTAL)
    rate = jnp.broadcast_to(dissipation_rate(energy, inverse), (4, LANES))
    for place in range(destinations):
        send_ref[place, pl.ds(3 * NDIR, 4), :] = rate


def take_lanes(values, lanes):
    return jnp.take_along_axis(values, lanes, axis=1, mode="promise_in_bounds")


def fine_kernel(
    first,
    fits_ref,
    state_ref,
    extra_ref,
    near_ref,
    x_ref,
    y_ref,
    points_ref,
    dirs_ref,
    keep_ref,
    growth_ref,
    rows_ref,
    listed_ref,
    first_ref,
    normal_ref,
    gather_in,
    scatter_in,
    *rest,
):
    if first:
        out_ref, sums_ref, start_ref, slope_ref = rest[:4]
    else:
        start_ref, slope_ref, out_ref = rest[:3]
    scratch = rest[4:] if first else rest[3:]
    field, words, speed, base_ref, gather_ref, scatter_ref, pairs, ends, inflow_ref, terms, moments, sems = scratch
    f32, bf16 = jnp.float32, jnp.bfloat16
    blocks = keep_ref.shape[0]
    half = blocks // 2
    edge_count = near_ref.shape[0]
    first_step = 0 if first else SUB
    halves = []
    for side in range(2):
        chunks = pl.ds(LISTED // CHUNK * side, LISTED // CHUNK)
        columns = pl.ds(half * LANES // CHUNK * side, half * LANES // CHUNK)
        halves.append(
            [
                pltpu.make_async_copy(source.at[part], target.at[part], sems.at[side, number])
                for number, (source, target, part) in enumerate(
                    (
                        (gather_in, gather_ref, chunks),
                        (scatter_in, scatter_ref, columns),
                    )
                )
            ]
        )
    order = [halves[0][0], halves[1][0], halves[0][1], halves[1][1]]
    for copy in order:
        copy.start()

    if first:
        total = state_ref[0, pl.ds(2 * NDIR, 40), :]
        for source in range(1, blocks):
            total = total + state_ref[source, pl.ds(2 * NDIR, 40), :]
        rolled = [total] + [pltpu.roll(total, LANES - 32 * piece, 1) for piece in range(1, 4)]
        high, low = split_bf16(jnp.concatenate(rolled, axis=0))
        bound = jnp.concatenate([high, low], axis=0).astype(jnp.bfloat16)

    else:
        total = extra_ref[0]
        for source in range(1, blocks):
            total = total + extra_ref[source]
        moments[...] = total

    def spread(place):
        values = jnp.dot(bound, extra_ref[place], preferred_element_type=jnp.float32)
        values = values[0:160] + values[160:320]
        pieces = [values[40 * piece : 40 * piece + 40] for piece in range(4)]
        for out, pair in (
            (start_ref, (pieces[0], pieces[2])),
            (slope_ref, (pieces[1] - pieces[0], pieces[3] - pieces[2])),
        ):
            for side in range(2):
                for group in range(4):
                    out[place, group_rows(4 * side + group), :] = pair[side][8 * group : 8 * group + 8]
            out[place, pl.ds(64, 4), :] = pair[0][32:36]
            out[place, pl.ds(68, 4), :] = pair[1][32:36]

    def enter(place, _):
        if first:
            loss = jnp.broadcast_to(state_ref[place, pl.ds(3 * NDIR, 1), :], (GROUP_ROWS, LANES))
            values = load_natural(state_ref, place)
            spread(place)
        else:
            loss = dissipation_rate(spread_row(moments, place), spread_row(moments, blocks + place))
            values = [state_ref[place, group_rows(group), :] for group in range(GROUPS)]
        lower, upper, last = [jnp.exp(-rows_ref[2, group_rows(group), :] * loss) for group in (0, 4, 8)]
        decay = [lower] * 4 + [upper] * 4 + [last]
        for group in range(GROUPS):
            rows = group_rows(group)
            field[0, place, rows, :] = values[group] * growth_ref[place, rows, :] * decay[group]
        for source in range(blocks):
            x, y = spread_row(normal_ref, 0, place, source), spread_row(normal_ref, 1, place, source)
            for group, number in enumerate((0, 1, 2, 3, 8)):
                flow = dirs_ref[0, group_rows(number), :] * x + dirs_ref[1, group_rows(number), :] * y
                base_ref[place, source, group_rows(group), :] = jnp.minimum(flow, 0.0)
        return 0

    lax.fori_loop(0, blocks, enter, 0)

    def boundary(place, rows, number):
        time_frac = jnp.asarray(number + (first_step + 1), jnp.int32).astype(f32) * (1.0 / (STEPS * SUB))
        return start_ref[place, rows, :] + time_frac * slope_ref[place, rows, :]

    def encode(group, top_code):
        rows = group_rows(group)
        values = [field[0, place, rows, :] for place in range(blocks)]
        top = functools.reduce(jnp.maximum, values)
        top = jnp.maximum(jnp.max(top, axis=1, keepdims=True), 1e-30)
        scale = jnp.broadcast_to(top_code / top, (GROUP_ROWS, LANES))
        speed[rows, :] = rows_ref[3, rows, :] * (top * (1.0 / top_code))
        return [(value * scale + 0.5).astype(jnp.int32) for value in values]

    def collect(side):
        for chunk in range(LISTED // CHUNK * side, LISTED // CHUNK * (side + 1)):
            found = jnp.dot(words[...], gather_ref[chunk], preferred_element_type=f32)
            for group in range(GROUPS):
                value = found[16 * group : 16 * group + 8] + found[16 * group + 8 : 16 * group + 16]
                high, low = split_bf16(value * listed_ref[chunk, group_rows(BASE_GROUP[group]), :])
                terms[chunk, pl.ds(16 * group, 16), :] = jnp.concatenate([high, low], axis=0).astype(bf16)
        for place in range(half * side, half * (side + 1)):
            inflow = [jnp.zeros((GROUP_ROWS, LANES), f32)] * GROUPS
            for source in range(blocks):
                lanes = spread_row(first_ref, place, source)
                for group in range(4):
                    base = base_ref[place, source, group_rows(group), :]
                    word = take_lanes(pairs[source, group_rows(group), :], lanes)
                    lower = (word & 65535).astype(f32)
                    upper = lax.shift_right_logical(word, 16).astype(f32)
                    inflow[group] = inflow[group] + base * lower
                    inflow[group + 4] = inflow[group + 4] + base * upper
                inflow[8] = inflow[8] + base_ref[place, source, group_rows(4), :] * take_lanes(ends[source], lanes)
            for group in range(GROUPS):
                factor = speed[group_rows(group), :] if group < 8 else rows_ref[3, group_rows(8), :]
                inflow_ref[place, group_rows(group), :] = factor * inflow[group]

    def update(side, number):
        parts = LISTED // CHUNK
        for chunk in range(half // 2 * side, half // 2 * (side + 1)):
            moved = None
            for part in range(parts):
                term = jnp.dot(
                    terms[parts * side + part],
                    scatter_ref[chunk, pl.ds(CHUNK * part, CHUNK), :],
                    preferred_element_type=f32,
                )
                moved = term if moved is None else moved + term
            for column in range(2):
                place = 2 * chunk + column
                lanes = slice(LANES * column, LANES * (column + 1))
                for group in range(GROUPS):
                    rows = group_rows(group)
                    more = moved[16 * group : 16 * group + 8, lanes] + moved[16 * group + 8 : 16 * group + 16, lanes]
                    field[0, place, rows, :] = (
                        field[0, place, rows, :] * keep_ref[place, rows, :]
                        - inflow_ref[place, rows, :]
                        - rows_ref[3, rows, :] * more
                        + boundary(place, rows, number)
                    )

    def fine_step(number, arrivals):
        for group in range(4):
            lower, upper = encode(group, 65535.0), encode(group + 4, 65535.0)
            for place in range(blocks):
                pairs[place, group_rows(group), :] = (upper[place] << 16) | lower[place]
        for place in range(blocks):
            ends[place] = field[0, place, group_rows(8), :]
            for group in range(GROUPS):
                high, low = split_bf16(field[0, place, group_rows(group), :])
                both = jnp.concatenate([high, low], axis=0).astype(bf16)
                words[pl.ds(16 * group, 16), pl.ds(LANES * place, LANES)] = both

        def arrive(count):
            for copy in arrivals[:count]:
                copy.wait()
            del arrivals[:count]

        arrive(1)
        collect(0)
        arrive(2)
        update(0, number)
        collect(1)
        arrive(1)
        update(1, number)

    def later_step(number, _):
        fine_step(number, [])
        return 0

    def plain_step(number, _):
        def block(place, _):
            free = spread_row(points_ref, 1, place)
            inflow = [jnp.zeros((GROUP_ROWS, LANES), f32)] * GROUPS
            for edge in range(edge_count):
                near = spread_row(near_ref, edge, place)
                lanes, home = near & (LANES - 1), near >> 7
                x, y = spread_row(x_ref, edge, place), spread_row(y_ref, edge, place)
                for group in range(GROUPS):
                    rows = group_rows(group)
                    value = jnp.zeros((GROUP_ROWS, LANES), f32)
                    for source in range(blocks):
                        value = jnp.where(home == source, take_lanes(field[0, source, rows, :], lanes), value)
                    flow = dirs_ref[0, rows, :] * x + dirs_ref[1, rows, :] * y
                    inflow[group] = inflow[group] + jnp.minimum(flow, 0.0) * free * value
            for group in range(GROUPS):
                rows = group_rows(group)
                field[1, place, rows, :] = (
                    field[0, place, rows, :] * keep_ref[place, rows, :]
                    - rows_ref[3, rows, :] * inflow[group]
                    + boundary(place, rows, number)
                )
            return 0

        lax.fori_loop(0, blocks, block, 0)
        field[0] = field[1]
        return 0

    fits = fits_ref[0]

    @pl.when(fits != 0)
    def _():
        fine_step(0, list(order))
        lax.fori_loop(1, SUB, later_step, 0)

    @pl.when(fits == 0)
    def _():
        for copy in order:
            copy.wait()
        lax.fori_loop(0, SUB, plain_step, 0)

    def leave(place, _):
        values = [field[0, place, group_rows(group), :] for group in range(GROUPS)]
        if first:
            energy, inverse = None, None
            for group in range(GROUPS):
                rows = group_rows(group)
                out_ref[place, rows, :] = values[group]
                part = rows_ref[4, rows, :] * values[group]
                energy = part if energy is None else energy + part
                part = rows_ref[5, rows, :] * values[group]
                inverse = part if inverse is None else inverse + part
            moments[pl.ds(place, 1), :] = jnp.sum(energy, axis=0, keepdims=True)
            moments[pl.ds(blocks + place, 1), :] = jnp.sum(inverse, axis=0, keepdims=True)
        else:
            store_natural(out_ref, place, values)
        return 0

    lax.fori_loop(0, blocks, leave, 0)
    if first:
        for target in range(sums_ref.shape[0]):
            sums_ref[target] = moments[...]


def in_vmem(count):
    return [pl.BlockSpec(memory_space=pltpu.VMEM)] * count


def params():
    return pltpu.CompilerParams(vmem_limit_bytes=56 << 20)


def whole_frequencies(
    spectra_in,
    coarse_spectra,
    wind_speed,
    wind_heading,
    sea_mask,
    neighbours,
    edge_x,
    edge_y,
    bound_points,
    bound_cells,
    bound_weights,
):
    device_count = lax.axis_size("pts")
    device_place = lax.axis_index("pts")
    comp_total, point_count = spectra_in.shape
    local_count = comp_total // device_count
    edge_count, grid_points = neighbours.shape
    blocks = grid_points // LANES
    bound_count = bound_points.shape[0]
    f32 = jnp.float32
    first_point = (device_place * point_count).astype(jnp.int32).reshape(1)
    send = pl.pallas_call(
        pack_kernel,
        out_shape=jax.ShapeDtypeStruct((device_count, 112, LANES), f32),
        in_specs=[pl.BlockSpec(memory_space=pltpu.SMEM)] + in_vmem(4),
        out_specs=pl.BlockSpec(memory_space=pltpu.VMEM),
        scratch_shapes=[pltpu.VMEM((comp_total, LANES), f32)],
        compiler_params=params(),
    )(first_point, spectra_in, coarse_spectra, bound_cells, bound_weights)
    received = lax.all_to_all(send, "pts", split_axis=0, concat_axis=0, tiled=True)

    by_block = (blocks, LANES)
    state_shape = jax.ShapeDtypeStruct((blocks, local_count, LANES), f32)
    edge_shape = (edge_count, blocks, LANES)
    keep, growth, rows, dirs, points, select, near, edge_x, edge_y = pl.pallas_call(
        setup_kernel,
        out_shape=[
            state_shape,
            state_shape,
            jax.ShapeDtypeStruct((6, local_count, LANES), f32),
            jax.ShapeDtypeStruct((2, local_count, LANES), f32),
            jax.ShapeDtypeStruct((3,) + by_block, f32),
            jax.ShapeDtypeStruct((blocks, LANES, LANES), jnp.bfloat16),
            jax.ShapeDtypeStruct(edge_shape, jnp.int32),
            jax.ShapeDtypeStruct(edge_shape, f32),
            jax.ShapeDtypeStruct(edge_shape, f32),
        ],
        in_specs=[pl.BlockSpec(memory_space=pltpu.SMEM)] * 2 + in_vmem(6),
        out_specs=in_vmem(9),
        compiler_params=params(),
        cost_estimate=pl.CostEstimate(flops=100_000_000, bytes_accessed=4_000_000, transcendentals=1_000_000),
    )(
        device_place.astype(jnp.int32).reshape(1),
        bound_points,
        wind_speed.reshape(by_block),
        wind_heading.reshape(by_block),
        sea_mask.reshape(by_block),
        neighbours,
        edge_x,
        edge_y,
    )

    shapes = [
        ((2 * LISTED // CHUNK, grid_points, CHUNK), jnp.bfloat16),
        ((grid_points // CHUNK, LISTED, CHUNK), jnp.bfloat16),
    ]
    tables = [pltpu.VMEM(shape, dtype) for shape, dtype in shapes]
    first_edge, normals, gather, scatter, listed, fits = pl.pallas_call(
        plan_kernel,
        out_shape=[
            jax.ShapeDtypeStruct((blocks,) + by_block, jnp.int32),
            jax.ShapeDtypeStruct((2, blocks) + by_block, f32),
        ]
        + [jax.ShapeDtypeStruct(shape, dtype) for shape, dtype in shapes]
        + [jax.ShapeDtypeStruct((2 * LISTED // CHUNK, 40, CHUNK), f32), jax.ShapeDtypeStruct((1,), jnp.int32)],
        in_specs=in_vmem(5),
        out_specs=in_vmem(2)
        + [pl.BlockSpec(memory_space=pl.ANY)] * 2
        + [pl.BlockSpec(memory_space=pltpu.VMEM), pl.BlockSpec(memory_space=pltpu.SMEM)],
        scratch_shapes=tables
        + [
            pltpu.VMEM((LANES, LANES), f32),
            pltpu.VMEM((2, LANES, LANES), f32),
            pltpu.VMEM((2, 8 * edge_count, grid_points // 2), f32),
            pltpu.VMEM((2 * LISTED // LANES, LANES), f32),
            pltpu.VMEM(edge_shape, jnp.int32),
            pltpu.SemaphoreType.DMA((2,)),
        ],
        compiler_params=params(),
        cost_estimate=pl.CostEstimate(flops=1_000_000_000, bytes_accessed=20_000_000, transcendentals=0),
    )(near, edge_x, edge_y, points, dirs)

    def fine(is_first, state, extra, bound):
        out_shape = [state_shape]
        if is_first:
            out_shape += [jax.ShapeDtypeStruct((device_count, 2 * blocks, LANES), f32), state_shape, state_shape]
        return pl.pallas_call(
            functools.partial(fine_kernel, is_first),
            out_shape=out_shape,
            in_specs=[pl.BlockSpec(memory_space=pltpu.SMEM)]
            + in_vmem(13)
            + [pl.BlockSpec(memory_space=pl.ANY)] * 2
            + in_vmem(len(bound)),
            out_specs=in_vmem(len(out_shape)),
            scratch_shapes=[
                pltpu.VMEM((2, blocks, local_count, LANES), f32),
                pltpu.VMEM((2 * local_count, grid_points), jnp.bfloat16),
                pltpu.VMEM((local_count, LANES), f32),
            ]
            + [pltpu.VMEM((blocks, blocks, 40, LANES), f32)]
            + tables
            + [
                pltpu.VMEM((blocks, 32, LANES), jnp.int32),
                pltpu.VMEM((blocks, GROUP_ROWS, LANES), f32),
                pltpu.VMEM((blocks, local_count, LANES), f32),
                pltpu.VMEM((2 * LISTED // CHUNK, 2 * local_count, CHUNK), jnp.bfloat16),
                pltpu.VMEM((2 * blocks, LANES), f32),
                pltpu.SemaphoreType.DMA((2, 2)),
            ],
            compiler_params=params(),
        )(
            fits,
            state,
            extra,
            near,
            edge_x,
            edge_y,
            points,
            dirs,
            keep,
            growth,
            rows,
            listed,
            first_edge,
            normals,
            gather,
            scatter,
            *bound,
        )

    field, sums, start, slope = fine(True, received, select, ())
    sums = lax.all_to_all(sums, "pts", split_axis=0, concat_axis=0, tiled=True)
    (field,) = fine(False, field, sums, (start, slope))
    field = lax.all_to_all(field, "pts", split_axis=0, concat_axis=0, tiled=True)
    return field.reshape(comp_total, point_count)


def shards(
    spectra_in,
    coarse_spectra,
    wind_speed,
    wind_heading,
    sea_mask,
    neighbours,
    edge_x,
    edge_y,
    bound_points,
    bound_cells,
    bound_weights,
):
    device_count = lax.axis_size("pts")
    device_place = lax.axis_index("pts")
    point_count = spectra_in.shape[1]
    comp_total = spectra_in.shape[0]
    local_count = comp_total // device_count
    active = sea_mask.astype(jnp.float32)
    blocks = neighbours.shape[1] // LANES
    if (
        local_count == 2 * NDIR
        and point_count == LANES
        and 4 * bound_points.shape[0] == LANES
        and coarse_spectra.shape[2] == LANES
        and blocks == device_count
        and blocks == 16
        and neighbours.shape[0] * blocks <= LANES
    ):
        return whole_frequencies(
            spectra_in,
            coarse_spectra,
            wind_speed,
            wind_heading,
            sea_mask,
            neighbours,
            edge_x,
            edge_y,
            bound_points,
            bound_cells,
            bound_weights,
        )
    all_comp = jnp.arange(comp_total, dtype=jnp.int32)
    my_comp = device_place * local_count + jnp.arange(local_count, dtype=jnp.int32)
    first_point = device_place * point_count
    own_speed = lax.dynamic_slice_in_dim(wind_speed, first_point, point_count)
    own_heading = lax.dynamic_slice_in_dim(wind_heading, first_point, point_count)
    own_active = lax.dynamic_slice_in_dim(active, first_point, point_count)
    coarse_here = lax.all_to_all(coarse_spectra, "pts", split_axis=1, concat_axis=2, tiled=True)
    bound_values = interpolate(coarse_here, bound_cells, bound_weights)
    outflow, inflow = coefficients(my_comp, edge_x, edge_y)
    spectra = spectra_in
    for coarse_step in range(STEPS):
        energy, inverse = statistics(spectra, all_comp)
        spectra = apply_sources(
            spectra, all_comp, energy, inverse, own_speed, own_heading, own_active
        )
        comp_field = to_components(spectra)
        comp_field = advect(
            comp_field,
            outflow,
            inflow,
            neighbours,
            active,
            bound_values,
            bound_points,
            coarse_step * SUB,
        )
        spectra = to_points(comp_field)
    return spectra


def solution(mesh):
    in_specs = (
        P(None, ("groups", "pts")),
        P(None, None, ("groups", "pts")),
        P("groups"),
        P("groups"),
        P(),
        P(),
        P(),
        P(),
        P(),
        P(),
        P(),
    )
    out_specs = P(None, ("groups", "pts"))
    return jax.shard_map(shards, mesh=mesh, in_specs=in_specs, out_specs=out_specs, check_vma=False)
```

```python
import functools
import math

import jax
import jax.numpy as jnp
import numpy as np
from jax import lax
from jax.experimental import pallas as pl
from jax.experimental.pallas import tpu as pltpu
from jax.sharding import PartitionSpec as P

NDIR = 36
NFREQ = 32
SUB = 4
STEPS = 2
LANES = 128


epsilon = 1e-06
courant = 0.1


def freq_tables(components):
    freq_index = (components // NDIR).astype(jnp.float32)
    dir_index = (components % NDIR).astype(jnp.float32)
    growth = jnp.log(jnp.asarray(1.1, jnp.float32))
    radian_freq = 0.25 * jnp.exp(freq_index * growth)
    freq_top = 0.25 * jnp.exp((NFREQ - 1) * growth)
    freq_total = NDIR * jnp.sum(0.25 * jnp.exp(jnp.arange(NFREQ).astype(jnp.float32) * growth))
    weight = radian_freq / freq_total
    dir_angle = dir_index * (2.0 * jnp.pi / NDIR)
    return (radian_freq, weight, dir_angle, freq_top)


def statistics(spectra, components):
    radian_freq, weight, dir_angle, freq_top = freq_tables(components)
    energy = jnp.sum(weight[:, None] * spectra, axis=0)
    inverse = jnp.sum((weight / radian_freq)[:, None] * spectra, axis=0)
    return (energy, inverse)


def apply_sources(spectra, components, energy, inverse, wind_speed, wind_heading, active):
    radian_freq, weight, dir_angle, freq_top = freq_tables(components)
    mean_freq = energy / (inverse + epsilon)
    mean_period = inverse / (energy + epsilon)
    steepness = energy * (0.5 * mean_freq) ** 2
    steep_ratio = steepness / (1.0 + steepness)
    relative = radian_freq / freq_top
    wind_in = (
        0.6
        * relative[:, None]
        * jax.nn.sigmoid(
            wind_speed[None, :]
            * jnp.cos(dir_angle[:, None] - wind_heading[None, :])
            * radian_freq[:, None]
            / 8.0
            - 1.0
        )
    )
    dissipation = (relative * relative)[:, None] * (mean_period * freq_top * steep_ratio)[None, :]
    return spectra * jnp.exp(wind_in - dissipation) * active[None, :]


def interpolate(coarse_block, bound_cells, bound_weights):
    norm_weights = bound_weights / jnp.sum(bound_weights, axis=0, keepdims=True)
    corners = coarse_block[:, :, bound_cells]
    return jnp.sum(norm_weights[None, None] * corners, axis=2)


def coefficients(components, edge_x, edge_y):
    radian_freq, weight, dir_angle, freq_top = freq_tables(components)
    group_speed = courant * 0.25 / radian_freq
    edge_coef = group_speed[None, :, None] * (
        jnp.cos(dir_angle)[None, :, None] * edge_x[:, None, :]
        + jnp.sin(dir_angle)[None, :, None] * edge_y[:, None, :]
    )
    return (jnp.sum(jnp.maximum(edge_coef, 0.0), axis=0), jnp.minimum(edge_coef, 0.0))


def advect(spectra, outflow, inflow, neighbours, active, bound_values, bound_points, start):
    edge_count = neighbours.shape[0]
    for sub_step in range(SUB):
        upwind = inflow[0] * spectra[:, neighbours[0]]
        for edge in range(1, edge_count):
            upwind = upwind + inflow[edge] * spectra[:, neighbours[edge]]
        spectra = (spectra - outflow * spectra - upwind) * active[None, :]
        time_frac = (start + sub_step + 1) / (STEPS * SUB)
        edge_values = (1.0 - time_frac) * bound_values[0] + time_frac * bound_values[1]
        spectra = spectra.at[:, bound_points].set(edge_values)
    return spectra


def to_components(spectra):
    return lax.all_to_all(spectra, "pts", split_axis=0, concat_axis=1, tiled=True)


def to_points(spectra):
    return lax.all_to_all(spectra, "pts", split_axis=1, concat_axis=0, tiled=True)


GROUPS = 9
GROUP_ROWS = 8
BASE_GROUP = (0, 1, 2, 3, 0, 1, 2, 3, 4)
LISTED = 768
CHUNK = 256


def group_rows(group):
    return pl.ds(GROUP_ROWS * group, GROUP_ROWS)


def load_natural(ref, block):
    lower = [ref[block, group_rows(group), :] for group in range(4)]
    upper = [ref[block, pl.ds(NDIR + GROUP_ROWS * group, GROUP_ROWS), :] for group in range(4)]
    sub = lax.broadcasted_iota(jnp.int32, (GROUP_ROWS, LANES), 0)
    last = jnp.where(sub < 4, ref[block, pl.ds(32, 8), :], ref[block, pl.ds(64, 8), :])
    return lower + upper + [last]


def store_natural(ref, block, values):
    for group in range(4):
        ref[block, group_rows(group), :] = values[group]
    for group in range(4):
        ref[block, pl.ds(NDIR + GROUP_ROWS * group, GROUP_ROWS), :] = values[4 + group]
    ref[block, pl.ds(32, 4), :] = values[8][0:4]
    ref[block, pl.ds(68, 4), :] = values[8][4:8]


def frequency(place):
    return 0.25 * 1.1**place


FREQ_TOP = frequency(NFREQ - 1)
FREQ_TOTAL = NDIR * sum(frequency(place) for place in range(NFREQ))


def setup_kernel(
    place_ref,
    bound_ref,
    speed_ref,
    heading_ref,
    mask_ref,
    near_in,
    x_in,
    y_in,
    keep_ref,
    growth_ref,
    rows_ref,
    dirs_ref,
    points_ref,
    select_ref,
    near_ref,
    x_ref,
    y_ref,
):
    f32 = jnp.float32
    edge_count = near_ref.shape[0]
    blocks = keep_ref.shape[0]
    sub = lax.broadcasted_iota(jnp.int32, (GROUP_ROWS, LANES), 0)
    for group in range(GROUPS):
        rows = group_rows(group)
        upper = jnp.where(sub < 4, 0, 1) if group == 8 else jnp.full((GROUP_ROWS, LANES), group // 4, jnp.int32)
        number = 32 + (sub & 3) if group == 8 else 8 * (group % 4) + sub
        radian_freq = 0.25 * jnp.exp((2 * place_ref[0] + upper).astype(f32) * math.log(1.1))
        relative = radian_freq * (1.0 / FREQ_TOP)
        rows_ref[0, rows, :] = radian_freq
        rows_ref[1, rows, :] = 0.6 * relative
        rows_ref[2, rows, :] = relative * relative * FREQ_TOP
        rows_ref[3, rows, :] = courant * 0.25 / radian_freq
        rows_ref[4, rows, :] = radian_freq * (1.0 / FREQ_TOTAL)
        rows_ref[5, rows, :] = jnp.full((GROUP_ROWS, LANES), 1.0 / FREQ_TOTAL, f32)
        angle = number.astype(f32) * (2.0 * math.pi / NDIR)
        dirs_ref[0, rows, :] = jnp.cos(angle)
        dirs_ref[1, rows, :] = jnp.sin(angle)

    for place in range(blocks):
        lanes = slice(LANES * place, LANES * (place + 1))
        for source, target in ((near_in, near_ref), (x_in, x_ref), (y_in, y_ref)):
            tile = source[:, lanes]
            for edge in range(edge_count):
                target[edge, place : place + 1, :] = tile[edge : edge + 1]

    count = bound_ref.shape[0]
    order = lax.broadcasted_iota(jnp.int32, (count, LANES), 0)
    lane = lax.broadcasted_iota(jnp.int32, (count, LANES), 1)
    spots = jnp.zeros((count, LANES), jnp.int32)
    for number in range(count):
        spots = jnp.where(order == number, bound_ref[number], spots)
    rest = jnp.zeros((LANES - count, LANES), f32)

    def block(place, _):
        hit = jnp.where(spots == lane + LANES * place, 1.0, 0.0)
        select_ref[place] = jnp.concatenate([hit, rest], axis=0).astype(jnp.bfloat16)
        fixed = jnp.max(hit, axis=0, keepdims=True) > 0.0
        sea = mask_ref[pl.ds(place, 1), :].astype(f32)
        open_row = jnp.where(fixed, 0.0, sea)
        points_ref[0, pl.ds(place, 1), :] = sea
        points_ref[1, pl.ds(place, 1), :] = open_row
        points_ref[2, pl.ds(place, 1), :] = jnp.where(fixed, 1.0, sea)
        active = jnp.broadcast_to(sea, (GROUP_ROWS, LANES))
        free = jnp.broadcast_to(open_row, (GROUP_ROWS, LANES))
        speed = spread_row(speed_ref, place) * 0.125
        heading = spread_row(heading_ref, place)
        along, across = speed * jnp.cos(heading), speed * jnp.sin(heading)
        total = []
        for group in (0, 1, 2, 3, 8):
            cosine, sine = dirs_ref[0, group_rows(group), :], dirs_ref[1, group_rows(group), :]
            out = jnp.zeros((GROUP_ROWS, LANES), f32)
            for edge in range(edge_count):
                flow = cosine * spread_row(x_ref, edge, place) + sine * spread_row(y_ref, edge, place)
                out = out + jnp.maximum(flow, 0.0)
            total.append(out)
        for group in range(GROUPS):
            rows = group_rows(group)
            cosine, sine = dirs_ref[0, rows, :], dirs_ref[1, rows, :]
            wind = (along * cosine + across * sine) * rows_ref[0, rows, :] - 1.0
            growth_ref[place, rows, :] = jnp.exp(rows_ref[1, rows, :] * jax.nn.sigmoid(wind)) * active
            keep_ref[place, rows, :] = (1.0 - rows_ref[3, rows, :] * total[BASE_GROUP[group]]) * free
        return 0

    lax.fori_loop(0, blocks, block, 0)


def spread_row(ref, *place):
    row = ref[place[:-1] + (pl.ds(place[-1], 1), slice(None))]
    return jnp.broadcast_to(row, (GROUP_ROWS, LANES))


def split_three(values):
    high = values.astype(jnp.bfloat16).astype(jnp.float32)
    rest = values - high
    middle = rest.astype(jnp.bfloat16).astype(jnp.float32)
    return high, middle, rest - middle


def plan_kernel(
    near_ref,
    x_ref,
    y_ref,
    points_ref,
    dirs_ref,
    first_ref,
    normal_ref,
    gather,
    scatter,
    listed_ref,
    fits_ref,
    marks,
    places,
    values,
    picked,
    homes,
):
    f32, bf16 = jnp.float32, jnp.bfloat16
    edge_count, blocks, _ = near_ref.shape
    for edge in range(edge_count):
        for part in range(blocks // GROUP_ROWS):
            rows = pl.ds(GROUP_ROWS * part, GROUP_ROWS)
            near = near_ref[edge, rows, :]
            lanes, home = near & (LANES - 1), near >> 7
            alive = jnp.zeros((GROUP_ROWS, LANES), f32)
            for source in range(blocks):
                alive = jnp.where(home == source, take_lanes(spread_row(points_ref, 2, source), lanes), alive)
            homes[edge, rows, :] = jnp.where(alive * points_ref[1, rows, :] > 0.0, home, -1)
    high = [homes[edge] for edge in range(edge_count)]

    def block(place, _):
        wanted = lax.broadcasted_iota(jnp.int32, (blocks, LANES), 0)
        lanes = jnp.zeros((blocks, LANES), jnp.int32)
        x = jnp.zeros((blocks, LANES), f32)
        y = jnp.zeros((blocks, LANES), f32)
        for edge in reversed(range(edge_count)):
            near = jnp.broadcast_to(near_ref[edge, pl.ds(place, 1), :], (blocks, LANES))
            hit = jnp.broadcast_to(homes[edge, pl.ds(place, 1), :], (blocks, LANES)) == wanted
            lanes = jnp.where(hit, near & (LANES - 1), lanes)
            x = jnp.where(hit, jnp.broadcast_to(x_ref[edge, pl.ds(place, 1), :], (blocks, LANES)), x)
            y = jnp.where(hit, jnp.broadcast_to(y_ref[edge, pl.ds(place, 1), :], (blocks, LANES)), y)
        first_ref[place] = lanes
        normal_ref[0, place] = x
        normal_ref[1, place] = y
        return 0

    lax.fori_loop(0, blocks, block, 0)

    marks[...] = jnp.zeros_like(marks)
    for edge in range(edge_count):
        again = jnp.zeros((blocks, LANES), f32)
        for before in range(edge):
            again = jnp.where(high[before] == high[edge], 1.0, again)
        marks[pl.ds(blocks * edge, blocks), :] = jnp.where(high[edge] >= 0, again, 0.0)
        x_parts, y_parts = split_three(x_ref[edge]), split_three(y_ref[edge])
        rows = ((near_ref[edge] & (LANES - 1)).astype(f32), (near_ref[edge] >> 7).astype(f32)) + x_parts + y_parts
        for place in range(blocks):
            side, column = divmod(place, blocks // 2)
            for number, row in enumerate(rows):
                values[side, pl.ds(8 * edge + number, 1), pl.ds(LANES * column, LANES)] = row[place : place + 1]
    left = lax.broadcasted_iota(jnp.int32, (LANES, LANES), 0)
    right = lax.broadcasted_iota(jnp.int32, (LANES, LANES), 1)
    mark = marks[...].astype(bf16)
    within = jnp.dot(mark, jnp.where(left < right, 1.0, 0.0).astype(bf16), preferred_element_type=f32)
    count = jnp.dot(mark, jnp.ones((LANES, LANES), bf16), preferred_element_type=f32)
    earlier = (right < left) & ((left & (blocks // 2)) == (right & (blocks // 2)))
    offset = jnp.dot(jnp.where(earlier, 1.0, 0.0).astype(bf16), count.astype(bf16), preferred_element_type=f32)
    position = jnp.where(marks[...] > 0.0, within + offset, -1.0)
    places[0] = position
    places[1] = offset
    fits_ref[0] = (jnp.max(position) < LISTED).astype(jnp.int32)

    rank = lax.broadcasted_iota(jnp.int32, (16, LANES), 0).astype(f32)

    def scatter_block(place, _):
        rows = [
            jnp.broadcast_to(places[0, pl.ds(blocks * edge + place, 1), :], (16, LANES)) for edge in range(edge_count)
        ]
        for tile in range(LISTED // 16):
            here = rank + float(16 * tile)
            hit = rows[0] == here
            for row in rows[1:]:
                hit = hit | (row == here)
            value = jnp.where(hit, 1.0, 0.0).astype(bf16)
            scatter[place // 2, pl.ds(16 * tile, 16), pl.ds(pl.multiple_of((place % 2) * LANES, LANES), LANES)] = value
        return 0

    lax.fori_loop(0, blocks, scatter_block, 0)

    chunks = blocks * LANES // (2 * CHUNK)
    for side in range(2):
        wide = None
        for column in range(chunks):
            term = lax.dot_general(
                values[side, :, pl.ds(CHUNK * column, CHUNK)].astype(bf16),
                scatter[chunks * side + column],
                (((1,), (1,)), ((), ())),
                preferred_element_type=f32,
            )
            wide = term if wide is None else wide + term
        for column in range(LISTED // LANES):
            here = lax.broadcasted_iota(jnp.int32, (8, LANES), 1).astype(f32) + float(LANES * column)
            chosen = wide[0:8, LANES * column : LANES * (column + 1)]
            for edge in range(1, edge_count):
                begin = spread_row(places, 1, blocks * edge + (blocks // 2) * side)
                chosen = jnp.where(
                    here >= begin, wide[8 * edge : 8 * edge + 8, LANES * column : LANES * (column + 1)], chosen
                )
            spot = (LISTED // LANES) * side + column
            x_row = jnp.broadcast_to(chosen[2:3] + chosen[3:4] + chosen[4:5], (GROUP_ROWS, LANES))
            y_row = jnp.broadcast_to(chosen[5:6] + chosen[6:7] + chosen[7:8], (GROUP_ROWS, LANES))
            picked[pl.ds(spot, 1), :] = chosen[0:1] + float(LANES) * chosen[1:2]
            lane = slice(LANES * (column % 2), LANES * (column % 2) + LANES)
            for group, rows in enumerate((0, 1, 2, 3, 8)):
                flow = dirs_ref[0, group_rows(rows), :] * x_row + dirs_ref[1, group_rows(rows), :] * y_row
                listed_ref[spot // 2, group_rows(group), lane] = jnp.minimum(flow, 0.0)

    def gather_block(spot, _):
        source = jnp.broadcast_to(picked[pl.ds(spot, 1), :], (16, LANES))
        for tile in range(gather.shape[1] // 16):
            value = jnp.where(rank + float(16 * tile) == source, 1.0, 0.0).astype(bf16)
            gather[spot // 2, pl.ds(16 * tile, 16), pl.ds(pl.multiple_of((spot % 2) * LANES, LANES), LANES)] = value
        return 0

    lax.fori_loop(0, 2 * LISTED // LANES, gather_block, 0)


def dissipation_rate(energy, inverse):
    mean_freq = energy / (inverse + epsilon)
    steepness = energy * (0.5 * mean_freq) * (0.5 * mean_freq)
    return inverse / (energy + epsilon) * (steepness / (1.0 + steepness))


def split_bf16(values):
    high = values.astype(jnp.bfloat16).astype(jnp.float32)
    return high, values - high


def pack_kernel(first_ref, spectra_ref, coarse_ref, cells_ref, weights_ref, send_ref, shares):
    destinations = send_ref.shape[0]
    f32 = jnp.float32
    lane = lax.broadcasted_iota(jnp.int32, (LANES, LANES), 1)
    cell = lax.broadcasted_iota(jnp.int32, (LANES, LANES), 0) + first_ref[0]
    weights = jnp.concatenate([weights_ref[...]] * 4, axis=1)
    norm = weights / jnp.sum(weights, axis=0, keepdims=True)
    cells = jnp.concatenate([cells_ref[...]] * 4, axis=1)
    table = jnp.zeros((LANES, LANES), f32)
    for corner in range(cells_ref.shape[0]):
        hit = jnp.broadcast_to(cells[corner : corner + 1], (LANES, LANES)) == cell
        table = table + jnp.where(hit, jnp.broadcast_to(norm[corner : corner + 1], (LANES, LANES)), 0.0)
    later = (lane & 32) != 0
    bf16 = jnp.bfloat16
    parts = [split_bf16(jnp.where(later, 0.0, table)), split_bf16(jnp.where(later, table, 0.0))]
    parts = [(high.astype(bf16), low.astype(bf16)) for high, low in parts]
    chunk = 8 * NDIR

    for start in range(0, spectra_ref.shape[0], chunk):
        result = None
        for time in range(2):
            high, low = split_bf16(coarse_ref[time, pl.ds(start, chunk), :])
            high, low = high.astype(bf16), low.astype(bf16)
            weight_high, weight_low = parts[time]
            for left, right in ((high, weight_high), (low, weight_high), (high, weight_low)):
                term = jnp.dot(left, right, preferred_element_type=f32)
                result = term if result is None else result + term
        shares[pl.ds(start, chunk), :] = result

    sub = lax.broadcasted_iota(jnp.int32, (GROUP_ROWS, LANES), 0) < 4
    energy = jnp.zeros((GROUP_ROWS, LANES), f32)
    inverse = jnp.zeros((GROUP_ROWS, LANES), f32)
    lower_lanes = lax.broadcasted_iota(jnp.int32, (NDIR, LANES), 1) < 64
    for place in range(destinations):
        start = 2 * NDIR * place
        values = [spectra_ref[pl.ds(start + GROUP_ROWS * group, GROUP_ROWS), :] for group in range(GROUPS)]
        for group in range(GROUPS):
            send_ref[place, group_rows(group), :] = values[group]
        lower = values[0] + values[1] + values[2] + values[3] + jnp.where(sub, values[4], 0.0)
        upper = values[5] + values[6] + values[7] + values[8] + jnp.where(sub, 0.0, values[4])
        energy = energy + frequency(2 * place) * lower + frequency(2 * place + 1) * upper
        inverse = inverse + (lower + upper)
        send_ref[place, pl.ds(2 * NDIR, NDIR), :] = jnp.where(
            lower_lanes, shares[pl.ds(start, NDIR), :], shares[pl.ds(start + NDIR, NDIR), :]
        )
    energy = jnp.sum(energy, axis=0, keepdims=True) * (1.0 / FREQ_TOTAL)
    inverse = jnp.sum(inverse, axis=0, keepdims=True) * (1.0 / FREQ_TOTAL)
    rate = jnp.broadcast_to(dissipation_rate(energy, inverse), (4, LANES))
    for place in range(destinations):
        send_ref[place, pl.ds(3 * NDIR, 4), :] = rate


def take_lanes(values, lanes):
    return jnp.take_along_axis(values, lanes, axis=1, mode="promise_in_bounds")


def fine_kernel(
    first,
    fits_ref,
    state_ref,
    extra_ref,
    near_ref,
    x_ref,
    y_ref,
    points_ref,
    dirs_ref,
    keep_ref,
    growth_ref,
    rows_ref,
    listed_ref,
    first_ref,
    normal_ref,
    gather_ref,
    scatter_ref,
    *rest,
):
    if first:
        out_ref, sums_ref, start_ref, slope_ref = rest[:4]
    else:
        start_ref, slope_ref, out_ref = rest[:3]
    scratch = rest[4:] if first else rest[3:]
    field, words, speed, base_ref, pairs, ends, inflow_ref, terms, moments = scratch
    f32, bf16 = jnp.float32, jnp.bfloat16
    blocks = keep_ref.shape[0]
    half = blocks // 2
    edge_count = near_ref.shape[0]
    first_step = 0 if first else SUB
    if first:
        total = state_ref[0, pl.ds(2 * NDIR, 40), :]
        for source in range(1, blocks):
            total = total + state_ref[source, pl.ds(2 * NDIR, 40), :]
        rolled = [total] + [pltpu.roll(total, LANES - 32 * piece, 1) for piece in range(1, 4)]
        high, low = split_bf16(jnp.concatenate(rolled, axis=0))
        bound = jnp.concatenate([high, low], axis=0).astype(jnp.bfloat16)

    else:
        total = extra_ref[0]
        for source in range(1, blocks):
            total = total + extra_ref[source]
        moments[...] = total

    def spread(place):
        values = jnp.dot(bound, extra_ref[place], preferred_element_type=jnp.float32)
        values = values[0:160] + values[160:320]
        pieces = [values[40 * piece : 40 * piece + 40] for piece in range(4)]
        for out, pair in (
            (start_ref, (pieces[0], pieces[2])),
            (slope_ref, (pieces[1] - pieces[0], pieces[3] - pieces[2])),
        ):
            for side in range(2):
                for group in range(4):
                    out[place, group_rows(4 * side + group), :] = pair[side][8 * group : 8 * group + 8]
            out[place, pl.ds(64, 4), :] = pair[0][32:36]
            out[place, pl.ds(68, 4), :] = pair[1][32:36]

    def enter(place, _):
        if first:
            loss = jnp.broadcast_to(state_ref[place, pl.ds(3 * NDIR, 1), :], (GROUP_ROWS, LANES))
            values = load_natural(state_ref, place)
            spread(place)
        else:
            loss = dissipation_rate(spread_row(moments, place), spread_row(moments, blocks + place))
            values = [state_ref[place, group_rows(group), :] for group in range(GROUPS)]
        lower, upper, last = [jnp.exp(-rows_ref[2, group_rows(group), :] * loss) for group in (0, 4, 8)]
        decay = [lower] * 4 + [upper] * 4 + [last]
        for group in range(GROUPS):
            rows = group_rows(group)
            field[0, place, rows, :] = values[group] * growth_ref[place, rows, :] * decay[group]
        for source in range(blocks):
            x, y = spread_row(normal_ref, 0, place, source), spread_row(normal_ref, 1, place, source)
            for group, number in enumerate((0, 1, 2, 3, 8)):
                flow = dirs_ref[0, group_rows(number), :] * x + dirs_ref[1, group_rows(number), :] * y
                base_ref[place, source, group_rows(group), :] = jnp.minimum(flow, 0.0)
        return 0

    lax.fori_loop(0, blocks, enter, 0)

    def boundary(place, rows, number):
        time_frac = jnp.asarray(number + (first_step + 1), jnp.int32).astype(f32) * (1.0 / (STEPS * SUB))
        return start_ref[place, rows, :] + time_frac * slope_ref[place, rows, :]

    def encode(group, top_code):
        rows = group_rows(group)
        values = [field[0, place, rows, :] for place in range(blocks)]
        top = functools.reduce(jnp.maximum, values)
        top = jnp.maximum(jnp.max(top, axis=1, keepdims=True), 1e-30)
        scale = jnp.broadcast_to(top_code / top, (GROUP_ROWS, LANES))
        speed[rows, :] = rows_ref[3, rows, :] * (top * (1.0 / top_code))
        return [(value * scale + 0.5).astype(jnp.int32) for value in values]

    def collect(side):
        for chunk in range(LISTED // CHUNK * side, LISTED // CHUNK * (side + 1)):
            found = jnp.dot(words[...], gather_ref[chunk], preferred_element_type=f32)
            for group in range(GROUPS):
                value = found[16 * group : 16 * group + 8] + found[16 * group + 8 : 16 * group + 16]
                high, low = split_bf16(value * listed_ref[chunk, group_rows(BASE_GROUP[group]), :])
                terms[chunk, pl.ds(16 * group, 16), :] = jnp.concatenate([high, low], axis=0).astype(bf16)
        for place in range(half * side, half * (side + 1)):
            inflow = [jnp.zeros((GROUP_ROWS, LANES), f32)] * GROUPS
            for source in range(blocks):
                lanes = spread_row(first_ref, place, source)
                for group in range(4):
                    base = base_ref[place, source, group_rows(group), :]
                    word = take_lanes(pairs[source, group_rows(group), :], lanes)
                    lower = (word & 65535).astype(f32)
                    upper = lax.shift_right_logical(word, 16).astype(f32)
                    inflow[group] = inflow[group] + base * lower
                    inflow[group + 4] = inflow[group + 4] + base * upper
                inflow[8] = inflow[8] + base_ref[place, source, group_rows(4), :] * take_lanes(ends[source], lanes)
            for group in range(GROUPS):
                factor = speed[group_rows(group), :] if group < 8 else rows_ref[3, group_rows(8), :]
                inflow_ref[place, group_rows(group), :] = factor * inflow[group]

    def update(side, number):
        parts = LISTED // CHUNK
        for chunk in range(half // 2 * side, half // 2 * (side + 1)):
            moved = None
            for part in range(parts):
                term = jnp.dot(
                    terms[parts * side + part],
                    scatter_ref[chunk, pl.ds(CHUNK * part, CHUNK), :],
                    preferred_element_type=f32,
                )
                moved = term if moved is None else moved + term
            for column in range(2):
                place = 2 * chunk + column
                lanes = slice(LANES * column, LANES * (column + 1))
                for group in range(GROUPS):
                    rows = group_rows(group)
                    more = moved[16 * group : 16 * group + 8, lanes] + moved[16 * group + 8 : 16 * group + 16, lanes]
                    field[0, place, rows, :] = (
                        field[0, place, rows, :] * keep_ref[place, rows, :]
                        - inflow_ref[place, rows, :]
                        - rows_ref[3, rows, :] * more
                        + boundary(place, rows, number)
                    )

    def fine_step(number, _):
        for group in range(4):
            lower, upper = encode(group, 65535.0), encode(group + 4, 65535.0)
            for place in range(blocks):
                pairs[place, group_rows(group), :] = (upper[place] << 16) | lower[place]
        for place in range(blocks):
            ends[place] = field[0, place, group_rows(8), :]
            for group in range(GROUPS):
                high, low = split_bf16(field[0, place, group_rows(group), :])
                both = jnp.concatenate([high, low], axis=0).astype(bf16)
                words[pl.ds(16 * group, 16), pl.ds(LANES * place, LANES)] = both

        collect(0)
        update(0, number)
        collect(1)
        update(1, number)
        return 0

    def plain_step(number, _):
        def block(place, _):
            free = spread_row(points_ref, 1, place)
            inflow = [jnp.zeros((GROUP_ROWS, LANES), f32)] * GROUPS
            for edge in range(edge_count):
                near = spread_row(near_ref, edge, place)
                lanes, home = near & (LANES - 1), near >> 7
                x, y = spread_row(x_ref, edge, place), spread_row(y_ref, edge, place)
                for group in range(GROUPS):
                    rows = group_rows(group)
                    value = jnp.zeros((GROUP_ROWS, LANES), f32)
                    for source in range(blocks):
                        value = jnp.where(home == source, take_lanes(field[0, source, rows, :], lanes), value)
                    flow = dirs_ref[0, rows, :] * x + dirs_ref[1, rows, :] * y
                    inflow[group] = inflow[group] + jnp.minimum(flow, 0.0) * free * value
            for group in range(GROUPS):
                rows = group_rows(group)
                field[1, place, rows, :] = (
                    field[0, place, rows, :] * keep_ref[place, rows, :]
                    - rows_ref[3, rows, :] * inflow[group]
                    + boundary(place, rows, number)
                )
            return 0

        lax.fori_loop(0, blocks, block, 0)
        field[0] = field[1]
        return 0

    fits = fits_ref[0]

    @pl.when(fits != 0)
    def _():
        lax.fori_loop(0, SUB, fine_step, 0)

    @pl.when(fits == 0)
    def _():
        lax.fori_loop(0, SUB, plain_step, 0)

    def leave(place, _):
        values = [field[0, place, group_rows(group), :] for group in range(GROUPS)]
        if first:
            energy, inverse = None, None
            for group in range(GROUPS):
                rows = group_rows(group)
                out_ref[place, rows, :] = values[group]
                part = rows_ref[4, rows, :] * values[group]
                energy = part if energy is None else energy + part
                part = rows_ref[5, rows, :] * values[group]
                inverse = part if inverse is None else inverse + part
            moments[pl.ds(place, 1), :] = jnp.sum(energy, axis=0, keepdims=True)
            moments[pl.ds(blocks + place, 1), :] = jnp.sum(inverse, axis=0, keepdims=True)
        else:
            store_natural(out_ref, place, values)
        return 0

    lax.fori_loop(0, blocks, leave, 0)
    if first:
        for target in range(sums_ref.shape[0]):
            sums_ref[target] = moments[...]


def in_vmem(count):
    return [pl.BlockSpec(memory_space=pltpu.VMEM)] * count


def params(mebibytes=16):
    return pltpu.CompilerParams(vmem_limit_bytes=mebibytes << 20)


def whole_frequencies(
    spectra_in,
    coarse_spectra,
    wind_speed,
    wind_heading,
    sea_mask,
    neighbours,
    edge_x,
    edge_y,
    bound_points,
    bound_cells,
    bound_weights,
):
    device_count = lax.axis_size("pts")
    device_place = lax.axis_index("pts")
    comp_total, point_count = spectra_in.shape
    local_count = comp_total // device_count
    edge_count, grid_points = neighbours.shape
    blocks = grid_points // LANES
    bound_count = bound_points.shape[0]
    f32 = jnp.float32
    first_point = (device_place * point_count).astype(jnp.int32).reshape(1)
    send = pl.pallas_call(
        pack_kernel,
        out_shape=jax.ShapeDtypeStruct((device_count, 112, LANES), f32),
        in_specs=[pl.BlockSpec(memory_space=pltpu.SMEM)] + in_vmem(4),
        out_specs=pl.BlockSpec(memory_space=pltpu.VMEM),
        scratch_shapes=[pltpu.VMEM((comp_total, LANES), f32)],
        compiler_params=params(),
    )(first_point, spectra_in, coarse_spectra, bound_cells, bound_weights)
    received = lax.all_to_all(send, "pts", split_axis=0, concat_axis=0, tiled=True)

    by_block = (blocks, LANES)
    state_shape = jax.ShapeDtypeStruct((blocks, local_count, LANES), f32)
    edge_shape = (edge_count, blocks, LANES)
    keep, growth, rows, dirs, points, select, near, edge_x, edge_y = pl.pallas_call(
        setup_kernel,
        out_shape=[
            state_shape,
            state_shape,
            jax.ShapeDtypeStruct((6, local_count, LANES), f32),
            jax.ShapeDtypeStruct((2, local_count, LANES), f32),
            jax.ShapeDtypeStruct((3,) + by_block, f32),
            jax.ShapeDtypeStruct((blocks, LANES, LANES), jnp.bfloat16),
            jax.ShapeDtypeStruct(edge_shape, jnp.int32),
            jax.ShapeDtypeStruct(edge_shape, f32),
            jax.ShapeDtypeStruct(edge_shape, f32),
        ],
        in_specs=[pl.BlockSpec(memory_space=pltpu.SMEM)] * 2 + in_vmem(6),
        out_specs=in_vmem(9),
        compiler_params=params(),
        cost_estimate=pl.CostEstimate(flops=100_000_000, bytes_accessed=4_000_000, transcendentals=1_000_000),
    )(
        device_place.astype(jnp.int32).reshape(1),
        bound_points,
        wind_speed.reshape(by_block),
        wind_heading.reshape(by_block),
        sea_mask.reshape(by_block),
        neighbours,
        edge_x,
        edge_y,
    )

    shapes = [
        ((2 * LISTED // CHUNK, grid_points, CHUNK), jnp.bfloat16),
        ((grid_points // CHUNK, LISTED, CHUNK), jnp.bfloat16),
    ]
    first_edge, normals, gather, scatter, listed, fits = pl.pallas_call(
        plan_kernel,
        out_shape=[
            jax.ShapeDtypeStruct((blocks,) + by_block, jnp.int32),
            jax.ShapeDtypeStruct((2, blocks) + by_block, f32),
        ]
        + [jax.ShapeDtypeStruct(shape, dtype) for shape, dtype in shapes]
        + [jax.ShapeDtypeStruct((2 * LISTED // CHUNK, 40, CHUNK), f32), jax.ShapeDtypeStruct((1,), jnp.int32)],
        in_specs=in_vmem(5),
        out_specs=in_vmem(5) + [pl.BlockSpec(memory_space=pltpu.SMEM)],
        scratch_shapes=[
            pltpu.VMEM((LANES, LANES), f32),
            pltpu.VMEM((2, LANES, LANES), f32),
            pltpu.VMEM((2, 8 * edge_count, grid_points // 2), f32),
            pltpu.VMEM((2 * LISTED // LANES, LANES), f32),
            pltpu.VMEM(edge_shape, jnp.int32),
        ],
        compiler_params=params(20),
        cost_estimate=pl.CostEstimate(flops=1_000_000_000, bytes_accessed=20_000_000, transcendentals=0),
    )(near, edge_x, edge_y, points, dirs)

    def fine(is_first, state, extra, bound):
        out_shape = [state_shape]
        if is_first:
            out_shape += [jax.ShapeDtypeStruct((device_count, 2 * blocks, LANES), f32), state_shape, state_shape]
        return pl.pallas_call(
            functools.partial(fine_kernel, is_first),
            out_shape=out_shape,
            in_specs=[pl.BlockSpec(memory_space=pltpu.SMEM)]
            + in_vmem(15 + len(bound)),
            out_specs=in_vmem(len(out_shape)),
            scratch_shapes=[
                pltpu.VMEM((2, blocks, local_count, LANES), f32),
                pltpu.VMEM((2 * local_count, grid_points), jnp.bfloat16),
                pltpu.VMEM((local_count, LANES), f32),
            ]
            + [
                pltpu.VMEM((blocks, blocks, 40, LANES), f32),
                pltpu.VMEM((blocks, 32, LANES), jnp.int32),
                pltpu.VMEM((blocks, GROUP_ROWS, LANES), f32),
                pltpu.VMEM((blocks, local_count, LANES), f32),
                pltpu.VMEM((2 * LISTED // CHUNK, 2 * local_count, CHUNK), jnp.bfloat16),
                pltpu.VMEM((2 * blocks, LANES), f32),
            ],
            compiler_params=params(28),
        )(
            fits,
            state,
            extra,
            near,
            edge_x,
            edge_y,
            points,
            dirs,
            keep,
            growth,
            rows,
            listed,
            first_edge,
            normals,
            gather,
            scatter,
            *bound,
        )

    field, sums, start, slope = fine(True, received, select, ())
    sums = lax.all_to_all(sums, "pts", split_axis=0, concat_axis=0, tiled=True)
    (field,) = fine(False, field, sums, (start, slope))
    field = lax.all_to_all(field, "pts", split_axis=0, concat_axis=0, tiled=True)
    return field.reshape(comp_total, point_count)


def shards(
    spectra_in,
    coarse_spectra,
    wind_speed,
    wind_heading,
    sea_mask,
    neighbours,
    edge_x,
    edge_y,
    bound_points,
    bound_cells,
    bound_weights,
):
    device_count = lax.axis_size("pts")
    device_place = lax.axis_index("pts")
    point_count = spectra_in.shape[1]
    comp_total = spectra_in.shape[0]
    local_count = comp_total // device_count
    active = sea_mask.astype(jnp.float32)
    blocks = neighbours.shape[1] // LANES
    if (
        local_count == 2 * NDIR
        and point_count == LANES
        and 4 * bound_points.shape[0] == LANES
        and coarse_spectra.shape[2] == LANES
        and blocks == device_count
        and blocks == 16
        and neighbours.shape[0] * blocks <= LANES
    ):
        return whole_frequencies(
            spectra_in,
            coarse_spectra,
            wind_speed,
            wind_heading,
            sea_mask,
            neighbours,
            edge_x,
            edge_y,
            bound_points,
            bound_cells,
            bound_weights,
        )
    all_comp = jnp.arange(comp_total, dtype=jnp.int32)
    my_comp = device_place * local_count + jnp.arange(local_count, dtype=jnp.int32)
    first_point = device_place * point_count
    own_speed = lax.dynamic_slice_in_dim(wind_speed, first_point, point_count)
    own_heading = lax.dynamic_slice_in_dim(wind_heading, first_point, point_count)
    own_active = lax.dynamic_slice_in_dim(active, first_point, point_count)
    coarse_here = lax.all_to_all(coarse_spectra, "pts", split_axis=1, concat_axis=2, tiled=True)
    bound_values = interpolate(coarse_here, bound_cells, bound_weights)
    outflow, inflow = coefficients(my_comp, edge_x, edge_y)
    spectra = spectra_in
    for coarse_step in range(STEPS):
        energy, inverse = statistics(spectra, all_comp)
        spectra = apply_sources(
            spectra, all_comp, energy, inverse, own_speed, own_heading, own_active
        )
        comp_field = to_components(spectra)
        comp_field = advect(
            comp_field,
            outflow,
            inflow,
            neighbours,
            active,
            bound_values,
            bound_points,
            coarse_step * SUB,
        )
        spectra = to_points(comp_field)
    return spectra


def solution(mesh):
    in_specs = (
        P(None, ("groups", "pts")),
        P(None, None, ("groups", "pts")),
        P("groups"),
        P("groups"),
        P(),
        P(),
        P(),
        P(),
        P(),
        P(),
        P(),
    )
    out_specs = P(None, ("groups", "pts"))
    return jax.shard_map(shards, mesh=mesh, in_specs=in_specs, out_specs=out_specs, check_vma=False)
```

```python
import functools
import math

import jax
import jax.numpy as jnp
import numpy as np
from jax import lax
from jax.experimental import pallas as pl
from jax.experimental.pallas import tpu as pltpu
from jax.sharding import PartitionSpec as P

NDIR = 36
NFREQ = 32
SUB = 4
STEPS = 2
LANES = 128


epsilon = 1e-06
courant = 0.1


def freq_tables(components):
    freq_index = (components // NDIR).astype(jnp.float32)
    dir_index = (components % NDIR).astype(jnp.float32)
    growth = jnp.log(jnp.asarray(1.1, jnp.float32))
    radian_freq = 0.25 * jnp.exp(freq_index * growth)
    freq_top = 0.25 * jnp.exp((NFREQ - 1) * growth)
    freq_total = NDIR * jnp.sum(0.25 * jnp.exp(jnp.arange(NFREQ).astype(jnp.float32) * growth))
    weight = radian_freq / freq_total
    dir_angle = dir_index * (2.0 * jnp.pi / NDIR)
    return (radian_freq, weight, dir_angle, freq_top)


def statistics(spectra, components):
    radian_freq, weight, dir_angle, freq_top = freq_tables(components)
    energy = jnp.sum(weight[:, None] * spectra, axis=0)
    inverse = jnp.sum((weight / radian_freq)[:, None] * spectra, axis=0)
    return (energy, inverse)


def apply_sources(spectra, components, energy, inverse, wind_speed, wind_heading, active):
    radian_freq, weight, dir_angle, freq_top = freq_tables(components)
    mean_freq = energy / (inverse + epsilon)
    mean_period = inverse / (energy + epsilon)
    steepness = energy * (0.5 * mean_freq) ** 2
    steep_ratio = steepness / (1.0 + steepness)
    relative = radian_freq / freq_top
    wind_in = (
        0.6
        * relative[:, None]
        * jax.nn.sigmoid(
            wind_speed[None, :]
            * jnp.cos(dir_angle[:, None] - wind_heading[None, :])
            * radian_freq[:, None]
            / 8.0
            - 1.0
        )
    )
    dissipation = (relative * relative)[:, None] * (mean_period * freq_top * steep_ratio)[None, :]
    return spectra * jnp.exp(wind_in - dissipation) * active[None, :]


def interpolate(coarse_block, bound_cells, bound_weights):
    norm_weights = bound_weights / jnp.sum(bound_weights, axis=0, keepdims=True)
    corners = coarse_block[:, :, bound_cells]
    return jnp.sum(norm_weights[None, None] * corners, axis=2)


def coefficients(components, edge_x, edge_y):
    radian_freq, weight, dir_angle, freq_top = freq_tables(components)
    group_speed = courant * 0.25 / radian_freq
    edge_coef = group_speed[None, :, None] * (
        jnp.cos(dir_angle)[None, :, None] * edge_x[:, None, :]
        + jnp.sin(dir_angle)[None, :, None] * edge_y[:, None, :]
    )
    return (jnp.sum(jnp.maximum(edge_coef, 0.0), axis=0), jnp.minimum(edge_coef, 0.0))


def advect(spectra, outflow, inflow, neighbours, active, bound_values, bound_points, start):
    edge_count = neighbours.shape[0]
    for sub_step in range(SUB):
        upwind = inflow[0] * spectra[:, neighbours[0]]
        for edge in range(1, edge_count):
            upwind = upwind + inflow[edge] * spectra[:, neighbours[edge]]
        spectra = (spectra - outflow * spectra - upwind) * active[None, :]
        time_frac = (start + sub_step + 1) / (STEPS * SUB)
        edge_values = (1.0 - time_frac) * bound_values[0] + time_frac * bound_values[1]
        spectra = spectra.at[:, bound_points].set(edge_values)
    return spectra


def to_components(spectra):
    return lax.all_to_all(spectra, "pts", split_axis=0, concat_axis=1, tiled=True)


def to_points(spectra):
    return lax.all_to_all(spectra, "pts", split_axis=1, concat_axis=0, tiled=True)


GROUPS = 9
GROUP_ROWS = 8
BASE_GROUP = (0, 1, 2, 3, 0, 1, 2, 3, 4)
LISTED = 768
CHUNK = 256


def group_rows(group):
    return pl.ds(GROUP_ROWS * group, GROUP_ROWS)


def load_natural(ref, block):
    lower = [ref[block, group_rows(group), :] for group in range(4)]
    upper = [ref[block, pl.ds(NDIR + GROUP_ROWS * group, GROUP_ROWS), :] for group in range(4)]
    sub = lax.broadcasted_iota(jnp.int32, (GROUP_ROWS, LANES), 0)
    last = jnp.where(sub < 4, ref[block, pl.ds(32, 8), :], ref[block, pl.ds(64, 8), :])
    return lower + upper + [last]


def store_natural(ref, block, values):
    for group in range(4):
        ref[block, group_rows(group), :] = values[group]
    for group in range(4):
        ref[block, pl.ds(NDIR + GROUP_ROWS * group, GROUP_ROWS), :] = values[4 + group]
    ref[block, pl.ds(32, 4), :] = values[8][0:4]
    ref[block, pl.ds(68, 4), :] = values[8][4:8]


def frequency(place):
    return 0.25 * 1.1**place


FREQ_TOP = frequency(NFREQ - 1)
FREQ_TOTAL = NDIR * sum(frequency(place) for place in range(NFREQ))


def setup_kernel(
    place_ref,
    bound_ref,
    speed_ref,
    heading_ref,
    mask_ref,
    near_in,
    x_in,
    y_in,
    keep_ref,
    growth_ref,
    rows_ref,
    dirs_ref,
    points_ref,
    select_ref,
    near_ref,
    x_ref,
    y_ref,
):
    f32 = jnp.float32
    edge_count = near_ref.shape[0]
    blocks = keep_ref.shape[0]
    sub = lax.broadcasted_iota(jnp.int32, (GROUP_ROWS, LANES), 0)
    for group in range(GROUPS):
        rows = group_rows(group)
        upper = jnp.where(sub < 4, 0, 1) if group == 8 else jnp.full((GROUP_ROWS, LANES), group // 4, jnp.int32)
        number = 32 + (sub & 3) if group == 8 else 8 * (group % 4) + sub
        radian_freq = 0.25 * jnp.exp((2 * place_ref[0] + upper).astype(f32) * math.log(1.1))
        relative = radian_freq * (1.0 / FREQ_TOP)
        rows_ref[0, rows, :] = radian_freq
        rows_ref[1, rows, :] = 0.6 * relative
        rows_ref[2, rows, :] = relative * relative * FREQ_TOP
        rows_ref[3, rows, :] = courant * 0.25 / radian_freq
        rows_ref[4, rows, :] = radian_freq * (1.0 / FREQ_TOTAL)
        rows_ref[5, rows, :] = jnp.full((GROUP_ROWS, LANES), 1.0 / FREQ_TOTAL, f32)
        angle = number.astype(f32) * (2.0 * math.pi / NDIR)
        dirs_ref[0, rows, :] = jnp.cos(angle)
        dirs_ref[1, rows, :] = jnp.sin(angle)

    for place in range(blocks):
        lanes = slice(LANES * place, LANES * (place + 1))
        for source, target in ((near_in, near_ref), (x_in, x_ref), (y_in, y_ref)):
            tile = source[:, lanes]
            for edge in range(edge_count):
                target[edge, place : place + 1, :] = tile[edge : edge + 1]

    count = bound_ref.shape[0]
    order = lax.broadcasted_iota(jnp.int32, (count, LANES), 0)
    lane = lax.broadcasted_iota(jnp.int32, (count, LANES), 1)
    spots = jnp.zeros((count, LANES), jnp.int32)
    for number in range(count):
        spots = jnp.where(order == number, bound_ref[number], spots)
    rest = jnp.zeros((LANES - count, LANES), f32)

    def block(place, _):
        hit = jnp.where(spots == lane + LANES * place, 1.0, 0.0)
        select_ref[place] = jnp.concatenate([hit, rest], axis=0).astype(jnp.bfloat16)
        fixed = jnp.max(hit, axis=0, keepdims=True) > 0.0
        sea = mask_ref[pl.ds(place, 1), :].astype(f32)
        open_row = jnp.where(fixed, 0.0, sea)
        points_ref[0, pl.ds(place, 1), :] = sea
        points_ref[1, pl.ds(place, 1), :] = open_row
        points_ref[2, pl.ds(place, 1), :] = jnp.where(fixed, 1.0, sea)
        active = jnp.broadcast_to(sea, (GROUP_ROWS, LANES))
        free = jnp.broadcast_to(open_row, (GROUP_ROWS, LANES))
        speed = spread_row(speed_ref, place) * 0.125
        heading = spread_row(heading_ref, place)
        along, across = speed * jnp.cos(heading), speed * jnp.sin(heading)
        total = []
        for group in (0, 1, 2, 3, 8):
            cosine, sine = dirs_ref[0, group_rows(group), :], dirs_ref[1, group_rows(group), :]
            out = jnp.zeros((GROUP_ROWS, LANES), f32)
            for edge in range(edge_count):
                flow = cosine * spread_row(x_ref, edge, place) + sine * spread_row(y_ref, edge, place)
                out = out + jnp.maximum(flow, 0.0)
            total.append(out)
        for group in range(GROUPS):
            rows = group_rows(group)
            cosine, sine = dirs_ref[0, rows, :], dirs_ref[1, rows, :]
            wind = (along * cosine + across * sine) * rows_ref[0, rows, :] - 1.0
            growth_ref[place, rows, :] = jnp.exp(rows_ref[1, rows, :] * jax.nn.sigmoid(wind)) * active
            keep_ref[place, rows, :] = (1.0 - rows_ref[3, rows, :] * total[BASE_GROUP[group]]) * free
        return 0

    lax.fori_loop(0, blocks, block, 0)


def spread_row(ref, *place):
    row = ref[place[:-1] + (pl.ds(place[-1], 1), slice(None))]
    return jnp.broadcast_to(row, (GROUP_ROWS, LANES))


def split_three(values):
    high = values.astype(jnp.bfloat16).astype(jnp.float32)
    rest = values - high
    middle = rest.astype(jnp.bfloat16).astype(jnp.float32)
    return high, middle, rest - middle


def plan_kernel(
    near_ref,
    x_ref,
    y_ref,
    points_ref,
    dirs_ref,
    first_ref,
    normal_ref,
    gather,
    scatter,
    listed_ref,
    fits_ref,
    marks,
    places,
    values,
    picked,
    homes,
):
    f32, bf16 = jnp.float32, jnp.bfloat16
    edge_count, blocks, _ = near_ref.shape
    for edge in range(edge_count):
        for part in range(blocks // GROUP_ROWS):
            rows = pl.ds(GROUP_ROWS * part, GROUP_ROWS)
            near = near_ref[edge, rows, :]
            lanes, home = near & (LANES - 1), near >> 7
            alive = jnp.zeros((GROUP_ROWS, LANES), f32)
            for source in range(blocks):
                alive = jnp.where(home == source, take_lanes(spread_row(points_ref, 2, source), lanes), alive)
            homes[edge, rows, :] = jnp.where(alive * points_ref[1, rows, :] > 0.0, home, -1)
    high = [homes[edge] for edge in range(edge_count)]

    def block(place, _):
        wanted = lax.broadcasted_iota(jnp.int32, (blocks, LANES), 0)
        lanes = jnp.zeros((blocks, LANES), jnp.int32)
        x = jnp.zeros((blocks, LANES), f32)
        y = jnp.zeros((blocks, LANES), f32)
        for edge in reversed(range(edge_count)):
            near = jnp.broadcast_to(near_ref[edge, pl.ds(place, 1), :], (blocks, LANES))
            hit = jnp.broadcast_to(homes[edge, pl.ds(place, 1), :], (blocks, LANES)) == wanted
            lanes = jnp.where(hit, near & (LANES - 1), lanes)
            x = jnp.where(hit, jnp.broadcast_to(x_ref[edge, pl.ds(place, 1), :], (blocks, LANES)), x)
            y = jnp.where(hit, jnp.broadcast_to(y_ref[edge, pl.ds(place, 1), :], (blocks, LANES)), y)
        first_ref[place] = lanes
        normal_ref[0, place] = x
        normal_ref[1, place] = y
        return 0

    lax.fori_loop(0, blocks, block, 0)

    marks[...] = jnp.zeros_like(marks)
    for edge in range(edge_count):
        again = jnp.zeros((blocks, LANES), f32)
        for before in range(edge):
            again = jnp.where(high[before] == high[edge], 1.0, again)
        marks[pl.ds(blocks * edge, blocks), :] = jnp.where(high[edge] >= 0, again, 0.0)
        x_parts, y_parts = split_three(x_ref[edge]), split_three(y_ref[edge])
        rows = ((near_ref[edge] & (LANES - 1)).astype(f32), (near_ref[edge] >> 7).astype(f32)) + x_parts + y_parts
        for place in range(blocks):
            side, column = divmod(place, blocks // 2)
            for number, row in enumerate(rows):
                values[side, pl.ds(8 * edge + number, 1), pl.ds(LANES * column, LANES)] = row[place : place + 1]
    left = lax.broadcasted_iota(jnp.int32, (LANES, LANES), 0)
    right = lax.broadcasted_iota(jnp.int32, (LANES, LANES), 1)
    mark = marks[...].astype(bf16)
    within = jnp.dot(mark, jnp.where(left < right, 1.0, 0.0).astype(bf16), preferred_element_type=f32)
    count = jnp.dot(mark, jnp.ones((LANES, LANES), bf16), preferred_element_type=f32)
    earlier = (right < left) & ((left & (blocks // 2)) == (right & (blocks // 2)))
    offset = jnp.dot(jnp.where(earlier, 1.0, 0.0).astype(bf16), count.astype(bf16), preferred_element_type=f32)
    position = jnp.where(marks[...] > 0.0, within + offset, -1.0)
    places[0] = position
    places[1] = offset
    fits_ref[0] = (jnp.max(position) < LISTED).astype(jnp.int32)

    rank = lax.broadcasted_iota(jnp.int32, (16, LANES), 0).astype(f32)

    def scatter_block(place, _):
        rows = [
            jnp.broadcast_to(places[0, pl.ds(blocks * edge + place, 1), :], (16, LANES)) for edge in range(edge_count)
        ]
        for tile in range(LISTED // 16):
            here = rank + float(16 * tile)
            hit = rows[0] == here
            for row in rows[1:]:
                hit = hit | (row == here)
            value = jnp.where(hit, 1.0, 0.0).astype(bf16)
            scatter[place // 2, pl.ds(16 * tile, 16), pl.ds(pl.multiple_of((place % 2) * LANES, LANES), LANES)] = value
        return 0

    lax.fori_loop(0, blocks, scatter_block, 0)

    chunks = blocks * LANES // (2 * CHUNK)
    for side in range(2):
        wide = None
        for column in range(chunks):
            term = lax.dot_general(
                values[side, :, pl.ds(CHUNK * column, CHUNK)].astype(bf16),
                scatter[chunks * side + column],
                (((1,), (1,)), ((), ())),
                preferred_element_type=f32,
            )
            wide = term if wide is None else wide + term
        for column in range(LISTED // LANES):
            here = lax.broadcasted_iota(jnp.int32, (8, LANES), 1).astype(f32) + float(LANES * column)
            chosen = wide[0:8, LANES * column : LANES * (column + 1)]
            for edge in range(1, edge_count):
                begin = spread_row(places, 1, blocks * edge + (blocks // 2) * side)
                chosen = jnp.where(
                    here >= begin, wide[8 * edge : 8 * edge + 8, LANES * column : LANES * (column + 1)], chosen
                )
            spot = (LISTED // LANES) * side + column
            x_row = jnp.broadcast_to(chosen[2:3] + chosen[3:4] + chosen[4:5], (GROUP_ROWS, LANES))
            y_row = jnp.broadcast_to(chosen[5:6] + chosen[6:7] + chosen[7:8], (GROUP_ROWS, LANES))
            picked[pl.ds(spot, 1), :] = chosen[0:1] + float(LANES) * chosen[1:2]
            lane = slice(LANES * (column % 2), LANES * (column % 2) + LANES)
            for group, rows in enumerate((0, 1, 2, 3, 8)):
                flow = dirs_ref[0, group_rows(rows), :] * x_row + dirs_ref[1, group_rows(rows), :] * y_row
                listed_ref[spot // 2, group_rows(group), lane] = jnp.minimum(flow, 0.0)

    def gather_block(spot, _):
        source = jnp.broadcast_to(picked[pl.ds(spot, 1), :], (16, LANES))
        for tile in range(gather.shape[1] // 16):
            value = jnp.where(rank + float(16 * tile) == source, 1.0, 0.0).astype(bf16)
            gather[spot // 2, pl.ds(16 * tile, 16), pl.ds(pl.multiple_of((spot % 2) * LANES, LANES), LANES)] = value
        return 0

    lax.fori_loop(0, 2 * LISTED // LANES, gather_block, 0)


def dissipation_rate(energy, inverse):
    mean_freq = energy / (inverse + epsilon)
    steepness = energy * (0.5 * mean_freq) * (0.5 * mean_freq)
    return inverse / (energy + epsilon) * (steepness / (1.0 + steepness))


def split_bf16(values):
    high = values.astype(jnp.bfloat16).astype(jnp.float32)
    return high, values - high


def two_terms(values):
    return jnp.concatenate(split_bf16(values), axis=0).astype(jnp.bfloat16)


def pack_kernel(first_ref, spectra_ref, coarse_ref, cells_ref, weights_ref, send_ref, shares):
    destinations = send_ref.shape[0]
    f32 = jnp.float32
    lane = lax.broadcasted_iota(jnp.int32, (LANES, LANES), 1)
    cell = lax.broadcasted_iota(jnp.int32, (LANES, LANES), 0) + first_ref[0]
    weights = jnp.concatenate([weights_ref[...]] * 4, axis=1)
    norm = weights / jnp.sum(weights, axis=0, keepdims=True)
    cells = jnp.concatenate([cells_ref[...]] * 4, axis=1)
    table = jnp.zeros((LANES, LANES), f32)
    for corner in range(cells_ref.shape[0]):
        hit = jnp.broadcast_to(cells[corner : corner + 1], (LANES, LANES)) == cell
        table = table + jnp.where(hit, jnp.broadcast_to(norm[corner : corner + 1], (LANES, LANES)), 0.0)
    later = (lane & 32) != 0
    bf16 = jnp.bfloat16
    parts = [split_bf16(jnp.where(later, 0.0, table)), split_bf16(jnp.where(later, table, 0.0))]
    parts = [(high.astype(bf16), low.astype(bf16)) for high, low in parts]
    chunk = 8 * NDIR

    for start in range(0, spectra_ref.shape[0], chunk):
        result = None
        for time in range(2):
            high, low = split_bf16(coarse_ref[time, pl.ds(start, chunk), :])
            high, low = high.astype(bf16), low.astype(bf16)
            weight_high, weight_low = parts[time]
            for left, right in ((high, weight_high), (low, weight_high), (high, weight_low)):
                term = jnp.dot(left, right, preferred_element_type=f32)
                result = term if result is None else result + term
        shares[pl.ds(start, chunk), :] = result

    sub = lax.broadcasted_iota(jnp.int32, (GROUP_ROWS, LANES), 0) < 4
    energy = jnp.zeros((GROUP_ROWS, LANES), f32)
    inverse = jnp.zeros((GROUP_ROWS, LANES), f32)
    lower_lanes = lax.broadcasted_iota(jnp.int32, (NDIR, LANES), 1) < 64
    for place in range(destinations):
        start = 2 * NDIR * place
        values = [spectra_ref[pl.ds(start + GROUP_ROWS * group, GROUP_ROWS), :] for group in range(GROUPS)]
        for group in range(GROUPS):
            send_ref[place, group_rows(group), :] = values[group]
        lower = values[0] + values[1] + values[2] + values[3] + jnp.where(sub, values[4], 0.0)
        upper = values[5] + values[6] + values[7] + values[8] + jnp.where(sub, 0.0, values[4])
        energy = energy + frequency(2 * place) * lower + frequency(2 * place + 1) * upper
        inverse = inverse + (lower + upper)
        send_ref[place, pl.ds(2 * NDIR, NDIR), :] = jnp.where(
            lower_lanes, shares[pl.ds(start, NDIR), :], shares[pl.ds(start + NDIR, NDIR), :]
        )
    energy = jnp.sum(energy, axis=0, keepdims=True) * (1.0 / FREQ_TOTAL)
    inverse = jnp.sum(inverse, axis=0, keepdims=True) * (1.0 / FREQ_TOTAL)
    rate = jnp.broadcast_to(dissipation_rate(energy, inverse), (4, LANES))
    for place in range(destinations):
        send_ref[place, pl.ds(3 * NDIR, 4), :] = rate


def take_lanes(values, lanes):
    return jnp.take_along_axis(values, lanes, axis=1, mode="promise_in_bounds")


def fine_kernel(
    first,
    fits_ref,
    state_ref,
    extra_ref,
    near_ref,
    x_ref,
    y_ref,
    points_ref,
    dirs_ref,
    keep_ref,
    growth_ref,
    rows_ref,
    listed_ref,
    first_ref,
    normal_ref,
    gather_in,
    scatter_in,
    *rest,
):
    if first:
        out_ref, sums_ref, start_ref, slope_ref = rest[:4]
    else:
        start_ref, slope_ref, out_ref = rest[:3]
    scratch = rest[4:] if first else rest[3:]
    field, words, speed, base_ref, gather_ref, scatter_ref, pairs, ends, inflow_ref, terms, moments, sems = scratch
    copies = [
        pltpu.make_async_copy(source.at[part], target.at[part], sems.at[kind, part])
        for kind, (source, target) in enumerate(((gather_in, gather_ref), (scatter_in, scatter_ref)))
        for part in range(target.shape[0])
    ]
    for copy in copies:
        copy.start()
    f32, bf16 = jnp.float32, jnp.bfloat16
    blocks = keep_ref.shape[0]
    half = blocks // 2
    edge_count = near_ref.shape[0]
    first_step = 0 if first else SUB
    if first:
        total = state_ref[0, pl.ds(2 * NDIR, 40), :]
        for source in range(1, blocks):
            total = total + state_ref[source, pl.ds(2 * NDIR, 40), :]
        rolled = [total] + [pltpu.roll(total, LANES - 32 * piece, 1) for piece in range(1, 4)]
        high, low = split_bf16(jnp.concatenate(rolled, axis=0))
        bound = jnp.concatenate([high, low], axis=0).astype(jnp.bfloat16)

    else:
        total = extra_ref[0]
        for source in range(1, blocks):
            total = total + extra_ref[source]
        moments[...] = total

    def spread(place):
        values = jnp.dot(bound, extra_ref[place], preferred_element_type=jnp.float32)
        values = values[0:160] + values[160:320]
        pieces = [values[40 * piece : 40 * piece + 40] for piece in range(4)]
        for out, pair in (
            (start_ref, (pieces[0], pieces[2])),
            (slope_ref, (pieces[1] - pieces[0], pieces[3] - pieces[2])),
        ):
            for side in range(2):
                for group in range(4):
                    out[place, group_rows(4 * side + group), :] = pair[side][8 * group : 8 * group + 8]
            out[place, pl.ds(64, 4), :] = pair[0][32:36]
            out[place, pl.ds(68, 4), :] = pair[1][32:36]

    def enter(place, _):
        if first:
            loss = jnp.broadcast_to(state_ref[place, pl.ds(3 * NDIR, 1), :], (GROUP_ROWS, LANES))
            values = load_natural(state_ref, place)
            spread(place)
        else:
            loss = dissipation_rate(spread_row(moments, place), spread_row(moments, blocks + place))
            values = [state_ref[place, group_rows(group), :] for group in range(GROUPS)]
        lower, upper, last = [jnp.exp(-rows_ref[2, group_rows(group), :] * loss) for group in (0, 4, 8)]
        decay = [lower] * 4 + [upper] * 4 + [last]
        for group in range(GROUPS):
            rows = group_rows(group)
            value = values[group] * growth_ref[place, rows, :] * decay[group]
            field[0, place, rows, :] = value
            words[0, pl.ds(16 * group, 16), pl.ds(pl.multiple_of(LANES * place, LANES), LANES)] = two_terms(value)
        for source in range(blocks):
            x, y = spread_row(normal_ref, 0, place, source), spread_row(normal_ref, 1, place, source)
            for group, number in enumerate((0, 1, 2, 3, 8)):
                flow = dirs_ref[0, group_rows(number), :] * x + dirs_ref[1, group_rows(number), :] * y
                base_ref[place, source, group_rows(group), :] = jnp.minimum(flow, 0.0)
        return 0

    lax.fori_loop(0, blocks, enter, 0)

    def boundary(place, rows, number):
        time_frac = jnp.asarray(number + (first_step + 1), jnp.int32).astype(f32) * (1.0 / (STEPS * SUB))
        return start_ref[place, rows, :] + time_frac * slope_ref[place, rows, :]

    def encode(group, top_code):
        rows = group_rows(group)
        values = [field[0, place, rows, :] for place in range(blocks)]
        top = functools.reduce(jnp.maximum, values)
        top = jnp.maximum(jnp.max(top, axis=1, keepdims=True), 1e-30)
        scale = jnp.broadcast_to(top_code / top, (GROUP_ROWS, LANES))
        speed[rows, :] = rows_ref[3, rows, :] * (top * (1.0 / top_code))
        return [(value * scale + 0.5).astype(jnp.int32) for value in values]

    def collect(side, now):
        for chunk in range(LISTED // CHUNK * side, LISTED // CHUNK * (side + 1)):
            found = jnp.dot(words[now], gather_ref[chunk], preferred_element_type=f32)
            for group in range(GROUPS):
                value = found[16 * group : 16 * group + 8] + found[16 * group + 8 : 16 * group + 16]
                high, low = split_bf16(value * listed_ref[chunk, group_rows(BASE_GROUP[group]), :])
                terms[chunk, pl.ds(16 * group, 16), :] = jnp.concatenate([high, low], axis=0).astype(bf16)
        for place in range(half * side, half * (side + 1)):
            inflow = [jnp.zeros((GROUP_ROWS, LANES), f32)] * GROUPS
            for source in range(blocks):
                lanes = spread_row(first_ref, place, source)
                for group in range(4):
                    base = base_ref[place, source, group_rows(group), :]
                    word = take_lanes(pairs[source, group_rows(group), :], lanes)
                    lower = (word & 65535).astype(f32)
                    upper = lax.shift_right_logical(word, 16).astype(f32)
                    inflow[group] = inflow[group] + base * lower
                    inflow[group + 4] = inflow[group + 4] + base * upper
                inflow[8] = inflow[8] + base_ref[place, source, group_rows(4), :] * take_lanes(ends[source], lanes)
            for group in range(GROUPS):
                factor = speed[group_rows(group), :] if group < 8 else rows_ref[3, group_rows(8), :]
                inflow_ref[place, group_rows(group), :] = factor * inflow[group]

    def update(side, number, later):
        parts = LISTED // CHUNK
        for chunk in range(half // 2 * side, half // 2 * (side + 1)):
            moved = None
            for part in range(parts):
                term = jnp.dot(
                    terms[parts * side + part],
                    scatter_ref[chunk, pl.ds(CHUNK * part, CHUNK), :],
                    preferred_element_type=f32,
                )
                moved = term if moved is None else moved + term
            for column in range(2):
                place = 2 * chunk + column
                lanes = slice(LANES * column, LANES * (column + 1))
                for group in range(GROUPS):
                    rows = group_rows(group)
                    more = moved[16 * group : 16 * group + 8, lanes] + moved[16 * group + 8 : 16 * group + 16, lanes]
                    value = (
                        field[0, place, rows, :] * keep_ref[place, rows, :]
                        - inflow_ref[place, rows, :]
                        - rows_ref[3, rows, :] * more
                        + boundary(place, rows, number)
                    )
                    field[0, place, rows, :] = value
                    words[later, pl.ds(16 * group, 16), pl.ds(LANES * place, LANES)] = two_terms(value)

    def fine_step(number, _):
        now = lax.rem(number, 2)
        for group in range(4):
            lower, upper = encode(group, 65535.0), encode(group + 4, 65535.0)
            for place in range(blocks):
                pairs[place, group_rows(group), :] = (upper[place] << 16) | lower[place]
        for place in range(blocks):
            ends[place] = field[0, place, group_rows(8), :]

        collect(0, now)
        update(0, number, 1 - now)
        collect(1, now)
        update(1, number, 1 - now)
        return 0

    def plain_step(number, _):
        def block(place, _):
            free = spread_row(points_ref, 1, place)
            inflow = [jnp.zeros((GROUP_ROWS, LANES), f32)] * GROUPS
            for edge in range(edge_count):
                near = spread_row(near_ref, edge, place)
                lanes, home = near & (LANES - 1), near >> 7
                x, y = spread_row(x_ref, edge, place), spread_row(y_ref, edge, place)
                for group in range(GROUPS):
                    rows = group_rows(group)
                    value = jnp.zeros((GROUP_ROWS, LANES), f32)
                    for source in range(blocks):
                        value = jnp.where(home == source, take_lanes(field[0, source, rows, :], lanes), value)
                    flow = dirs_ref[0, rows, :] * x + dirs_ref[1, rows, :] * y
                    inflow[group] = inflow[group] + jnp.minimum(flow, 0.0) * free * value
            for group in range(GROUPS):
                rows = group_rows(group)
                field[1, place, rows, :] = (
                    field[0, place, rows, :] * keep_ref[place, rows, :]
                    - rows_ref[3, rows, :] * inflow[group]
                    + boundary(place, rows, number)
                )
            return 0

        lax.fori_loop(0, blocks, block, 0)
        field[0] = field[1]
        return 0

    for copy in copies:
        copy.wait()
    fits = fits_ref[0]

    @pl.when(fits != 0)
    def _():
        lax.fori_loop(0, SUB, fine_step, 0)

    @pl.when(fits == 0)
    def _():
        lax.fori_loop(0, SUB, plain_step, 0)

    def leave(place, _):
        values = [field[0, place, group_rows(group), :] for group in range(GROUPS)]
        if first:
            energy, inverse = None, None
            for group in range(GROUPS):
                rows = group_rows(group)
                out_ref[place, rows, :] = values[group]
                part = rows_ref[4, rows, :] * values[group]
                energy = part if energy is None else energy + part
                part = rows_ref[5, rows, :] * values[group]
                inverse = part if inverse is None else inverse + part
            moments[pl.ds(place, 1), :] = jnp.sum(energy, axis=0, keepdims=True)
            moments[pl.ds(blocks + place, 1), :] = jnp.sum(inverse, axis=0, keepdims=True)
        else:
            store_natural(out_ref, place, values)
        return 0

    lax.fori_loop(0, blocks, leave, 0)
    if first:
        for target in range(sums_ref.shape[0]):
            sums_ref[target] = moments[...]


def in_vmem(count):
    return [pl.BlockSpec(memory_space=pltpu.VMEM)] * count


def params(mebibytes=56):
    return pltpu.CompilerParams(vmem_limit_bytes=mebibytes << 20)


def whole_frequencies(
    spectra_in,
    coarse_spectra,
    wind_speed,
    wind_heading,
    sea_mask,
    neighbours,
    edge_x,
    edge_y,
    bound_points,
    bound_cells,
    bound_weights,
):
    device_count = lax.axis_size("pts")
    device_place = lax.axis_index("pts")
    comp_total, point_count = spectra_in.shape
    local_count = comp_total // device_count
    edge_count, grid_points = neighbours.shape
    blocks = grid_points // LANES
    bound_count = bound_points.shape[0]
    f32 = jnp.float32
    first_point = (device_place * point_count).astype(jnp.int32).reshape(1)
    send = pl.pallas_call(
        pack_kernel,
        out_shape=jax.ShapeDtypeStruct((device_count, 112, LANES), f32),
        in_specs=[pl.BlockSpec(memory_space=pltpu.SMEM)] + in_vmem(4),
        out_specs=pl.BlockSpec(memory_space=pltpu.VMEM),
        scratch_shapes=[pltpu.VMEM((comp_total, LANES), f32)],
        compiler_params=params(),
    )(first_point, spectra_in, coarse_spectra, bound_cells, bound_weights)
    received = lax.all_to_all(send, "pts", split_axis=0, concat_axis=0, tiled=True)

    by_block = (blocks, LANES)
    state_shape = jax.ShapeDtypeStruct((blocks, local_count, LANES), f32)
    edge_shape = (edge_count, blocks, LANES)
    keep, growth, rows, dirs, points, select, near, edge_x, edge_y = pl.pallas_call(
        setup_kernel,
        out_shape=[
            state_shape,
            state_shape,
            jax.ShapeDtypeStruct((6, local_count, LANES), f32),
            jax.ShapeDtypeStruct((2, local_count, LANES), f32),
            jax.ShapeDtypeStruct((3,) + by_block, f32),
            jax.ShapeDtypeStruct((blocks, LANES, LANES), jnp.bfloat16),
            jax.ShapeDtypeStruct(edge_shape, jnp.int32),
            jax.ShapeDtypeStruct(edge_shape, f32),
            jax.ShapeDtypeStruct(edge_shape, f32),
        ],
        in_specs=[pl.BlockSpec(memory_space=pltpu.SMEM)] * 2 + in_vmem(6),
        out_specs=in_vmem(9),
        compiler_params=params(),
        cost_estimate=pl.CostEstimate(flops=100_000_000, bytes_accessed=4_000_000, transcendentals=1_000_000),
    )(
        device_place.astype(jnp.int32).reshape(1),
        bound_points,
        wind_speed.reshape(by_block),
        wind_heading.reshape(by_block),
        sea_mask.reshape(by_block),
        neighbours,
        edge_x,
        edge_y,
    )

    shapes = [
        ((2 * LISTED // CHUNK, grid_points, CHUNK), jnp.bfloat16),
        ((grid_points // CHUNK, LISTED, CHUNK), jnp.bfloat16),
    ]
    first_edge, normals, gather, scatter, listed, fits = pl.pallas_call(
        plan_kernel,
        out_shape=[
            jax.ShapeDtypeStruct((blocks,) + by_block, jnp.int32),
            jax.ShapeDtypeStruct((2, blocks) + by_block, f32),
        ]
        + [jax.ShapeDtypeStruct(shape, dtype) for shape, dtype in shapes]
        + [jax.ShapeDtypeStruct((2 * LISTED // CHUNK, 40, CHUNK), f32), jax.ShapeDtypeStruct((1,), jnp.int32)],
        in_specs=in_vmem(5),
        out_specs=in_vmem(5) + [pl.BlockSpec(memory_space=pltpu.SMEM)],
        scratch_shapes=[
            pltpu.VMEM((LANES, LANES), f32),
            pltpu.VMEM((2, LANES, LANES), f32),
            pltpu.VMEM((2, 8 * edge_count, grid_points // 2), f32),
            pltpu.VMEM((2 * LISTED // LANES, LANES), f32),
            pltpu.VMEM(edge_shape, jnp.int32),
        ],
        compiler_params=params(),
        cost_estimate=pl.CostEstimate(flops=1_000_000_000, bytes_accessed=20_000_000, transcendentals=0),
    )(near, edge_x, edge_y, points, dirs)

    def fine(is_first, state, extra, bound):
        out_shape = [state_shape]
        if is_first:
            out_shape += [jax.ShapeDtypeStruct((device_count, 2 * blocks, LANES), f32), state_shape, state_shape]
        return pl.pallas_call(
            functools.partial(fine_kernel, is_first),
            out_shape=out_shape,
            in_specs=[pl.BlockSpec(memory_space=pltpu.SMEM)]
            + in_vmem(13)
            + [pl.BlockSpec(memory_space=pl.ANY)] * 2
            + in_vmem(len(bound)),
            out_specs=in_vmem(len(out_shape)),
            scratch_shapes=[
                pltpu.VMEM((2, blocks, local_count, LANES), f32),
                pltpu.VMEM((2, 2 * local_count, grid_points), jnp.bfloat16),
                pltpu.VMEM((local_count, LANES), f32),
            ]
            + [
                pltpu.VMEM((blocks, blocks, 40, LANES), f32),
            ]
            + [pltpu.VMEM(shape, dtype) for shape, dtype in shapes]
            + [
                pltpu.VMEM((blocks, 32, LANES), jnp.int32),
                pltpu.VMEM((blocks, GROUP_ROWS, LANES), f32),
                pltpu.VMEM((blocks, local_count, LANES), f32),
                pltpu.VMEM((2 * LISTED // CHUNK, 2 * local_count, CHUNK), jnp.bfloat16),
                pltpu.VMEM((2 * blocks, LANES), f32),
                pltpu.SemaphoreType.DMA((2, 8)),
            ],
            compiler_params=params(56),
        )(
            fits,
            state,
            extra,
            near,
            edge_x,
            edge_y,
            points,
            dirs,
            keep,
            growth,
            rows,
            listed,
            first_edge,
            normals,
            gather,
            scatter,
            *bound,
        )

    field, sums, start, slope = fine(True, received, select, ())
    sums = lax.all_to_all(sums, "pts", split_axis=0, concat_axis=0, tiled=True)
    (field,) = fine(False, field, sums, (start, slope))
    field = lax.all_to_all(field, "pts", split_axis=0, concat_axis=0, tiled=True)
    return field.reshape(comp_total, point_count)


def shards(
    spectra_in,
    coarse_spectra,
    wind_speed,
    wind_heading,
    sea_mask,
    neighbours,
    edge_x,
    edge_y,
    bound_points,
    bound_cells,
    bound_weights,
):
    device_count = lax.axis_size("pts")
    device_place = lax.axis_index("pts")
    point_count = spectra_in.shape[1]
    comp_total = spectra_in.shape[0]
    local_count = comp_total // device_count
    active = sea_mask.astype(jnp.float32)
    blocks = neighbours.shape[1] // LANES
    if (
        local_count == 2 * NDIR
        and point_count == LANES
        and 4 * bound_points.shape[0] == LANES
        and coarse_spectra.shape[2] == LANES
        and blocks == device_count
        and blocks == 16
        and neighbours.shape[0] * blocks <= LANES
    ):
        return whole_frequencies(
            spectra_in,
            coarse_spectra,
            wind_speed,
            wind_heading,
            sea_mask,
            neighbours,
            edge_x,
            edge_y,
            bound_points,
            bound_cells,
            bound_weights,
        )
    all_comp = jnp.arange(comp_total, dtype=jnp.int32)
    my_comp = device_place * local_count + jnp.arange(local_count, dtype=jnp.int32)
    first_point = device_place * point_count
    own_speed = lax.dynamic_slice_in_dim(wind_speed, first_point, point_count)
    own_heading = lax.dynamic_slice_in_dim(wind_heading, first_point, point_count)
    own_active = lax.dynamic_slice_in_dim(active, first_point, point_count)
    coarse_here = lax.all_to_all(coarse_spectra, "pts", split_axis=1, concat_axis=2, tiled=True)
    bound_values = interpolate(coarse_here, bound_cells, bound_weights)
    outflow, inflow = coefficients(my_comp, edge_x, edge_y)
    spectra = spectra_in
    for coarse_step in range(STEPS):
        energy, inverse = statistics(spectra, all_comp)
        spectra = apply_sources(
            spectra, all_comp, energy, inverse, own_speed, own_heading, own_active
        )
        comp_field = to_components(spectra)
        comp_field = advect(
            comp_field,
            outflow,
            inflow,
            neighbours,
            active,
            bound_values,
            bound_points,
            coarse_step * SUB,
        )
        spectra = to_points(comp_field)
    return spectra


def solution(mesh):
    in_specs = (
        P(None, ("groups", "pts")),
        P(None, None, ("groups", "pts")),
        P("groups"),
        P("groups"),
        P(),
        P(),
        P(),
        P(),
        P(),
        P(),
        P(),
    )
    out_specs = P(None, ("groups", "pts"))
    return jax.shard_map(shards, mesh=mesh, in_specs=in_specs, out_specs=out_specs, check_vma=False)
```
